32 devices in a mesh: group: 2 (over y), dom: 8 (over z, x), shot: 2 (over core).
Axes of the slice: x: 2, y: 2, z: 4, core: 2. Of those that a mesh axis runs over, the one named last changes fastest.
Arguments:
- checkpoint: float32 [4, 2, 64, 96, 256], P(('group', 'shot'), None, 'dom'), parts along dimension 0, may hold values from -6 to 6
- adjoint: float32 [4, 2, 64, 96, 256], P(('group', 'shot'), None, 'dom'), parts along dimension 0, may hold values from -6 to 6
- kappa: float32 [128, 128, 256], P(('group', 'dom')), parts along dimension 0, may hold values from 0.04 to 0.12
- buoyancy: float32 [128, 128, 256], P(('group', 'dom')), parts along dimension 0, may hold values from 0.5 to 2
- wavelet: float32 [1024], replicated, may hold values from 60 to 300
- src_cell: int32 [4], P(('group', 'shot')), parts along dimension 0, may hold values from 0 to 1572863
- rec_cell: int32 [4, 6400], P(('group', 'shot')), parts along dimension 0, may hold values from 0 to 1572863
- residuals: float32 [4, 2, 6400], P(('group', 'shot')), parts along dimension 0, may hold values from -64 to 64
- offsets: int32 [4], P(('group', 'shot')), parts along dimension 0, may hold values from 0 to 32
- ckpt_step: int32 [4], P(('group', 'shot')), parts along dimension 0, may hold values from 0 to 1023
Outputs:
- grad_kappa: float32 [128, 128, 256], P(('group', 'dom'), 'shot'), parts along dimension 0
- grad_buoy: float32 [128, 128, 256], P(('group', 'dom'), 'shot'), parts along dimension 0
- adjoint_next: float32 [4, 2, 64, 96, 256], P(('group', 'shot'), None, 'dom'), parts along dimension 0
The draws below stay inside these ranges and needn't reach their ends.
There are 2 independent parts, one for each index of `group`. The reference program is written for one: setup_inputs(seed, part) draws one part's arguments, and reference() takes and returns one part's arrays. A program takes and returns all parts, laid end to end along the dimension named above; an argument that names none is the same for every part. Nothing has to cross between parts.
Inputs may be any that keep to these rules, and one draw needn't show every extreme that they name: `src_cell`: a flat cell of the shot's aperture. `rec_cell`: flat cells of the shot's aperture; several receivers may share a cell.
All inputs are finite; a program needn't handle non-finite values.
Results may differ from the reference program's by a relative error of at most 0.00011.
Values sent between devices are 32-bit elements; how exact they have to be, the bound alone decides.
No kernel may reach another device: no remote copies, remote signals or barrier semaphores. Data moves between devices by JAX's collectives and lax.ppermute only.
A program may use at most 64 MiB of HBM per device.

```python
import math
import jax
import jax.numpy as jnp
from jax import lax

NY = 96
NZ = 256
MY = 128
NREC = 6400
NT = 1024
NX = 64
SHOTS = 2


def plant(array, own_key, low, largest):
    longest = array.shape.index(max(array.shape))
    spots = []
    for shift in (0, 1):
        where = [jax.random.randint(jax.random.fold_in(own_key, axis), (), 0, length) for axis, length in enumerate(array.shape)]
        where[longest] = (where[longest] + shift) % array.shape[longest]
        spots.append(tuple(where))
    return array.at[spots[0]].set(low).at[spots[1]].set(largest)


def block_levels(key, extent, cuts, smallest, largest):
    def one(position, blocks):
        draws = jax.random.uniform(jax.random.fold_in(jax.random.fold_in(key, 6), position), (blocks,), jnp.float32, smallest / len(cuts), largest / len(cuts))
        return jnp.repeat(jnp.exp(draws), extent[position] // blocks).reshape((-1,) + (1,) * (len(extent) - position - 1))

    level = one(*cuts[0])
    for cut in cuts[1:]:
        level = level * one(*cut)
    return level


def centred(rng, extent, width, most, split=(), dtype=jnp.bfloat16):
    entries = jax.random.normal(rng, extent, jnp.float32) * width
    if len(split) > 0:
        entries = block_levels(rng, extent, split, -0.22, 0.18) * entries
    return jnp.clip(entries, min=-most, max=most).astype(dtype)


def setup_inputs(seed: int = 0, part: int = 0) -> dict:
    splits = jax.random.split(jax.random.key(seed), 11)
    part_splits = jax.random.split(jax.random.fold_in(splits[10], part), 11)
    return {
        "checkpoint": centred(part_splits[0], (SHOTS, 2, NX, NY, NZ), 1.0, 6.0, ((0, 2), (2, 8)), jnp.float32),
        "adjoint": centred(part_splits[1], (SHOTS, 2, NX, NY, NZ), 1.0, 6.0, ((0, 2), (2, 8)), jnp.float32),
        "kappa": jnp.clip(jnp.exp(math.log(0.12) - 1.0986123 * jax.random.uniform(part_splits[2], (NX, MY, NZ), jnp.float32) ** block_levels(part_splits[2], (NX, MY, NZ), ((0, 8),), -0.2, 0.2)), 0.04, 0.12),
        "buoyancy": jnp.clip(jnp.exp(math.log(2.0) - 1.3862944 * jax.random.uniform(part_splits[3], (NX, MY, NZ), jnp.float32) ** block_levels(part_splits[3], (NX, MY, NZ), ((0, 8),), -0.2, 0.2)), 0.5, 2.0),
        "wavelet": jnp.clip(jax.random.uniform(splits[4], (NT,), jnp.float32, 60.0, 300.0), 60.0, 300.0),
        "src_cell": jax.random.randint(part_splits[5], (SHOTS,), 0, NX * NY * NZ).astype(jnp.int32),
        "rec_cell": plant(jax.random.randint(part_splits[6], (SHOTS, NREC), 0, NX * NY * NZ), jax.random.fold_in(part_splits[6], 1), 0, (NX * NY * NZ) - 1).astype(jnp.int32),
        "residuals": centred(part_splits[7], (SHOTS, 2, NREC), 10.0, 64.0, ((0, 2),), jnp.float32),
        "offsets": jax.random.randint(part_splits[8], (SHOTS,), 0, MY - NY + 1).astype(jnp.int32),
        "ckpt_step": jax.random.randint(part_splits[9], (SHOTS,), 0, NT).astype(jnp.int32),
    }


def view(padded, sx, sy, sz):
    rank = padded.ndim
    out = padded
    for axis, shift in ((rank - 3, sx), (rank - 2, sy), (rank - 1, sz)):
        count = padded.shape[axis] - 2
        out = lax.slice_in_dim(out, 1 + shift, 1 + shift + count, axis=axis)
    return out


def stencil(field_pad, buoy_pad):
    centre = view(field_pad, 0, 0, 0)
    bcentre = view(buoy_pad, 0, 0, 0)
    total = jnp.zeros_like(centre)
    for shifts in ((1, 0, 0), (-1, 0, 0), (0, 1, 0), (0, -1, 0), (0, 0, 1), (0, 0, -1)):
        face = 0.5 * (bcentre + view(buoy_pad, shifts[0], shifts[1], shifts[2]))
        total = total + face * (view(field_pad, shifts[0], shifts[1], shifts[2]) - centre)
    return total


def image_buoy(field_pad, adjoint_pad):
    pcentre = view(field_pad, 0, 0, 0)
    qcentre = view(adjoint_pad, 0, 0, 0)
    total = jnp.zeros_like(pcentre)
    for shifts in ((1, 0, 0), (0, 1, 0), (0, 0, 1)):
        total = total + (view(adjoint_pad, shifts[0], shifts[1], shifts[2]) - qcentre) * (view(field_pad, shifts[0], shifts[1], shifts[2]) - pcentre)
    return total


def pad_three(field):
    return jnp.pad(field, ((1, 1), (1, 1), (1, 1)))


def inject(field, cells, values):
    flat = field.reshape(-1).at[cells].add(values)
    return flat.reshape(field.shape)


def reference(checkpoint, adjoint, kappa, buoyancy, wavelet, src_cell, rec_cell, residuals, offsets, ckpt_step):
    grad_k = jnp.zeros(kappa.shape, jnp.float32)
    grad_b = jnp.zeros(kappa.shape, jnp.float32)
    outs = []
    for shot_id in range(SHOTS):
        start = (jnp.int32(0), offsets[shot_id].astype(jnp.int32), jnp.int32(0))
        kwin = lax.dynamic_slice(kappa, start, (NX, NY, NZ))
        bwin = lax.dynamic_slice(buoyancy, start, (NX, NY, NZ))
        buoy_pad = pad_three(bwin)
        p_old = checkpoint[shot_id, 0]
        p_now = checkpoint[shot_id, 1]
        q_late = adjoint[shot_id, 0]
        q_now = adjoint[shot_id, 1]
        p_pad = pad_three(p_now)
        lap_now = stencil(p_pad, buoy_pad)
        amp = wavelet[ckpt_step[shot_id]]
        p_next = inject(2.0 * p_now - p_old + kwin * lap_now, src_cell[shot_id:shot_id + 1], amp[None])
        pn_pad = pad_three(p_next)
        lap_next = stencil(pn_pad, buoy_pad)
        q_pad = pad_three(kwin * q_now)
        q_mid = inject(2.0 * q_now - q_late + stencil(q_pad, buoy_pad), rec_cell[shot_id], residuals[shot_id, 0])
        qm_pad = pad_three(kwin * q_mid)
        q_last = inject(2.0 * q_mid - q_now + stencil(qm_pad, buoy_pad), rec_cell[shot_id], residuals[shot_id, 1])
        part_k = q_mid * lap_now + q_now * lap_next
        part_b = -(image_buoy(p_pad, qm_pad) + image_buoy(pn_pad, q_pad))
        cur_k = lax.dynamic_slice(grad_k, start, (NX, NY, NZ))
        grad_k = lax.dynamic_update_slice(grad_k, cur_k + part_k, start)
        cur_b = lax.dynamic_slice(grad_b, start, (NX, NY, NZ))
        grad_b = lax.dynamic_update_slice(grad_b, cur_b + part_b, start)
        outs.append(jnp.stack([q_mid, q_last]))
    return grad_k, grad_b, jnp.stack(outs)
```

```python
import functools

import jax
import jax.numpy as jnp
from jax import lax
from jax.experimental import pallas as pl
from jax.experimental.pallas import tpu as pltpu
from jax.sharding import PartitionSpec as P

F32 = jnp.float32
BF16 = jnp.bfloat16
LANES = 128
GROUP_ROWS = 5

VM = pl.BlockSpec(memory_space=pltpu.VMEM)
SM = pl.BlockSpec(memory_space=pltpu.SMEM)
ANY = pl.BlockSpec(memory_space=pl.ANY)


def vmem(*shape):
    return pltpu.VMEM(shape, F32)


def keep(x):
    return pltpu.with_memory_space_constraint(x, pltpu.VMEM)


def params():
    return pltpu.CompilerParams(vmem_limit_bytes=24 * 1024 * 1024)


def edges(width):
    even = lax.rem(lax.axis_index("dom"), 2) == 0
    last = jnp.int32(width - 1)
    first = jnp.int32(0)
    return jnp.where(even, last, first), jnp.where(even, first, last)


def window(block, off, ny):
    rows = block.shape[0]
    return pltpu.roll(block, lax.rem(rows - off, rows), 0)[:ny]


def placed(plane, off, rows):
    fill = jnp.zeros((rows - plane.shape[0], plane.shape[1]), plane.dtype)
    return pltpu.roll(jnp.concatenate([plane, fill], axis=0), off, 0)


def up(v, axis):
    return pltpu.roll(v, v.shape[axis] - 1, axis)


def down(v, axis):
    return pltpu.roll(v, 1, axis)


def first_send(off, ckpt, adj, kappa, buoy, send_b, send_a, q_e, k_e, b_e, sem):
    width, ny, nz = ckpt.shape[2:]
    edge_a, edge_b = edges(width)
    copies = []
    for n, (edge, send) in enumerate(((edge_b, send_b), (edge_a, send_a))):
        copies.append(
            (
                pltpu.make_async_copy(ckpt.at[0, 1, edge], send.at[0], sem.at[n, 0]),
                pltpu.make_async_copy(adj.at[0, 1, edge], q_e.at[n], sem.at[n, 1]),
                pltpu.make_async_copy(kappa.at[edge], k_e.at[n], sem.at[n, 2]),
                pltpu.make_async_copy(buoy.at[edge], b_e.at[n], sem.at[n, 3]),
            )
        )
    for group in copies:
        for copy in group:
            copy.start()
    for n, send in enumerate((send_b, send_a)):
        for copy in copies[n]:
            copy.wait()
        send[1] = window(k_e[n], off[0], ny) * q_e[n]
        send[2] = window(b_e[n], off[0], ny)


def receivers(rec, res, total, cells0, nz, rank_s, row_a_s, row_b_s, z_s, val_s, left, right_hi, right_lo):
    rows, lanes = rec.shape
    cells = left.shape[0] * nz
    shift = nz.bit_length() - 1
    local = rec[...] - cells0
    inside = (local >= 0) & (local < cells)
    row = lax.shift_right_logical(local, jnp.int32(shift))
    row_a_s[...] = lax.shift_right_logical(row, jnp.int32(2)).astype(F32)
    row_b_s[...] = (row & 3).astype(F32)
    z_s[...] = (local & (nz - 1)).astype(F32)
    for step in range(2):
        value = res[step]
        high = value.astype(BF16).astype(F32)
        val_s[2 * step] = high
        val_s[2 * step + 1] = value - high
    mask = jnp.where(inside, 1.0, 0.0).astype(BF16)
    before = lax.broadcasted_iota(jnp.int32, (lanes, lanes), 0) < lax.broadcasted_iota(
        jnp.int32, (lanes, lanes), 1
    )
    in_row = jnp.dot(mask, jnp.where(before, 1.0, 0.0).astype(BF16), preferred_element_type=F32)
    row_sum = jnp.dot(mask, jnp.ones((lanes, lanes), BF16), preferred_element_type=F32)
    r = lax.broadcasted_iota(jnp.int32, (rows, rows), 0)
    c = lax.broadcasted_iota(jnp.int32, (rows, rows), 1)
    group_r = lax.shift_right_logical(r * 3277, jnp.int32(14))
    group_c = lax.shift_right_logical(c * 3277, jnp.int32(14))
    earlier = jnp.where((group_r == group_c) & (c < r), 1.0, 0.0).astype(BF16)
    row_start = jnp.dot(earlier, row_sum.astype(BF16), preferred_element_type=F32)
    rank = jnp.where(inside, in_row + row_start, -1.0)
    rank_s[...] = rank
    passes = lax.shift_right_logical(jnp.max(rank).astype(jnp.int32), jnp.int32(7)) + 1
    passes = jnp.maximum(passes, 1)
    groups = rows // GROUP_ROWS
    slot = lax.broadcasted_iota(jnp.int32, (LANES, lanes), 0).astype(F32)
    sub8 = lax.broadcasted_iota(jnp.int32, (8, lanes), 0)
    row_iota = lax.broadcasted_iota(jnp.int32, (left.shape[0], LANES), 0).astype(F32)
    depth_iota = lax.broadcasted_iota(jnp.int32, (LANES, nz), 1).astype(F32)

    def one_pass(number, first):
        base = (number * LANES).astype(F32) if not isinstance(number, int) else float(number * LANES)
        for g in range(groups):
            picks = []
            fields = []
            for n in range(GROUP_ROWS):
                at = pl.ds(g * GROUP_ROWS + n, 1)
                want = jnp.broadcast_to(rank_s[at, :] - base, (LANES, lanes))
                picks.append(jnp.where(want == slot, 1.0, 0.0).astype(BF16))
                data = jnp.zeros((8, lanes), F32)
                sources = [row_a_s, row_b_s, z_s] + [val_s.at[m] for m in range(4)]
                for m, source in enumerate(sources):
                    data = jnp.where(sub8 == m, jnp.broadcast_to(source[at, :], (8, lanes)), data)
                fields.append(data.astype(BF16))
            pick = jnp.concatenate(picks, axis=1)
            data = jnp.concatenate(fields, axis=1)
            dims = (((1,), (1,)), ((), ()))
            by_slot = lax.dot_general(pick, data, dims, preferred_element_type=F32)
            by_field = lax.dot_general(data, pick, dims, preferred_element_type=F32)
            where_row = by_field[0:1, :] * 4.0 + by_field[1:2, :]
            here = pl.ds(g * LANES, LANES)
            left[:, here] = jnp.where(row_iota == where_row, 1.0, 0.0).astype(BF16)
            same = by_slot[:, 2:3] == depth_iota
            for step in range(2):
                cols = pl.ds(step * nz, nz)
                right_hi[here, cols] = jnp.where(same, by_slot[:, 3 + 2 * step : 4 + 2 * step], 0.0).astype(BF16)
                right_lo[here, cols] = jnp.where(same, by_slot[:, 4 + 2 * step : 5 + 2 * step], 0.0).astype(BF16)
        out = jnp.dot(left[...], right_hi[...], preferred_element_type=F32) + jnp.dot(
            left[...], right_lo[...], preferred_element_type=F32
        )
        if first:
            total[...] = out
        else:
            total[...] += out

    one_pass(0, True)

    @pl.when(passes > 1)
    def _():
        def body(number, carry):
            one_pass(number, False)
            return carry

        lax.fori_loop(1, passes, body, 0)


def lap_plane(f, f_next, gx_last, hx, fy, fz, dg):
    gx = hx * (f_next - f)
    gy = fy * (up(f, 0) - f)
    gz = fz * (up(f, 1) - f)
    out = (gx - gx_last) + (gy - down(gy, 0)) + (gz - down(gz, 1)) - dg * f
    return out, gx


def step_one(
    off, step, src, wav, rec, res, ckpt, adj, kappa, buoy, after,
    p, q, kq, kw, hb, fy_o, fz_o, dg_o, lap, pn, qm, total,
    p_old, q_late, k_full, b_full, count, gx_p, gx_q,
    rank_s, row_a_s, row_b_s, z_s, val_s, left, right_hi, right_lo, sem,
):
    width, ny, nz = p.shape
    copies = [
        pltpu.make_async_copy(source, target, sem.at[n])
        for n, (source, target) in enumerate(
            (
                (kappa, k_full), (buoy, b_full), (adj.at[0, 1], q), (ckpt.at[0, 1], p),
                (ckpt.at[0, 0], p_old), (adj.at[0, 0], q_late),
            )
        )
    ]
    for copy in copies:
        copy.start()
    cells0 = lax.axis_index("dom") * (width * ny * nz)
    receivers(rec, res, total, cells0, nz, rank_s, row_a_s, row_b_s, z_s, val_s, left, right_hi, right_lo)
    ys = lax.broadcasted_iota(jnp.int32, (ny, nz), 0)
    zs = lax.broadcasted_iota(jnp.int32, (ny, nz), 1)
    end_y = (ys == 0) | (ys == ny - 1)
    end_z = (zs == 0) | (zs == nz - 1)
    count[...] = jnp.where(end_y, 1.0, 0.0) + jnp.where(end_z, 1.0, 0.0)
    gx_p[...] = jnp.zeros((ny, nz), F32)
    gx_q[...] = jnp.zeros((ny, nz), F32)
    for copy in copies:
        copy.wait()

    def windows(x, carry):
        k = window(k_full[x], off[0], ny)
        kw[x] = k
        kq[x] = k * q[x]
        hb[x] = 0.5 * window(b_full[x], off[0], ny)
        return carry

    lax.fori_loop(0, width, windows, 0)

    def plane(x, carry):
        xn = jnp.minimum(x + 1, width - 1)
        h = hb[x]
        hx = h + hb[xn]
        fy = jnp.where(ys == ny - 1, 0.0, h + up(h, 0))
        fz = jnp.where(zs == nz - 1, 0.0, h + up(h, 1))
        dg = h * count[...]
        fy_o[x] = fy
        fz_o[x] = fz
        dg_o[x] = dg
        here = p[x]
        lap_p, gx = lap_plane(here, p[xn], gx_p[...], hx, fy, fz, dg)
        gx_p[...] = gx
        lap[x] = lap_p
        pn[x] = 2.0 * here - p_old[x] + kw[x] * lap_p
        lap_q, gx = lap_plane(kq[x], kq[xn], gx_q[...], hx, fy, fz, dg)
        gx_q[...] = gx
        at = pl.ds(pl.multiple_of(x * ny, 8), ny)
        qm[x] = 2.0 * q[x] - q_late[x] + lap_q + total[at, 0:nz]
        return carry

    lax.fori_loop(0, width, plane, 0)
    cell = src[0] - cells0

    @pl.when((cell >= 0) & (cell < width * ny * nz))
    def _():
        shift = nz.bit_length() - 1
        row = lax.shift_right_logical(cell, jnp.int32(shift))
        x = lax.div(row, jnp.int32(ny))
        y = row - x * ny
        spot = lax.broadcasted_iota(jnp.int32, (1, nz), 1) == (cell & (nz - 1))
        pn[x, pl.ds(y, 1), :] += jnp.where(spot, wav[step[0]], 0.0)


def edge_one(which, recv, p, kq, kw, hb, lap, pn, qm, send, kept):
    edge = edges(p.shape[0])[which]
    face = hb[edge] + 0.5 * recv[2]
    flux = face * (recv[0] - p[edge])
    kept[0] = lap[edge] + flux
    k = kw[edge]
    send[0] = pn[edge] + k * flux
    mid = qm[edge] + face * (recv[1] - kq[edge])
    kept[1] = mid
    send[1] = k * mid


def step_two(
    off, send_a, kept_a, send_b, kept_b, p, q, kq, kw, hb, fy_i, fz_i, dg_i, lap_i, pn_i, qm_i, total,
    adj_out, last_e, mine, other,
    pn, qm, kqm, last, g_full, gx_s, sem,
):
    width, ny, nz = p.shape
    half = mine.shape[2]
    edge_a, edge_b = edges(width)
    ys = lax.broadcasted_iota(jnp.int32, (ny, nz), 0)
    zs = lax.broadcasted_iota(jnp.int32, (ny, nz), 1)
    gx_s[...] = jnp.zeros(gx_s.shape, F32)

    def gather(x, carry):
        pn[x] = pn_i[x]
        mid = qm_i[x]
        qm[x] = mid
        kqm[x] = kw[x] * mid
        return carry

    lax.fori_loop(0, width, gather, 0)
    for edge, send, kept in ((edge_a, send_a, kept_a), (edge_b, send_b, kept_b)):
        pn[edge] = send[0]
        kqm[edge] = send[1]
        qm[edge] = kept[1]
    mid_copy = pltpu.make_async_copy(qm, adj_out.at[0, 0], sem.at[0])
    mid_copy.start()
    model_y = g_full.shape[2]

    def plane(x, carry):
        xn = jnp.minimum(x + 1, width - 1)
        hx = hb[x] + hb[xn]
        fy = fy_i[x]
        fz = fz_i[x]
        dg = dg_i[x]

        def diffs(ref):
            f = ref[x]
            return f, ref[xn] - f, up(f, 0) - f, up(f, 1) - f

        def lap(d, slot):
            f, dx, dy, dz = d
            gx = hx * dx
            gy = fy * dy
            gz = fz * dz
            out = (gx - gx_s[slot]) + (gy - down(gy, 0)) + (gz - down(gz, 1)) - dg * f
            gx_s[slot] = gx
            return out

        dpn = diffs(pn)
        lap2 = lap(dpn, 0)
        dqm = diffs(kqm)
        at = pl.ds(pl.multiple_of(x * ny, 8), ny)
        last[x] = 2.0 * qm[x] - q[x] + lap(dqm, 1) + total[at, nz : 2 * nz]
        lap1 = jnp.where(x == edge_a, kept_a[0], jnp.where(x == edge_b, kept_b[0], lap_i[x]))
        g_full[0, x] = placed(qm[x] * lap1 + q[x] * lap2, off[0], model_y)
        dp = diffs(p)
        dq = diffs(kq)
        prod = [a * b + c * d for a, b, c, d in zip(dp, dqm, dpn, dq)]
        gb = prod[1]
        gb += jnp.where(ys == ny - 1, prod[0], prod[2])
        gb += jnp.where(zs == nz - 1, prod[0], prod[3])
        g_full[1, x] = placed(-gb, off[0], model_y)
        return carry

    lax.fori_loop(0, width, plane, 0)
    last_copy = pltpu.make_async_copy(last, adj_out.at[0, 1], sem.at[1])
    last_copy.start()
    last_e[0] = last[edge_a]
    last_e[1] = last[edge_b]
    shot = lax.axis_index("shot")
    own = pl.ds(pl.multiple_of(shot * half, 8), half)
    far = pl.ds(pl.multiple_of((1 - shot) * half, 8), half)
    for g in range(2):
        mine[g] = g_full[g, :, own, :]
        other[g] = g_full[g, :, far, :]
    mid_copy.wait()
    last_copy.wait()


def edge_two(
    off, recv_a, recv_b, recv2_a, recv2_b, send_a, send_b, p, q, kq, hb, last_e, adj_in,
    adj_out, mine, other, full, ql, sem,
):
    width, ny, nz = p.shape
    half = mine.shape[1]
    which = edges(width)
    model_y = full.shape[1]
    full[2] = jnp.zeros(full.shape[1:], F32)
    copies = []
    for n, (recv, recv2, send) in enumerate(((recv_a, recv2_a, send_a), (recv_b, recv2_b, send_b))):
        edge = which[n]
        face = hb[edge] + 0.5 * recv[2]
        dpn = recv2[0] - send[0]
        dqm = recv2[1] - send[1]
        ql[n] = last_e[n] + face * dqm
        copy = pltpu.make_async_copy(ql.at[n], adj_out.at[0, 1, edge], sem.at[n])
        copy.start()
        copies.append(copy)
        slot = jnp.where(edge == width - 1, 1, 0)
        full[slot] = placed(q[edge] * (face * dpn), off[0], model_y)

        @pl.when(edge == width - 1)
        def _():
            full[2] = placed(-(dqm * (recv[0] - p[edge]) + dpn * (recv[1] - kq[edge])), off[0], model_y)

    shot = lax.axis_index("shot")
    mine[...] = full[:, pl.ds(pl.multiple_of(shot * half, 8), half), :]
    other[...] = full[:, pl.ds(pl.multiple_of((1 - shot) * half, 8), half), :]
    for copy in copies:
        copy.wait()


def combine(mine, recv, mine_e, recv_e, grad_k, grad_b):
    width = grad_k.shape[0]
    grad_k[...] = mine[0] + recv[0]
    grad_b[...] = mine[1] + recv[1]
    grad_k[0] += mine_e[0] + recv_e[0]
    grad_k[width - 1] += mine_e[1] + recv_e[1]
    grad_b[width - 1] += mine_e[2] + recv_e[2]


def pairs(count, first):
    out = []
    for low in range(first, count - 1, 2):
        out += [(low, low + 1), (low + 1, low)]
    return out


def shards(
    checkpoint, adjoint, kappa, buoyancy, wavelet, src_cell, rec_cell, residuals, offsets, ckpt_step
):
    width, ny, nz = checkpoint.shape[2:]
    model_y = kappa.shape[1]
    half = model_y // 2
    count = lax.axis_size("dom")
    pairs_a = pairs(count, 0)
    pairs_b = pairs(count, 1)
    nrec = rec_cell.shape[1]
    rrows = nrec // LANES
    groups = rrows // GROUP_ROWS
    slots = groups * LANES
    layer = (ny, nz)
    field = (width, ny, nz)
    dma = pltpu.SemaphoreType.DMA

    send_b, send_a = pl.pallas_call(
        first_send,
        in_specs=[SM, ANY, ANY, ANY, ANY],
        out_specs=[VM, VM],
        out_shape=[vmem(3, *layer)] * 2,
        scratch_shapes=[vmem(2, *layer), vmem(2, model_y, nz), vmem(2, model_y, nz), dma((2, 4))],
        compiler_params=params(),
    )(offsets, checkpoint, adjoint, kappa, buoyancy)
    recv_b = lax.ppermute(send_b, "dom", pairs_b)
    recv_a = lax.ppermute(send_a, "dom", pairs_a)

    p, q, kq, kw, hb, fy, fz, dg, lap, pn, qm, total = pl.pallas_call(
        step_one,
        in_specs=[SM, SM, SM, SM, VM, VM, ANY, ANY, ANY, ANY, ANY],
        out_specs=[VM] * 12,
        out_shape=[vmem(*field)] * 11 + [vmem(width * ny, 2 * nz)],
        scratch_shapes=[
            vmem(*field), vmem(*field), vmem(width, model_y, nz), vmem(width, model_y, nz),
            vmem(*layer), vmem(*layer), vmem(*layer),
            vmem(rrows, LANES), vmem(rrows, LANES), vmem(rrows, LANES), vmem(rrows, LANES),
            vmem(4, rrows, LANES),
            pltpu.VMEM((width * ny, slots), BF16),
            pltpu.VMEM((slots, 2 * nz), BF16),
            pltpu.VMEM((slots, 2 * nz), BF16),
            dma((6,)),
        ],
        compiler_params=params(),
        cost_estimate=pl.CostEstimate(flops=10_000_000_000, bytes_accessed=6_000_000, transcendentals=0),
    )(
        offsets, ckpt_step, src_cell, wavelet,
        rec_cell.reshape(rrows, LANES), residuals.reshape(2, rrows, LANES),
        checkpoint, adjoint, kappa, buoyancy, send_a,
    )

    def first_edge(which, recv):
        return pl.pallas_call(
            functools.partial(edge_one, which),
            in_specs=[VM] * 8,
            out_specs=[VM, VM],
            out_shape=[vmem(2, *layer)] * 2,
            compiler_params=params(),
        )(keep(recv), keep(p), keep(kq), keep(kw), keep(hb), keep(lap), keep(pn), keep(qm))

    send2_b, kept_b = first_edge(1, recv_b)
    recv2_b = lax.ppermute(send2_b, "dom", pairs_b)
    send2_a, kept_a = first_edge(0, recv_a)
    recv2_a = lax.ppermute(send2_a, "dom", pairs_a)

    adj_part, last_e, mine, other = pl.pallas_call(
        step_two,
        in_specs=[SM] + [VM] * 16,
        out_specs=[ANY, VM, VM, VM],
        out_shape=[
            jax.ShapeDtypeStruct((1, 2, *field), F32),
            vmem(2, *layer),
            vmem(2, width, half, nz),
            vmem(2, width, half, nz),
        ],
        scratch_shapes=[
            vmem(*field), vmem(*field), vmem(*field), vmem(*field),
            vmem(2, width, model_y, nz), vmem(2, *layer), dma((2,)),
        ],
        compiler_params=params(),
        cost_estimate=pl.CostEstimate(flops=6_000_000_000, bytes_accessed=2_000_000, transcendentals=0),
    )(
        offsets,
        *[keep(v) for v in (send2_a, kept_a, send2_b, kept_b, p, q, kq, kw, hb, fy, fz, dg, lap, pn, qm, total)],
    )
    swap = [(0, 1), (1, 0)]
    recv_g = lax.ppermute(other, "shot", swap)

    adj_next, mine_e, other_e = pl.pallas_call(
        edge_two,
        in_specs=[SM] + [VM] * 11 + [ANY],
        out_specs=[ANY, VM, VM],
        out_shape=[
            jax.ShapeDtypeStruct((1, 2, *field), F32),
            vmem(3, half, nz),
            vmem(3, half, nz),
        ],
        scratch_shapes=[vmem(3, model_y, nz), vmem(2, *layer), dma((2,))],
        input_output_aliases={12: 0},
        compiler_params=params(),
    )(
        offsets,
        *[keep(v) for v in (recv_a, recv_b, recv2_a, recv2_b, send2_a, send2_b, p, q, kq, hb, last_e)],
        adj_part,
    )
    recv_e = lax.ppermute(other_e, "shot", swap)
    grad_k, grad_b = pl.pallas_call(
        combine,
        in_specs=[VM] * 4,
        out_specs=[VM, VM],
        out_shape=[jax.ShapeDtypeStruct((width, half, nz), F32)] * 2,
        compiler_params=params(),
    )(keep(mine), keep(recv_g), keep(mine_e), keep(recv_e))
    return grad_k, grad_b, adj_next


def solution(mesh):
    in_specs = (
        P(("group", "shot"), None, "dom", None, None),
        P(("group", "shot"), None, "dom", None, None),
        P(("group", "dom"), None, None),
        P(("group", "dom"), None, None),
        P(),
        P(("group", "shot")),
        P(("group", "shot"), None),
        P(("group", "shot"), None, None),
        P(("group", "shot")),
        P(("group", "shot")),
    )
    out_specs = (
        P(("group", "dom"), "shot", None),
        P(("group", "dom"), "shot", None),
        P(("group", "shot"), None, "dom", None, None),
    )
    return jax.shard_map(shards, mesh=mesh, in_specs=in_specs, out_specs=out_specs, check_vma=False)
```

```python
import functools

import jax
import jax.numpy as jnp
from jax import lax
from jax.experimental import pallas as pl
from jax.experimental.pallas import tpu as pltpu
from jax.sharding import PartitionSpec as P

F32 = jnp.float32
BF16 = jnp.bfloat16
LANES = 128
GROUP_ROWS = 5

VM = pl.BlockSpec(memory_space=pltpu.VMEM)
SM = pl.BlockSpec(memory_space=pltpu.SMEM)
ANY = pl.BlockSpec(memory_space=pl.ANY)


def vmem(*shape):
    return pltpu.VMEM(shape, F32)


def keep(x):
    return pltpu.with_memory_space_constraint(x, pltpu.VMEM)


def far(x):
    return pltpu.with_memory_space_constraint(x, pltpu.HBM)


def cost(us):
    return pl.CostEstimate(flops=int(us * 1_000_000_000), bytes_accessed=1024, transcendentals=0)


def params():
    return pltpu.CompilerParams(vmem_limit_bytes=24 * 1024 * 1024)


def edges(width):
    even = lax.rem(lax.axis_index("dom"), 2) == 0
    last = jnp.int32(width - 1)
    first = jnp.int32(0)
    return jnp.where(even, last, first), jnp.where(even, first, last)


def window(block, off, ny):
    rows = block.shape[0]
    return pltpu.roll(block, lax.rem(rows - off, rows), 0)[:ny]


def placed(plane, off, rows):
    fill = jnp.zeros((rows - plane.shape[0], plane.shape[1]), plane.dtype)
    return pltpu.roll(jnp.concatenate([plane, fill], axis=0), off, 0)


def up(v, axis):
    return pltpu.roll(v, v.shape[axis] - 1, axis)


def down(v, axis):
    return pltpu.roll(v, 1, axis)


def first_send(off, ckpt, adj, kappa, buoy, send_b, send_a, q_e, k_e, b_e, sem):
    width, ny, nz = ckpt.shape[2:]
    edge_a, edge_b = edges(width)
    copies = []
    for n, (edge, send) in enumerate(((edge_b, send_b), (edge_a, send_a))):
        copies.append(
            (
                pltpu.make_async_copy(ckpt.at[0, 1, edge], send.at[0], sem.at[n, 0]),
                pltpu.make_async_copy(adj.at[0, 1, edge], q_e.at[n], sem.at[n, 1]),
                pltpu.make_async_copy(kappa.at[edge], k_e.at[n], sem.at[n, 2]),
                pltpu.make_async_copy(buoy.at[edge], b_e.at[n], sem.at[n, 3]),
            )
        )
    for group in copies:
        for copy in group:
            copy.start()
    for n, send in enumerate((send_b, send_a)):
        for copy in copies[n]:
            copy.wait()
        send[1] = window(k_e[n], off[0], ny) * q_e[n]
        send[2] = window(b_e[n], off[0], ny)


def receivers(rec, res, total, cells0, nz, rank_s, row_a_s, row_b_s, z_s, val_s, left, right_hi, right_lo):
    rows, lanes = rec.shape
    cells = left.shape[0] * nz
    shift = nz.bit_length() - 1
    local = rec[...] - cells0
    inside = (local >= 0) & (local < cells)
    row = lax.shift_right_logical(local, jnp.int32(shift))
    row_a_s[...] = lax.shift_right_logical(row, jnp.int32(2)).astype(F32)
    row_b_s[...] = (row & 3).astype(F32)
    z_s[...] = (local & (nz - 1)).astype(F32)
    for step in range(2):
        value = res[step]
        high = value.astype(BF16).astype(F32)
        val_s[2 * step] = high
        val_s[2 * step + 1] = value - high
    mask = jnp.where(inside, 1.0, 0.0).astype(BF16)
    before = lax.broadcasted_iota(jnp.int32, (lanes, lanes), 0) < lax.broadcasted_iota(
        jnp.int32, (lanes, lanes), 1
    )
    in_row = jnp.dot(mask, jnp.where(before, 1.0, 0.0).astype(BF16), preferred_element_type=F32)
    row_sum = jnp.dot(mask, jnp.ones((lanes, lanes), BF16), preferred_element_type=F32)
    r = lax.broadcasted_iota(jnp.int32, (rows, rows), 0)
    c = lax.broadcasted_iota(jnp.int32, (rows, rows), 1)
    group_r = lax.shift_right_logical(r * 3277, jnp.int32(14))
    group_c = lax.shift_right_logical(c * 3277, jnp.int32(14))
    earlier = jnp.where((group_r == group_c) & (c < r), 1.0, 0.0).astype(BF16)
    row_start = jnp.dot(earlier, row_sum.astype(BF16), preferred_element_type=F32)
    rank = jnp.where(inside, in_row + row_start, -1.0)
    rank_s[...] = rank
    passes = lax.shift_right_logical(jnp.max(rank).astype(jnp.int32), jnp.int32(7)) + 1
    passes = jnp.maximum(passes, 1)
    groups = rows // GROUP_ROWS
    slot = lax.broadcasted_iota(jnp.int32, (LANES, lanes), 0).astype(F32)
    sub8 = lax.broadcasted_iota(jnp.int32, (8, lanes), 0)
    row_iota = lax.broadcasted_iota(jnp.int32, (left.shape[0], LANES), 0).astype(F32)
    depth_iota = lax.broadcasted_iota(jnp.int32, (LANES, nz), 1).astype(F32)

    def one_pass(number, first):
        base = (number * LANES).astype(F32) if not isinstance(number, int) else float(number * LANES)
        for g in range(groups):
            picks = []
            fields = []
            for n in range(GROUP_ROWS):
                at = pl.ds(g * GROUP_ROWS + n, 1)
                want = jnp.broadcast_to(rank_s[at, :] - base, (LANES, lanes))
                picks.append(jnp.where(want == slot, 1.0, 0.0).astype(BF16))
                data = jnp.zeros((8, lanes), F32)
                sources = [row_a_s, row_b_s, z_s] + [val_s.at[m] for m in range(4)]
                for m, source in enumerate(sources):
                    data = jnp.where(sub8 == m, jnp.broadcast_to(source[at, :], (8, lanes)), data)
                fields.append(data.astype(BF16))
            pick = jnp.concatenate(picks, axis=1)
            data = jnp.concatenate(fields, axis=1)
            dims = (((1,), (1,)), ((), ()))
            by_slot = lax.dot_general(pick, data, dims, preferred_element_type=F32)
            by_field = lax.dot_general(data, pick, dims, preferred_element_type=F32)
            where_row = by_field[0:1, :] * 4.0 + by_field[1:2, :]
            here = pl.ds(g * LANES, LANES)
            left[:, here] = jnp.where(row_iota == where_row, 1.0, 0.0).astype(BF16)
            same = by_slot[:, 2:3] == depth_iota
            for step in range(2):
                cols = pl.ds(step * nz, nz)
                right_hi[here, cols] = jnp.where(same, by_slot[:, 3 + 2 * step : 4 + 2 * step], 0.0).astype(BF16)
                right_lo[here, cols] = jnp.where(same, by_slot[:, 4 + 2 * step : 5 + 2 * step], 0.0).astype(BF16)
        out = jnp.dot(left[...], right_hi[...], preferred_element_type=F32) + jnp.dot(
            left[...], right_lo[...], preferred_element_type=F32
        )
        if first:
            total[...] = out
        else:
            total[...] += out

    one_pass(0, True)

    @pl.when(passes > 1)
    def _():
        def body(number, carry):
            one_pass(number, False)
            return carry

        lax.fori_loop(1, passes, body, 0)


def lap_plane(f, f_next, gx_last, hx, fy, fz, dg):
    gx = hx * (f_next - f)
    gy = fy * (up(f, 0) - f)
    gz = fz * (up(f, 1) - f)
    out = (gx - gx_last) + (gy - down(gy, 0)) + (gz - down(gz, 1)) - dg * f
    return out, gx


def step_one(
    off, step, src, wav, rec, res, ckpt, adj, kappa, buoy, after,
    p, q, kq, kw, hb, fy_o, fz_o, dg_o, lap, pn, qm, total,
    p_old, q_late, k_full, b_full, count, gx_p, gx_q,
    rank_s, row_a_s, row_b_s, z_s, val_s, left, right_hi, right_lo, sem,
):
    width, ny, nz = p.shape
    copies = [
        pltpu.make_async_copy(source, target, sem.at[n])
        for n, (source, target) in enumerate(
            (
                (kappa, k_full), (buoy, b_full), (adj.at[0, 1], q), (ckpt.at[0, 1], p),
                (ckpt.at[0, 0], p_old), (adj.at[0, 0], q_late),
            )
        )
    ]
    for copy in copies:
        copy.start()
    cells0 = lax.axis_index("dom") * (width * ny * nz)
    receivers(rec, res, total, cells0, nz, rank_s, row_a_s, row_b_s, z_s, val_s, left, right_hi, right_lo)
    ys = lax.broadcasted_iota(jnp.int32, (ny, nz), 0)
    zs = lax.broadcasted_iota(jnp.int32, (ny, nz), 1)
    end_y = (ys == 0) | (ys == ny - 1)
    end_z = (zs == 0) | (zs == nz - 1)
    count[...] = jnp.where(end_y, 1.0, 0.0) + jnp.where(end_z, 1.0, 0.0)
    gx_p[...] = jnp.zeros((ny, nz), F32)
    gx_q[...] = jnp.zeros((ny, nz), F32)
    for copy in copies:
        copy.wait()

    def windows(x, carry):
        k = window(k_full[x], off[0], ny)
        kw[x] = k
        kq[x] = k * q[x]
        hb[x] = 0.5 * window(b_full[x], off[0], ny)
        return carry

    lax.fori_loop(0, width, windows, 0)

    def plane(x, carry):
        xn = jnp.minimum(x + 1, width - 1)
        h = hb[x]
        hx = h + hb[xn]
        fy = jnp.where(ys == ny - 1, 0.0, h + up(h, 0))
        fz = jnp.where(zs == nz - 1, 0.0, h + up(h, 1))
        dg = h * count[...]
        fy_o[x] = fy
        fz_o[x] = fz
        dg_o[x] = dg
        here = p[x]
        lap_p, gx = lap_plane(here, p[xn], gx_p[...], hx, fy, fz, dg)
        gx_p[...] = gx
        lap[x] = lap_p
        pn[x] = 2.0 * here - p_old[x] + kw[x] * lap_p
        lap_q, gx = lap_plane(kq[x], kq[xn], gx_q[...], hx, fy, fz, dg)
        gx_q[...] = gx
        at = pl.ds(pl.multiple_of(x * ny, 8), ny)
        qm[x] = 2.0 * q[x] - q_late[x] + lap_q + total[at, 0:nz]
        return carry

    lax.fori_loop(0, width, plane, 0)
    cell = src[0] - cells0

    @pl.when((cell >= 0) & (cell < width * ny * nz))
    def _():
        shift = nz.bit_length() - 1
        row = lax.shift_right_logical(cell, jnp.int32(shift))
        x = lax.div(row, jnp.int32(ny))
        y = row - x * ny
        spot = lax.broadcasted_iota(jnp.int32, (1, nz), 1) == (cell & (nz - 1))
        pn[x, pl.ds(y, 1), :] += jnp.where(spot, wav[step[0]], 0.0)


def edge_one(which, recv, p, kq, kw, hb, lap, pn, qm, send, kept):
    edge = edges(p.shape[0])[which]
    face = hb[edge] + 0.5 * recv[2]
    flux = face * (recv[0] - p[edge])
    kept[0] = lap[edge] + flux
    k = kw[edge]
    send[0] = pn[edge] + k * flux
    mid = qm[edge] + face * (recv[1] - kq[edge])
    kept[1] = mid
    send[1] = k * mid


def step_two(
    off, send_a, kept_a, send_b, kept_b, p, q, kq, kw, hb, fy_i, fz_i, dg_i, lap_i, pn_i, qm_i, total,
    adj_out, last_e, parts,
    pn, qm, kqm, last, gx_s, sem,
):
    width, ny, nz = p.shape
    edge_a, edge_b = edges(width)
    ys = lax.broadcasted_iota(jnp.int32, (ny, nz), 0)
    zs = lax.broadcasted_iota(jnp.int32, (ny, nz), 1)
    gx_s[...] = jnp.zeros(gx_s.shape, F32)

    def gather(x, carry):
        pn[x] = pn_i[x]
        mid = qm_i[x]
        qm[x] = mid
        kqm[x] = kw[x] * mid
        return carry

    lax.fori_loop(0, width, gather, 0)
    for edge, send, kept in ((edge_a, send_a, kept_a), (edge_b, send_b, kept_b)):
        pn[edge] = send[0]
        kqm[edge] = send[1]
        qm[edge] = kept[1]
    mid_copy = pltpu.make_async_copy(qm, adj_out.at[0, 0], sem.at[0])
    mid_copy.start()

    def plane(x, carry):
        xn = jnp.minimum(x + 1, width - 1)
        hx = hb[x] + hb[xn]
        fy = fy_i[x]
        fz = fz_i[x]
        dg = dg_i[x]

        def diffs(ref):
            f = ref[x]
            return f, ref[xn] - f, up(f, 0) - f, up(f, 1) - f

        def lap(d, slot):
            f, dx, dy, dz = d
            gx = hx * dx
            gy = fy * dy
            gz = fz * dz
            out = (gx - gx_s[slot]) + (gy - down(gy, 0)) + (gz - down(gz, 1)) - dg * f
            gx_s[slot] = gx
            return out

        dpn = diffs(pn)
        lap2 = lap(dpn, 0)
        dqm = diffs(kqm)
        at = pl.ds(pl.multiple_of(x * ny, 8), ny)
        last[x] = 2.0 * qm[x] - q[x] + lap(dqm, 1) + total[at, nz : 2 * nz]
        lap1 = jnp.where(x == edge_a, kept_a[0], jnp.where(x == edge_b, kept_b[0], lap_i[x]))
        parts[0, x] = qm[x] * lap1 + q[x] * lap2
        dp = diffs(p)
        dq = diffs(kq)
        prod = [a * b + c * d for a, b, c, d in zip(dp, dqm, dpn, dq)]
        gb = prod[1]
        gb += jnp.where(ys == ny - 1, prod[0], prod[2])
        gb += jnp.where(zs == nz - 1, prod[0], prod[3])
        parts[1, x] = -gb
        return carry

    lax.fori_loop(0, width, plane, 0)
    last_copy = pltpu.make_async_copy(last, adj_out.at[0, 1], sem.at[1])
    last_copy.start()
    last_e[0] = last[edge_a]
    last_e[1] = last[edge_b]
    mid_copy.wait()
    last_copy.wait()


def edge_terms(edge, recv, recv2, send, p, q, kq, hb):
    face = hb[edge] + 0.5 * recv[2]
    dpn = recv2[0] - send[0]
    dqm = recv2[1] - send[1]
    add_k = q[edge] * (face * dpn)
    add_b = -(dqm * (recv[0] - p[edge]) + dpn * (recv[1] - kq[edge]))
    return face * dqm, add_k, jnp.where(edge == p.shape[0] - 1, add_b, 0.0)


def split(plane, off, half):
    whole = placed(plane, off, 2 * half)
    shot = lax.axis_index("shot")
    return (
        jnp.where(shot == 0, whole[:half], whole[half:]),
        jnp.where(shot == 0, whole[half:], whole[:half]),
    )


def edge_b_two(
    off, recv, recv2, send, p, q, kq, hb, last_e, parts, adj_in,
    adj_out, mine, other, add, ql, sem,
):
    width = p.shape[0]
    half = mine.shape[2]
    edge = edges(width)[1]
    add_q, add[0], add[1] = edge_terms(edge, recv, recv2, send, p, q, kq, hb)
    ql[...] = last_e[1] + add_q
    copy = pltpu.make_async_copy(ql, adj_out.at[0, 1, edge], sem.at[0])
    copy.start()

    def plane(x, carry):
        here = jnp.where(x == edge, 1.0, 0.0)
        for g in range(2):
            mine[g, x], other[g, x] = split(parts[g, x] + here * add[g], off[0], half)
        return carry

    lax.fori_loop(0, width, plane, 0)
    copy.wait()


def edge_a_two(
    off, recv, recv2, send, p, q, kq, hb, last_e, adj_in,
    adj_out, mine, other, ql, sem,
):
    width = p.shape[0]
    half = mine.shape[1]
    edge = edges(width)[0]
    add_q, add_k, add_b = edge_terms(edge, recv, recv2, send, p, q, kq, hb)
    ql[...] = last_e[0] + add_q
    copy = pltpu.make_async_copy(ql, adj_out.at[0, 1, edge], sem.at[0])
    copy.start()
    mine[0], other[0] = split(add_k, off[0], half)
    mine[1], other[1] = split(add_b, off[0], half)
    copy.wait()


def combine(mine, recv, mine_e, recv_e, grad_k, grad_b):
    width = grad_k.shape[0]
    edge = edges(width)[0]
    grad_k[...] = mine[0] + recv[0]
    grad_b[...] = mine[1] + recv[1]
    grad_k[edge] += mine_e[0] + recv_e[0]
    grad_b[edge] += mine_e[1] + recv_e[1]


def pairs(count, first):
    out = []
    for low in range(first, count - 1, 2):
        out += [(low, low + 1), (low + 1, low)]
    return out


def shards(
    checkpoint, adjoint, kappa, buoyancy, wavelet, src_cell, rec_cell, residuals, offsets, ckpt_step
):
    width, ny, nz = checkpoint.shape[2:]
    model_y = kappa.shape[1]
    half = model_y // 2
    count = lax.axis_size("dom")
    pairs_a = pairs(count, 0)
    pairs_b = pairs(count, 1)
    nrec = rec_cell.shape[1]
    rrows = nrec // LANES
    groups = rrows // GROUP_ROWS
    slots = groups * LANES
    layer = (ny, nz)
    field = (width, ny, nz)
    dma = pltpu.SemaphoreType.DMA

    inputs = [far(x) for x in (checkpoint, adjoint, kappa, buoyancy)]
    send_b, send_a = pl.pallas_call(
        first_send,
        in_specs=[SM, ANY, ANY, ANY, ANY],
        out_specs=[VM, VM],
        out_shape=[vmem(3, *layer)] * 2,
        scratch_shapes=[vmem(2, *layer), vmem(2, model_y, nz), vmem(2, model_y, nz), dma((2, 4))],
        compiler_params=params(),
    )(offsets, *inputs)
    recv_b = lax.ppermute(send_b, "dom", pairs_b)
    recv_a = lax.ppermute(send_a, "dom", pairs_a)

    p, q, kq, kw, hb, fy, fz, dg, lap, pn, qm, total = pl.pallas_call(
        step_one,
        in_specs=[SM, SM, SM, SM, VM, VM, ANY, ANY, ANY, ANY, VM],
        out_specs=[VM] * 12,
        out_shape=[vmem(*field)] * 11 + [vmem(width * ny, 2 * nz)],
        scratch_shapes=[
            vmem(*field), vmem(*field), vmem(width, model_y, nz), vmem(width, model_y, nz),
            vmem(*layer), vmem(*layer), vmem(*layer),
            vmem(rrows, LANES), vmem(rrows, LANES), vmem(rrows, LANES), vmem(rrows, LANES),
            vmem(4, rrows, LANES),
            pltpu.VMEM((width * ny, slots), BF16),
            pltpu.VMEM((slots, 2 * nz), BF16),
            pltpu.VMEM((slots, 2 * nz), BF16),
            dma((6,)),
        ],
        compiler_params=params(),
        cost_estimate=cost(40),
    )(
        offsets, ckpt_step, src_cell, wavelet,
        rec_cell.reshape(rrows, LANES), residuals.reshape(2, rrows, LANES),
        *inputs, keep(send_a),
    )

    def first_edge(which, recv):
        return pl.pallas_call(
            functools.partial(edge_one, which),
            in_specs=[VM] * 8,
            out_specs=[VM, VM],
            out_shape=[vmem(2, *layer)] * 2,
            compiler_params=params(),
        )(keep(recv), keep(p), keep(kq), keep(kw), keep(hb), keep(lap), keep(pn), keep(qm))

    send2_b, kept_b = first_edge(1, recv_b)
    recv2_b = lax.ppermute(send2_b, "dom", pairs_b)
    send2_a, kept_a = first_edge(0, recv_a)
    recv2_a = lax.ppermute(send2_a, "dom", pairs_a)

    adj_part, last_e, parts = pl.pallas_call(
        step_two,
        in_specs=[SM] + [VM] * 16,
        out_specs=[ANY, VM, VM],
        out_shape=[pltpu.HBM((1, 2, *field), F32), vmem(2, *layer), vmem(2, *field)],
        scratch_shapes=[
            vmem(*field), vmem(*field), vmem(*field), vmem(*field), vmem(2, *layer), dma((2,)),
        ],
        compiler_params=params(),
        cost_estimate=cost(40),
    )(
        offsets,
        *[keep(v) for v in (send2_a, kept_a, send2_b, kept_b, p, q, kq, kw, hb, fy, fz, dg, lap, pn, qm, total)],
    )
    swap = [(0, 1), (1, 0)]
    adj_part, mine, other = pl.pallas_call(
        edge_b_two,
        in_specs=[SM] + [VM] * 9 + [ANY],
        out_specs=[ANY, VM, VM],
        out_shape=[pltpu.HBM((1, 2, *field), F32), vmem(2, width, half, nz), vmem(2, width, half, nz)],
        scratch_shapes=[vmem(2, *layer), vmem(*layer), dma((1,))],
        input_output_aliases={10: 0},
        compiler_params=params(),
        cost_estimate=cost(1),
    )(
        offsets,
        *[keep(v) for v in (recv_b, recv2_b, send2_b, p, q, kq, hb, last_e, parts)],
        far(adj_part),
    )
    recv_g = lax.ppermute(other, "shot", swap)
    adj_next, mine_e, other_e = pl.pallas_call(
        edge_a_two,
        in_specs=[SM] + [VM] * 8 + [ANY],
        out_specs=[ANY, VM, VM],
        out_shape=[pltpu.HBM((1, 2, *field), F32), vmem(2, half, nz), vmem(2, half, nz)],
        scratch_shapes=[vmem(*layer), dma((1,))],
        input_output_aliases={9: 0},
        compiler_params=params(),
        cost_estimate=cost(40),
    )(
        offsets,
        *[keep(v) for v in (recv_a, recv2_a, send2_a, p, q, kq, hb, last_e)],
        far(adj_part),
    )
    recv_e = lax.ppermute(other_e, "shot", swap)
    grad_k, grad_b = pl.pallas_call(
        combine,
        in_specs=[VM] * 4,
        out_specs=[VM, VM],
        out_shape=[jax.ShapeDtypeStruct((width, half, nz), F32)] * 2,
        compiler_params=params(),
    )(keep(mine), keep(recv_g), keep(mine_e), keep(recv_e))
    return grad_k, grad_b, adj_next


def solution(mesh):
    in_specs = (
        P(("group", "shot"), None, "dom", None, None),
        P(("group", "shot"), None, "dom", None, None),
        P(("group", "dom"), None, None),
        P(("group", "dom"), None, None),
        P(),
        P(("group", "shot")),
        P(("group", "shot"), None),
        P(("group", "shot"), None, None),
        P(("group", "shot")),
        P(("group", "shot")),
    )
    out_specs = (
        P(("group", "dom"), "shot", None),
        P(("group", "dom"), "shot", None),
        P(("group", "shot"), None, "dom", None, None),
    )
    return jax.shard_map(shards, mesh=mesh, in_specs=in_specs, out_specs=out_specs, check_vma=False)
```

```python
import functools

import jax
import jax.numpy as jnp
from jax import lax
from jax.experimental import pallas as pl
from jax.experimental.pallas import tpu as pltpu
from jax.sharding import PartitionSpec as P

F32 = jnp.float32
BF16 = jnp.bfloat16
LANES = 128
TILE = 8
GROUP_ROWS = 5
CHUNK = 16
LEAD = 0
RECV_COST = 40
ENDS_COST = 40
MIDDLE_COST = 40
EDGE_COST = 1
TWO_COST = (40, 2)
EDGE_B_COST = 2

VM = pl.BlockSpec(memory_space=pltpu.VMEM)
SM = pl.BlockSpec(memory_space=pltpu.SMEM)
ANY = pl.BlockSpec(memory_space=pl.ANY)


def vmem(*shape):
    return pltpu.VMEM(shape, F32)


def near(x):
    return pltpu.with_memory_space_constraint(x, pltpu.VMEM)


def far(x):
    return pltpu.with_memory_space_constraint(x, pltpu.HBM)


def cost(us):
    return pl.CostEstimate(flops=int(us * 1_000_000_000), bytes_accessed=1024, transcendentals=0)


def params():
    return pltpu.CompilerParams(vmem_limit_bytes=24 * 1024 * 1024)


def edges(width):
    even = lax.rem(lax.axis_index("dom"), 2) == 0
    last = jnp.int32(width - 1)
    first = jnp.int32(0)
    ends = jnp.where(even, last, first), jnp.where(even, first, last)
    return ends[LEAD], ends[1 - LEAD]


def window(block, off, ny):
    rows = block.shape[0]
    return pltpu.roll(block, lax.rem(rows - off, rows), 0)[:ny]


def placed(plane, off, rows):
    fill = jnp.zeros((rows - plane.shape[0], plane.shape[1]), plane.dtype)
    return pltpu.roll(jnp.concatenate([plane, fill], axis=0), off, 0)


def edge_copies(edge, ckpt, adj, kappa, buoy, send, q_e, k_e, b_e, sem):
    return [
        pltpu.make_async_copy(adj.at[0, 1, edge], q_e, sem.at[1]),
        pltpu.make_async_copy(kappa.at[edge], k_e, sem.at[2]),
        pltpu.make_async_copy(buoy.at[edge], b_e, sem.at[3]),
        pltpu.make_async_copy(ckpt.at[0, 1, edge], send.at[0], sem.at[0]),
    ]


def edge_fill(off, send, q_e, k_e, b_e):
    ny = q_e.shape[0]
    send[1] = window(k_e[...], off, ny) * q_e[...]
    send[2] = window(b_e[...], off, ny)


def first_send(off, ckpt, adj, kappa, buoy, send, q_e, k_e, b_e, sem):
    edge = edges(ckpt.shape[2])[0]
    copies = edge_copies(edge, ckpt, adj, kappa, buoy, send, q_e, k_e, b_e, sem)
    for copy in copies:
        copy.start()
    for copy in copies:
        copy.wait()
    edge_fill(off[0], send, q_e, k_e, b_e)


def receivers(
    off, rec, res, ckpt, adj, kappa, buoy, after, total, send,
    q_e, k_e, b_e, cell_s, rank_s, row_a_s, row_b_s, z_s, val_s, left, right_hi, right_lo, sem,
):
    nz = total.shape[1] // 2
    edge = edges(ckpt.shape[2])[1]
    copies = edge_copies(edge, ckpt, adj, kappa, buoy, send, q_e, k_e, b_e, sem)
    for copy in copies:
        copy.start()
    rows, lanes = cell_s.shape
    for r in range(rows):
        at = pl.ds(r * lanes, lanes)
        cell_s[r : r + 1, :] = rec[:, at]
        for step in range(2):
            val_s[2 * step, r : r + 1, :] = res[0, step : step + 1, at]
    cells = total.shape[0] * nz
    shift = nz.bit_length() - 1
    local = cell_s[...] - lax.axis_index("dom") * cells
    inside = (local >= 0) & (local < cells)
    row = lax.shift_right_logical(local, jnp.int32(shift))
    row_a_s[...] = lax.shift_right_logical(row, jnp.int32(2)).astype(F32)
    row_b_s[...] = (row & 3).astype(F32)
    z_s[...] = (local & (nz - 1)).astype(F32)
    for step in range(2):
        value = val_s[2 * step]
        high = value.astype(BF16).astype(F32)
        val_s[2 * step] = high
        val_s[2 * step + 1] = value - high
    mask = jnp.where(inside, 1.0, 0.0).astype(BF16)
    before = lax.broadcasted_iota(jnp.int32, (lanes, lanes), 0) < lax.broadcasted_iota(
        jnp.int32, (lanes, lanes), 1
    )
    in_row = jnp.dot(mask, jnp.where(before, 1.0, 0.0).astype(BF16), preferred_element_type=F32)
    row_sum = jnp.dot(mask, jnp.ones((lanes, lanes), BF16), preferred_element_type=F32)
    r = lax.broadcasted_iota(jnp.int32, (rows, rows), 0)
    c = lax.broadcasted_iota(jnp.int32, (rows, rows), 1)
    group_r = lax.shift_right_logical(r * 3277, jnp.int32(14))
    group_c = lax.shift_right_logical(c * 3277, jnp.int32(14))
    earlier = jnp.where((group_r == group_c) & (c < r), 1.0, 0.0).astype(BF16)
    row_start = jnp.dot(earlier, row_sum.astype(BF16), preferred_element_type=F32)
    rank = jnp.where(inside, in_row + row_start, -1.0)
    rank_s[...] = rank
    passes = lax.shift_right_logical(jnp.max(rank).astype(jnp.int32), jnp.int32(7)) + 1
    groups = rows // GROUP_ROWS
    slot = lax.broadcasted_iota(jnp.int32, (LANES, lanes), 0).astype(F32)
    sub8 = lax.broadcasted_iota(jnp.int32, (TILE, lanes), 0)
    row_iota = lax.broadcasted_iota(jnp.int32, (left.shape[0], LANES), 0).astype(F32)
    depth_iota = lax.broadcasted_iota(jnp.int32, (LANES, nz), 1).astype(F32)

    def one_pass(base, first):
        for g in range(groups):
            picks = []
            fields = []
            for n in range(GROUP_ROWS):
                at = pl.ds(g * GROUP_ROWS + n, 1)
                want = jnp.broadcast_to(rank_s[at, :] - base, (LANES, lanes))
                picks.append(jnp.where(want == slot, 1.0, 0.0).astype(BF16))
                data = jnp.zeros((TILE, lanes), F32)
                sources = [row_a_s, row_b_s, z_s] + [val_s.at[m] for m in range(4)]
                for m, source in enumerate(sources):
                    data = jnp.where(sub8 == m, jnp.broadcast_to(source[at, :], (TILE, lanes)), data)
                fields.append(data.astype(BF16))
            pick = jnp.concatenate(picks, axis=1)
            data = jnp.concatenate(fields, axis=1)
            dims = (((1,), (1,)), ((), ()))
            by_slot = lax.dot_general(pick, data, dims, preferred_element_type=F32)
            by_field = lax.dot_general(data, pick, dims, preferred_element_type=F32)
            where_row = by_field[0:1, :] * 4.0 + by_field[1:2, :]
            here = pl.ds(g * LANES, LANES)
            left[:, here] = jnp.where(row_iota == where_row, 1.0, 0.0).astype(BF16)
            same = by_slot[:, 2:3] == depth_iota
            for step in range(2):
                cols = pl.ds(step * nz, nz)
                high = by_slot[:, 3 + 2 * step : 4 + 2 * step]
                low = by_slot[:, 4 + 2 * step : 5 + 2 * step]
                right_hi[here, cols] = jnp.where(same, high, 0.0).astype(BF16)
                right_lo[here, cols] = jnp.where(same, low, 0.0).astype(BF16)
        out = jnp.dot(left[...], right_hi[...], preferred_element_type=F32) + jnp.dot(
            left[...], right_lo[...], preferred_element_type=F32
        )
        if first:
            total[...] = out
        else:
            total[...] += out

    one_pass(0.0, True)

    @pl.when(passes > 1)
    def _():
        def body(number, carry):
            one_pass((number * LANES).astype(F32), False)
            return carry

        lax.fori_loop(1, passes, body, 0)

    for copy in copies:
        copy.wait()
    edge_fill(off[0], send, q_e, k_e, b_e)


def next_row(f, tile):
    rows = f.shape[0]
    return pltpu.roll(jnp.concatenate([f, tile], axis=0), rows + TILE - 1, 0)[:rows]


def last_row(f, tile):
    return pltpu.roll(jnp.concatenate([tile, f], axis=0), 1, 0)[TILE:]


def next_depth(blocks, end):
    moved = [pltpu.roll(f, LANES - 1, 1) for f in blocks]
    return [jnp.where(end, behind, here) for here, behind in zip(moved, moved[1:] + [0.0])]


def last_depth(blocks, start, first):
    moved = [pltpu.roll(g, 1, 1) for g in blocks]
    return [jnp.where(start, ahead, here) for here, ahead in zip(moved, [first] + moved[:-1])]


class Chunks:
    def __init__(self, ny, nz):
        self.starts = list(range(0, ny, CHUNK))
        self.ny = ny
        self.blocks = nz // LANES
        lane = lax.broadcasted_iota(jnp.int32, (CHUNK, LANES), 1)
        row = lax.broadcasted_iota(jnp.int32, (CHUNK, LANES), 0)
        self.end = lane == LANES - 1
        self.start = lane == 0
        self.top = row == 0

    def load(self, ref, lead, y):
        return [ref[(*lead, pl.ds(y, CHUNK), pl.ds(n * LANES, LANES))] for n in range(self.blocks)]

    def store(self, ref, lead, y, values):
        for n, value in enumerate(values):
            ref[(*lead, pl.ds(y, CHUNK), pl.ds(n * LANES, LANES))] = value

    def behind(self, ref, lead, y):
        if y + CHUNK == self.ny:
            return [jnp.zeros((TILE, LANES), F32)] * self.blocks
        return [
            ref[(*lead, pl.ds(y + CHUNK, TILE), pl.ds(n * LANES, LANES))] for n in range(self.blocks)
        ]

    def rows_up(self, ref, lead, y, f):
        return [next_row(a, b) for a, b in zip(f, self.behind(ref, lead, y))]

    def diffs(self, ref, x, xn, y):
        f = self.load(ref, (x,), y)
        dx = [a - b for a, b in zip(self.load(ref, (xn,), y), f)]
        dy = [a - b for a, b in zip(self.rows_up(ref, (x,), y, f), f)]
        dz = [a - b for a, b in zip(next_depth(f, self.end), f)]
        return f, dx, dy, dz

    def lap(self, d, faces, h, gx_ref, slot, y, carry):
        f, dx, dy, dz = d
        gx, gy, gz = ([a * b for a, b in zip(face, diff)] for face, diff in zip(faces, (dx, dy, dz)))
        old = self.load(gx_ref, (slot,), y)
        self.store(gx_ref, (slot,), y, gx)
        if y == 0:
            ahead = [jnp.where(self.top, a * b, pltpu.roll(g, 1, 0)) for a, b, g in zip(h, f, gy)]
        else:
            ahead = [last_row(g, t) for g, t in zip(gy, carry)]
        back = last_depth(gz, self.start, h[0] * f[0])
        out = [
            (a - b) + (c - e) + (m - n) for a, b, c, e, m, n in zip(gx, old, gy, ahead, gz, back)
        ]
        return out, [g[CHUNK - TILE :] for g in gy]


def one_plane(ch, x, xn, p, q, kq, kw, hb, p_old, q_late, total, fy_o, fz_o, lap_o, pn, qm, kqm, gx_s):
    ny = ch.ny
    tail_p = tail_q = None
    for y in ch.starts:
        h = ch.load(hb, (x,), y)
        fx = [a + b for a, b in zip(h, ch.load(hb, (xn,), y))]
        fy = [a + b for a, b in zip(h, ch.rows_up(hb, (x,), y, h))]
        fz = [a + b for a, b in zip(h, next_depth(h, ch.end))]
        ch.store(fy_o, (x,), y, fy)
        ch.store(fz_o, (x,), y, fz)
        faces = (fx, fy, fz)
        k = ch.load(kw, (x,), y)
        d = ch.diffs(p, x, xn, y)
        lap_p, tail_p = ch.lap(d, faces, h, gx_s, 0, y, tail_p)
        ch.store(lap_o, (x,), y, lap_p)
        old = ch.load(p_old, (x,), y)
        ch.store(pn, (x,), y, [2.0 * a - b + c * e for a, b, c, e in zip(d[0], old, k, lap_p)])
        d = ch.diffs(kq, x, xn, y)
        lap_q, tail_q = ch.lap(d, faces, h, gx_s, 1, y, tail_q)
        now = ch.load(q, (x,), y)
        late = ch.load(q_late, (x,), y)
        at = pl.ds(pl.multiple_of(x * ny + y, TILE), CHUNK)
        add = [total[at, pl.ds(n * LANES, LANES)] for n in range(ch.blocks)]
        mid = [2.0 * a - b + c + e for a, b, c, e in zip(now, late, lap_q, add)]
        ch.store(qm, (x,), y, mid)
        ch.store(kqm, (x,), y, [a * b for a, b in zip(k, mid)])


def add_source(step, src, wav, pn, low, high):
    width, ny, nz = pn.shape
    cell = src[0] - lax.axis_index("dom") * (width * ny * nz)
    plane = ny * nz

    @pl.when((cell >= low * plane) & (cell < high * plane))
    def _():
        shift = nz.bit_length() - 1
        row = lax.shift_right_logical(cell, jnp.int32(shift))
        x = lax.div(row, jnp.int32(ny))
        y = row - x * ny
        spot = lax.broadcasted_iota(jnp.int32, (1, nz), 1) == (cell & (nz - 1))
        pn[x, pl.ds(y, 1), :] += jnp.where(spot, wav[step[0]], 0.0)


def step_one_ends(
    off, step, src, wav_in, ckpt, adj, k_full, b_full, total, after,
    kq, kw, hb, fy, fz, lap, pn, qm, kqm,
    gx_s, wav, sem,
):
    width, ny, nz = kq.shape
    copy = pltpu.make_async_copy(wav_in, wav, sem.at[0])
    copy.start()
    p_old, p, q_late, q = ckpt.at[0, 0], ckpt.at[0, 1], adj.at[0, 0], adj.at[0, 1]

    def windows(x, carry):
        k = window(k_full[x], off[0], ny)
        kw[x] = k
        kq[x] = k * q[x]
        hb[x] = 0.5 * window(b_full[x], off[0], ny)
        return carry

    lax.fori_loop(0, width, windows, 0)
    ch = Chunks(ny, nz)
    end = width - 1
    rest = (p, q, kq, kw, hb, p_old, q_late, total, fy, fz, lap, pn, qm, kqm, gx_s)

    def ends(n, carry):
        x = n * end
        before = jnp.maximum(x - 1, 0)
        face = hb[before] + hb[x]
        gx_s[0] = face * (p[x] - p[before])
        gx_s[1] = face * (kq[x] - kq[before])
        one_plane(ch, x, jnp.minimum(x + 1, end), *rest)
        return carry

    lax.fori_loop(0, 2, ends, 0)
    copy.wait()
    add_source(step, src, wav, pn, 0, 1)
    add_source(step, src, wav, pn, end, width)


def step_one_middle(
    step, src, wav_in, ckpt, adj, kq, kw, hb, total, fy_i, fz_i, lap_i, pn_i, qm_i, kqm_i,
    fy, fz, lap, pn, qm, kqm,
    gx_s, wav, sem,
):
    width, ny, nz = kq.shape
    copy = pltpu.make_async_copy(wav_in, wav, sem.at[0])
    copy.start()
    p_old, p, q_late, q = ckpt.at[0, 0], ckpt.at[0, 1], adj.at[0, 0], adj.at[0, 1]
    ch = Chunks(ny, nz)
    face = hb[0] + hb[1]
    gx_s[0] = face * (p[1] - p[0])
    gx_s[1] = face * (kq[1] - kq[0])

    def plane(x, carry):
        one_plane(ch, x, x + 1, p, q, kq, kw, hb, p_old, q_late, total, fy, fz, lap, pn, qm, kqm, gx_s)
        return carry

    lax.fori_loop(1, width - 1, plane, 0)
    copy.wait()
    add_source(step, src, wav, pn, 1, width - 1)


def edge_one(which, recv, ckpt, kq, kw, hb, lap_i, pn_i, qm_i, kqm_i, send, lap, pn, qm, kqm):
    edge = edges(kq.shape[0])[which]
    p = ckpt.at[0, 1]
    face = hb[edge] + 0.5 * recv[2]
    flux = face * (recv[0] - p[edge])
    lap[edge] = lap_i[edge] + flux
    k = kw[edge]
    new = pn_i[edge] + k * flux
    send[0] = new
    pn[edge] = new
    mid = qm_i[edge] + face * (recv[1] - kq[edge])
    qm[edge] = mid
    mid = k * mid
    send[1] = mid
    kqm[edge] = mid


def step_two(part, ckpt, adj, kq, hb, fy_i, fz_i, lap_i, pn, qm, kqm, total, *refs):
    last, parts, gx_s = refs[-3:]
    width, ny, nz = kq.shape
    p, q = ckpt.at[0, 1], adj.at[0, 1]
    at_end = edges(width)[1] == width - 1
    if part == 0:
        low = jnp.where(at_end, 0, 2)
        high = low + width - 2
    else:
        low = jnp.where(at_end, width - 2, 0)
        high = low + 2
    before = jnp.maximum(low - 1, 0)
    face = hb[before] + hb[low]
    gx_s[0] = face * (pn[low] - pn[before])
    gx_s[1] = face * (kqm[low] - kqm[before])
    ch = Chunks(ny, nz)

    def plane(x, carry):
        xn = jnp.minimum(x + 1, width - 1)
        tail_p = tail_q = None
        for y in ch.starts:
            h = ch.load(hb, (x,), y)
            fx = [a + b for a, b in zip(h, ch.load(hb, (xn,), y))]
            faces = (fx, ch.load(fy_i, (x,), y), ch.load(fz_i, (x,), y))
            dpn = ch.diffs(pn, x, xn, y)
            lap_p, tail_p = ch.lap(dpn, faces, h, gx_s, 0, y, tail_p)
            mid = ch.load(qm, (x,), y)
            now = ch.load(q, (x,), y)
            lap_1 = ch.load(lap_i, (x,), y)
            ch.store(parts, (0, x), y, [a * b + c * e for a, b, c, e in zip(mid, lap_1, now, lap_p)])
            dqm = ch.diffs(kqm, x, xn, y)
            lap_q, tail_q = ch.lap(dqm, faces, h, gx_s, 1, y, tail_q)
            add = [
                total[pl.ds(pl.multiple_of(x * ny + y, TILE), CHUNK), pl.ds(nz + n * LANES, LANES)]
                for n in range(ch.blocks)
            ]
            ch.store(last, (x,), y, [2.0 * a - b + c + e for a, b, c, e in zip(mid, now, lap_q, add)])
            dp = ch.diffs(p, x, xn, y)
            sums = [
                sum(a * b for a, b in zip(u, v))
                for u, v in zip(zip(*dp[1:]), zip(*dqm[1:]))
            ]
            dq = ch.diffs(kq, x, xn, y)
            sums = [
                s + sum(a * b for a, b in zip(u, v))
                for s, u, v in zip(sums, zip(*dpn[1:]), zip(*dq[1:]))
            ]
            ch.store(parts, (1, x), y, [-s for s in sums])
        return carry

    lax.fori_loop(low, high, plane, 0)


def edge_terms(edge, recv, recv2, send, ckpt, adj, kq, hb):
    p, q = ckpt.at[0, 1], adj.at[0, 1]
    face = hb[edge] + 0.5 * recv[2]
    dpn = recv2[0] - send[0]
    dqm = recv2[1] - send[1]
    add_k = q[edge] * (face * dpn)
    add_b = -(dqm * (recv[0] - p[edge]) + dpn * (recv[1] - kq[edge]))
    return face * dqm, add_k, jnp.where(edge == kq.shape[0] - 1, add_b, 0.0)


def split(plane, off, half):
    whole = placed(plane, off, 2 * half)
    shot = lax.axis_index("shot")
    return (
        jnp.where(shot == 0, whole[:half], whole[half:]),
        jnp.where(shot == 0, whole[half:], whole[:half]),
    )


def first_edge_two(
    off, recv, recv2, send, ckpt, adj, kq, hb, last_i, parts, qm,
    adj_out, last, mine, other, add, sem,
):
    width = kq.shape[0]
    mid_copy = pltpu.make_async_copy(qm, adj_out.at[0, 0], sem.at[1])
    mid_copy.start()
    half = mine.shape[2]
    edge = edges(width)[0]
    add_q, add[0], add[1] = edge_terms(edge, recv, recv2, send, ckpt, adj, kq, hb)
    last[edge] = last_i[edge] + add_q
    copy = pltpu.make_async_copy(last, adj_out.at[0, 1], sem.at[0])
    copy.start()

    def plane(x, carry):
        here = jnp.where(x == edge, 1.0, 0.0)
        for g in range(2):
            mine[g, x], other[g, x] = split(parts[g, x] + here * add[g], off[0], half)
        return carry

    lax.fori_loop(0, width, plane, 0)
    copy.wait()
    mid_copy.wait()


def second_edge_two(off, recv, recv2, send, ckpt, adj, kq, hb, last, mine, other, last_e):
    half = mine.shape[1]
    edge = edges(kq.shape[0])[1]
    add_q, add_k, add_b = edge_terms(edge, recv, recv2, send, ckpt, adj, kq, hb)
    last_e[...] = last[edge] + add_q
    mine[0], other[0] = split(add_k, off[0], half)
    mine[1], other[1] = split(add_b, off[0], half)


def combine(mine, recv, mine_e, grad_k, grad_b, sums_e, sums, sem):
    edge = edges(sums.shape[1])[1]
    copies = []
    for g, grad in enumerate((grad_k, grad_b)):
        sums[g] = mine[g] + recv[g]
        copy = pltpu.make_async_copy(sums.at[g], grad, sem.at[g])
        copy.start()
        copies.append(copy)
    for g in range(2):
        sums_e[g] = sums[g, edge] + mine_e[g]
    for copy in copies:
        copy.wait()


def finish(sums_e, recv_e, last_e, grad_k_in, grad_b_in, adj_in, grad_k, grad_b, adj_out, sums, sem):
    edge = edges(grad_k.shape[0])[1]
    copies = [pltpu.make_async_copy(last_e, adj_out.at[0, 1, edge], sem.at[2])]
    copies[0].start()
    for g, grad in enumerate((grad_k, grad_b)):
        sums[g] = sums_e[g] + recv_e[g]
        copy = pltpu.make_async_copy(sums.at[g], grad.at[edge], sem.at[g])
        copy.start()
        copies.append(copy)
    for copy in copies:
        copy.wait()


def pairs(count, first):
    out = []
    for low in range(first, count - 1, 2):
        out += [(low, low + 1), (low + 1, low)]
    return out


def shards(
    checkpoint, adjoint, kappa, buoyancy, wavelet, src_cell, rec_cell, residuals, offsets, ckpt_step
):
    width, ny, nz = checkpoint.shape[2:]
    model_y = kappa.shape[1]
    half = model_y // 2
    count = lax.axis_size("dom")
    swaps = pairs(count, LEAD), pairs(count, 1 - LEAD)
    rrows = rec_cell.shape[1] // LANES
    slots = rrows // GROUP_ROWS * LANES
    layer = (ny, nz)
    field = (width, ny, nz)
    dma = pltpu.SemaphoreType.DMA
    adj_shape = pltpu.HBM((1, 2, *field), F32)
    grad_shape = pltpu.HBM((width, half, nz), F32)

    inputs = [far(x) for x in (checkpoint, adjoint, kappa, buoyancy)]
    edge_scratch = [vmem(*layer), vmem(model_y, nz), vmem(model_y, nz)]
    send_1 = pl.pallas_call(
        first_send,
        in_specs=[SM] + [ANY] * 4,
        out_specs=VM,
        out_shape=vmem(3, *layer),
        scratch_shapes=edge_scratch + [dma((4,))],
        compiler_params=params(),
    )(offsets, *inputs)
    recv_1 = lax.ppermute(send_1, "dom", swaps[0])

    total, send_2 = pl.pallas_call(
        receivers,
        in_specs=[SM, VM, VM] + [ANY] * 4 + [VM],
        out_specs=[VM, VM],
        out_shape=[vmem(width * ny, 2 * nz), vmem(3, *layer)],
        scratch_shapes=edge_scratch + [
            pltpu.VMEM((rrows, LANES), jnp.int32),
            vmem(rrows, LANES), vmem(rrows, LANES), vmem(rrows, LANES), vmem(rrows, LANES),
            vmem(4, rrows, LANES),
            pltpu.VMEM((width * ny, slots), BF16),
            pltpu.VMEM((slots, 2 * nz), BF16),
            pltpu.VMEM((slots, 2 * nz), BF16),
            dma((4,)),
        ],
        compiler_params=params(),
        cost_estimate=cost(RECV_COST),
    )(offsets, near(rec_cell), near(residuals), *inputs, near(send_1))
    recv_2 = lax.ppermute(send_2, "dom", swaps[1])

    kq, kw, hb, *state = pl.pallas_call(
        step_one_ends,
        in_specs=[SM] * 3 + [ANY] + [VM] * 6,
        out_specs=[VM] * 9,
        out_shape=[vmem(*field)] * 9,
        scratch_shapes=[vmem(2, *layer), pltpu.SMEM(wavelet.shape, F32), dma((1,))],
        compiler_params=params(),
        cost_estimate=cost(ENDS_COST),
    )(
        offsets, ckpt_step, src_cell, far(wavelet),
        *[near(v) for v in (checkpoint, adjoint, kappa, buoyancy, total, send_2)],
    )

    def first_edge(which, recv, state):
        send, *new = pl.pallas_call(
            functools.partial(edge_one, which),
            in_specs=[VM] * 9,
            out_specs=[VM] * 5,
            out_shape=[vmem(2, *layer)] + [vmem(*field)] * 4,
            input_output_aliases={5: 1, 6: 2, 7: 3, 8: 4},
            compiler_params=params(),
            cost_estimate=cost(EDGE_COST),
        )(*[near(v) for v in (recv, checkpoint, kq, kw, hb, *state[2:])])
        return send, list(state[:2]) + list(new)

    send2_1, state = first_edge(0, recv_1, state)
    recv2_1 = lax.ppermute(send2_1, "dom", swaps[0])
    state = pl.pallas_call(
        step_one_middle,
        in_specs=[SM] * 2 + [ANY] + [VM] * 12,
        out_specs=[VM] * 6,
        out_shape=[vmem(*field)] * 6,
        scratch_shapes=[vmem(2, *layer), pltpu.SMEM(wavelet.shape, F32), dma((1,))],
        input_output_aliases={9 + n: n for n in range(6)},
        compiler_params=params(),
        cost_estimate=cost(MIDDLE_COST),
    )(
        ckpt_step, src_cell, far(wavelet),
        *[near(v) for v in (checkpoint, adjoint, kq, kw, hb, total, *state)],
    )
    def second_step(part, state, *partial):
        out_shape = [vmem(*field), vmem(2, *field)]
        return pl.pallas_call(
            functools.partial(step_two, part),
            in_specs=[VM] * (11 + len(partial)),
            out_specs=[VM, VM],
            out_shape=out_shape,
            scratch_shapes=[vmem(2, *layer)],
            input_output_aliases={11 + n: n for n in range(len(partial))},
            compiler_params=params(),
            cost_estimate=cost(TWO_COST[part]),
        )(*[near(v) for v in (checkpoint, adjoint, kq, hb, *state, total, *partial)])

    partial = second_step(0, state)
    send2_2, state = first_edge(1, recv_2, state)
    recv2_2 = lax.ppermute(send2_2, "dom", swaps[1])
    last, parts = second_step(1, state, *partial)
    swap = [(0, 1), (1, 0)]
    adj_part, last, mine, other = pl.pallas_call(
        first_edge_two,
        in_specs=[SM] + [VM] * 10,
        out_specs=[ANY, VM, VM, VM],
        out_shape=[adj_shape, vmem(*field), vmem(2, width, half, nz), vmem(2, width, half, nz)],
        scratch_shapes=[vmem(2, *layer), dma((2,))],
        input_output_aliases={8: 1},
        compiler_params=params(),
        cost_estimate=cost(EDGE_B_COST),
    )(
        offsets,
        *[near(v) for v in (recv_1, recv2_1, send2_1, checkpoint, adjoint, kq, hb, last, parts, state[4])],
    )
    recv_g = lax.ppermute(other, "shot", swap)
    mine_e, other_e, last_e = pl.pallas_call(
        second_edge_two,
        in_specs=[SM] + [VM] * 8,
        out_specs=[VM, VM, VM],
        out_shape=[vmem(2, half, nz), vmem(2, half, nz), vmem(*layer)],
        compiler_params=params(),
        cost_estimate=cost(40),
    )(offsets, *[near(v) for v in (recv_2, recv2_2, send2_2, checkpoint, adjoint, kq, hb, last)])
    recv_e = lax.ppermute(other_e, "shot", swap)
    grad_k, grad_b, sums_e = pl.pallas_call(
        combine,
        in_specs=[VM] * 3,
        out_specs=[ANY, ANY, VM],
        out_shape=[grad_shape, grad_shape, vmem(2, half, nz)],
        scratch_shapes=[vmem(2, width, half, nz), dma((2,))],
        compiler_params=params(),
        cost_estimate=cost(40),
    )(near(mine), near(recv_g), near(mine_e))
    return pl.pallas_call(
        finish,
        in_specs=[VM] * 3 + [ANY] * 3,
        out_specs=[ANY] * 3,
        out_shape=[grad_shape, grad_shape, adj_shape],
        scratch_shapes=[vmem(2, half, nz), dma((3,))],
        input_output_aliases={3: 0, 4: 1, 5: 2},
        compiler_params=params(),
    )(near(sums_e), near(recv_e), near(last_e), far(grad_k), far(grad_b), far(adj_part))


def solution(mesh):
    in_specs = (
        P(("group", "shot"), None, "dom", None, None),
        P(("group", "shot"), None, "dom", None, None),
        P(("group", "dom"), None, None),
        P(("group", "dom"), None, None),
        P(),
        P(("group", "shot")),
        P(("group", "shot"), None),
        P(("group", "shot"), None, None),
        P(("group", "shot")),
        P(("group", "shot")),
    )
    out_specs = (
        P(("group", "dom"), "shot", None),
        P(("group", "dom"), "shot", None),
        P(("group", "shot"), None, "dom", None, None),
    )
    return jax.shard_map(shards, mesh=mesh, in_specs=in_specs, out_specs=out_specs, check_vma=False)
```

```python
import functools

import jax
import jax.numpy as jnp
from jax import lax
from jax.experimental import pallas as pl
from jax.experimental.pallas import tpu as pltpu
from jax.sharding import PartitionSpec as P

F32 = jnp.float32
BF16 = jnp.bfloat16
LANES = 128
TILE = 8
GROUP_ROWS = 5
CHUNK = 16
LEAD = 0
RECV_COST = 40
ENDS_COST = 40
MIDDLE_COST = 40
EDGE_COST = 1
TWO_COST = (40, 2)
EDGE_B_COST = 2

VM = pl.BlockSpec(memory_space=pltpu.VMEM)
SM = pl.BlockSpec(memory_space=pltpu.SMEM)
ANY = pl.BlockSpec(memory_space=pl.ANY)


def vmem(*shape):
    return pltpu.VMEM(shape, F32)


def near(x):
    return pltpu.with_memory_space_constraint(x, pltpu.VMEM)


def far(x):
    return pltpu.with_memory_space_constraint(x, pltpu.HBM)


def cost(us):
    return pl.CostEstimate(flops=int(us * 1_000_000_000), bytes_accessed=1024, transcendentals=0)


def params():
    return pltpu.CompilerParams(vmem_limit_bytes=24 * 1024 * 1024)


def edges(width):
    even = lax.rem(lax.axis_index("dom"), 2) == 0
    last = jnp.int32(width - 1)
    first = jnp.int32(0)
    ends = jnp.where(even, last, first), jnp.where(even, first, last)
    return ends[LEAD], ends[1 - LEAD]


def window(ref, lead, off, ny):
    rows, nz = ref.shape[-2:]
    base = jnp.minimum(off - lax.rem(off, TILE), rows - ny - TILE)
    skip = off - base
    block = ref[(*lead, pl.ds(pl.multiple_of(base, TILE), ny + TILE), slice(None))]
    tiles = block.reshape(ny // TILE + 1, TILE, nz)
    tiles = pltpu.roll(tiles, lax.rem(TILE - skip, TILE), 1)
    row = lax.broadcasted_iota(jnp.int32, (ny // TILE, TILE, nz), 1)
    return jnp.where(row < TILE - skip, tiles[:-1], tiles[1:]).reshape(ny, nz)


def placed(plane, off, rows):
    fill = jnp.zeros((rows - plane.shape[0], plane.shape[1]), plane.dtype)
    return pltpu.roll(jnp.concatenate([plane, fill], axis=0), off, 0)


def edge_copies(edge, ckpt, adj, kappa, buoy, send, q_e, k_e, b_e, sem):
    return [
        pltpu.make_async_copy(adj.at[0, 1, edge], q_e, sem.at[1]),
        pltpu.make_async_copy(kappa.at[edge], k_e, sem.at[2]),
        pltpu.make_async_copy(buoy.at[edge], b_e, sem.at[3]),
        pltpu.make_async_copy(ckpt.at[0, 1, edge], send.at[0], sem.at[0]),
    ]


def edge_fill(off, send, q_e, k_e, b_e):
    ny = q_e.shape[0]
    send[1] = window(k_e, (), off, ny) * q_e[...]
    send[2] = window(b_e, (), off, ny)


def first_send(off, ckpt, adj, kappa, buoy, send, q_e, k_e, b_e, sem):
    edge = edges(ckpt.shape[2])[0]
    copies = edge_copies(edge, ckpt, adj, kappa, buoy, send, q_e, k_e, b_e, sem)
    for copy in copies:
        copy.start()
    for copy in copies:
        copy.wait()
    edge_fill(off[0], send, q_e, k_e, b_e)


def receivers(
    off, rec, res, ckpt, adj, kappa, buoy, after, total, send,
    q_e, k_e, b_e, cell_s, rank_s, row_a_s, row_b_s, z_s, val_s, left, right_hi, right_lo, sem,
):
    nz = total.shape[1] // 2
    edge = edges(ckpt.shape[2])[1]
    copies = edge_copies(edge, ckpt, adj, kappa, buoy, send, q_e, k_e, b_e, sem)
    for copy in copies:
        copy.start()
    rows, lanes = cell_s.shape
    for r in range(rows):
        at = pl.ds(r * lanes, lanes)
        cell_s[r : r + 1, :] = rec[:, at]
        for step in range(2):
            val_s[2 * step, r : r + 1, :] = res[0, step : step + 1, at]
    cells = total.shape[0] * nz
    shift = nz.bit_length() - 1
    local = cell_s[...] - lax.axis_index("dom") * cells
    inside = (local >= 0) & (local < cells)
    row = lax.shift_right_logical(local, jnp.int32(shift))
    row_a_s[...] = lax.shift_right_logical(row, jnp.int32(2)).astype(F32)
    row_b_s[...] = (row & 3).astype(F32)
    z_s[...] = (local & (nz - 1)).astype(F32)
    for step in range(2):
        value = val_s[2 * step]
        high = value.astype(BF16).astype(F32)
        val_s[2 * step] = high
        val_s[2 * step + 1] = value - high
    mask = jnp.where(inside, 1.0, 0.0).astype(BF16)
    before = lax.broadcasted_iota(jnp.int32, (lanes, lanes), 0) < lax.broadcasted_iota(
        jnp.int32, (lanes, lanes), 1
    )
    in_row = jnp.dot(mask, jnp.where(before, 1.0, 0.0).astype(BF16), preferred_element_type=F32)
    row_sum = jnp.dot(mask, jnp.ones((lanes, lanes), BF16), preferred_element_type=F32)
    r = lax.broadcasted_iota(jnp.int32, (rows, rows), 0)
    c = lax.broadcasted_iota(jnp.int32, (rows, rows), 1)
    group_r = lax.shift_right_logical(r * 3277, jnp.int32(14))
    group_c = lax.shift_right_logical(c * 3277, jnp.int32(14))
    earlier = jnp.where((group_r == group_c) & (c < r), 1.0, 0.0).astype(BF16)
    row_start = jnp.dot(earlier, row_sum.astype(BF16), preferred_element_type=F32)
    rank = jnp.where(inside, in_row + row_start, -1.0)
    rank_s[...] = rank
    passes = lax.shift_right_logical(jnp.max(rank).astype(jnp.int32), jnp.int32(7)) + 1
    groups = rows // GROUP_ROWS
    slot = lax.broadcasted_iota(jnp.int32, (LANES, lanes), 0).astype(F32)
    sub8 = lax.broadcasted_iota(jnp.int32, (TILE, lanes), 0)
    row_iota = lax.broadcasted_iota(jnp.int32, (left.shape[0], LANES), 0).astype(F32)
    depth_iota = lax.broadcasted_iota(jnp.int32, (LANES, nz), 1).astype(F32)

    def one_pass(base, first):
        for g in range(groups):
            picks = []
            fields = []
            for n in range(GROUP_ROWS):
                at = pl.ds(g * GROUP_ROWS + n, 1)
                want = jnp.broadcast_to(rank_s[at, :] - base, (LANES, lanes))
                picks.append(jnp.where(want == slot, 1.0, 0.0).astype(BF16))
                data = jnp.zeros((TILE, lanes), F32)
                sources = [row_a_s, row_b_s, z_s] + [val_s.at[m] for m in range(4)]
                for m, source in enumerate(sources):
                    data = jnp.where(sub8 == m, jnp.broadcast_to(source[at, :], (TILE, lanes)), data)
                fields.append(data.astype(BF16))
            pick = jnp.concatenate(picks, axis=1)
            data = jnp.concatenate(fields, axis=1)
            dims = (((1,), (1,)), ((), ()))
            by_slot = lax.dot_general(pick, data, dims, preferred_element_type=F32)
            by_field = lax.dot_general(data, pick, dims, preferred_element_type=F32)
            where_row = by_field[0:1, :] * 4.0 + by_field[1:2, :]
            here = pl.ds(g * LANES, LANES)
            left[:, here] = jnp.where(row_iota == where_row, 1.0, 0.0).astype(BF16)
            same = by_slot[:, 2:3] == depth_iota
            for step in range(2):
                cols = pl.ds(step * nz, nz)
                high = by_slot[:, 3 + 2 * step : 4 + 2 * step]
                low = by_slot[:, 4 + 2 * step : 5 + 2 * step]
                right_hi[here, cols] = jnp.where(same, high, 0.0).astype(BF16)
                right_lo[here, cols] = jnp.where(same, low, 0.0).astype(BF16)
        out = jnp.dot(left[...], right_hi[...], preferred_element_type=F32) + jnp.dot(
            left[...], right_lo[...], preferred_element_type=F32
        )
        if first:
            total[...] = out
        else:
            total[...] += out

    one_pass(0.0, True)

    @pl.when(passes > 1)
    def _():
        def body(number, carry):
            one_pass((number * LANES).astype(F32), False)
            return carry

        lax.fori_loop(1, passes, body, 0)

    for copy in copies:
        copy.wait()
    edge_fill(off[0], send, q_e, k_e, b_e)


def next_row(f, tile):
    rows = f.shape[0]
    return pltpu.roll(jnp.concatenate([f, tile], axis=0), rows + TILE - 1, 0)[:rows]


def last_row(f, tile):
    return pltpu.roll(jnp.concatenate([tile, f], axis=0), 1, 0)[TILE:]


def next_depth(blocks, end):
    moved = [pltpu.roll(f, LANES - 1, 1) for f in blocks]
    return [jnp.where(end, behind, here) for here, behind in zip(moved, moved[1:] + [0.0])]


def last_depth(blocks, start, first):
    moved = [pltpu.roll(g, 1, 1) for g in blocks]
    return [jnp.where(start, ahead, here) for here, ahead in zip(moved, [first] + moved[:-1])]


class Chunks:
    def __init__(self, ny, nz):
        self.starts = list(range(0, ny, CHUNK))
        self.ny = ny
        self.blocks = nz // LANES
        lane = lax.broadcasted_iota(jnp.int32, (CHUNK, LANES), 1)
        row = lax.broadcasted_iota(jnp.int32, (CHUNK, LANES), 0)
        self.end = lane == LANES - 1
        self.start = lane == 0
        self.top = row == 0

    def load(self, ref, lead, y):
        return [ref[(*lead, pl.ds(y, CHUNK), pl.ds(n * LANES, LANES))] for n in range(self.blocks)]

    def store(self, ref, lead, y, values):
        for n, value in enumerate(values):
            ref[(*lead, pl.ds(y, CHUNK), pl.ds(n * LANES, LANES))] = value

    def behind(self, ref, lead, y):
        if y + CHUNK == self.ny:
            return [jnp.zeros((TILE, LANES), F32)] * self.blocks
        return [
            ref[(*lead, pl.ds(y + CHUNK, TILE), pl.ds(n * LANES, LANES))] for n in range(self.blocks)
        ]

    def rows_up(self, ref, lead, y, f):
        return [next_row(a, b) for a, b in zip(f, self.behind(ref, lead, y))]

    def diffs(self, ref, x, xn, y):
        f = self.load(ref, (x,), y)
        dx = [a - b for a, b in zip(self.load(ref, (xn,), y), f)]
        dy = [a - b for a, b in zip(self.rows_up(ref, (x,), y, f), f)]
        dz = [a - b for a, b in zip(next_depth(f, self.end), f)]
        return f, dx, dy, dz

    def lap(self, d, faces, h, gx_ref, slot, y, carry):
        f, dx, dy, dz = d
        gx, gy, gz = ([a * b for a, b in zip(face, diff)] for face, diff in zip(faces, (dx, dy, dz)))
        old = self.load(gx_ref, (slot,), y)
        self.store(gx_ref, (slot,), y, gx)
        if y == 0:
            ahead = [jnp.where(self.top, a * b, pltpu.roll(g, 1, 0)) for a, b, g in zip(h, f, gy)]
        else:
            ahead = [last_row(g, t) for g, t in zip(gy, carry)]
        back = last_depth(gz, self.start, h[0] * f[0])
        out = [
            (a - b) + (c - e) + (m - n) for a, b, c, e, m, n in zip(gx, old, gy, ahead, gz, back)
        ]
        return out, [g[CHUNK - TILE :] for g in gy]


def one_plane(ch, x, xn, p, q, kq, kw, hb, p_old, q_late, total, fy_o, fz_o, lap_o, pn, qm, kqm, gx_s):
    ny = ch.ny
    tail_p = tail_q = None
    for y in ch.starts:
        h = ch.load(hb, (x,), y)
        fx = [a + b for a, b in zip(h, ch.load(hb, (xn,), y))]
        fy = [a + b for a, b in zip(h, ch.rows_up(hb, (x,), y, h))]
        fz = [a + b for a, b in zip(h, next_depth(h, ch.end))]
        ch.store(fy_o, (x,), y, fy)
        ch.store(fz_o, (x,), y, fz)
        faces = (fx, fy, fz)
        k = ch.load(kw, (x,), y)
        d = ch.diffs(p, x, xn, y)
        lap_p, tail_p = ch.lap(d, faces, h, gx_s, 0, y, tail_p)
        ch.store(lap_o, (x,), y, lap_p)
        old = ch.load(p_old, (x,), y)
        ch.store(pn, (x,), y, [2.0 * a - b + c * e for a, b, c, e in zip(d[0], old, k, lap_p)])
        d = ch.diffs(kq, x, xn, y)
        lap_q, tail_q = ch.lap(d, faces, h, gx_s, 1, y, tail_q)
        now = ch.load(q, (x,), y)
        late = ch.load(q_late, (x,), y)
        at = pl.ds(pl.multiple_of(x * ny + y, TILE), CHUNK)
        add = [total[at, pl.ds(n * LANES, LANES)] for n in range(ch.blocks)]
        mid = [2.0 * a - b + c + e for a, b, c, e in zip(now, late, lap_q, add)]
        ch.store(qm, (x,), y, mid)
        ch.store(kqm, (x,), y, [a * b for a, b in zip(k, mid)])


def add_source(step, src, wav, pn, low, high):
    width, ny, nz = pn.shape
    cell = src[0] - lax.axis_index("dom") * (width * ny * nz)
    plane = ny * nz

    @pl.when((cell >= low * plane) & (cell < high * plane))
    def _():
        shift = nz.bit_length() - 1
        row = lax.shift_right_logical(cell, jnp.int32(shift))
        x = lax.div(row, jnp.int32(ny))
        y = row - x * ny
        spot = lax.broadcasted_iota(jnp.int32, (1, nz), 1) == (cell & (nz - 1))
        pn[x, pl.ds(y, 1), :] += jnp.where(spot, wav[step[0]], 0.0)


def step_one_ends(
    off, step, src, wav_in, ckpt, adj, k_full, b_full, total, after,
    kq, kw, hb, fy, fz, lap, pn, qm, kqm,
    gx_s, wav, sem,
):
    width, ny, nz = kq.shape
    copy = pltpu.make_async_copy(wav_in, wav, sem.at[0])
    copy.start()
    p_old, p, q_late, q = ckpt.at[0, 0], ckpt.at[0, 1], adj.at[0, 0], adj.at[0, 1]

    def windows(x, carry):
        k = window(k_full, (x,), off[0], ny)
        kw[x] = k
        kq[x] = k * q[x]
        hb[x] = 0.5 * window(b_full, (x,), off[0], ny)
        return carry

    lax.fori_loop(0, width, windows, 0)
    ch = Chunks(ny, nz)
    end = width - 1
    rest = (p, q, kq, kw, hb, p_old, q_late, total, fy, fz, lap, pn, qm, kqm, gx_s)

    def ends(n, carry):
        x = n * end
        before = jnp.maximum(x - 1, 0)
        face = hb[before] + hb[x]
        gx_s[0] = face * (p[x] - p[before])
        gx_s[1] = face * (kq[x] - kq[before])
        one_plane(ch, x, jnp.minimum(x + 1, end), *rest)
        return carry

    lax.fori_loop(0, 2, ends, 0)
    copy.wait()
    add_source(step, src, wav, pn, 0, 1)
    add_source(step, src, wav, pn, end, width)


def step_one_middle(
    step, src, wav_in, ckpt, adj, kq, kw, hb, total, fy_i, fz_i, lap_i, pn_i, qm_i, kqm_i,
    fy, fz, lap, pn, qm, kqm,
    gx_s, wav, sem,
):
    width, ny, nz = kq.shape
    copy = pltpu.make_async_copy(wav_in, wav, sem.at[0])
    copy.start()
    p_old, p, q_late, q = ckpt.at[0, 0], ckpt.at[0, 1], adj.at[0, 0], adj.at[0, 1]
    ch = Chunks(ny, nz)
    face = hb[0] + hb[1]
    gx_s[0] = face * (p[1] - p[0])
    gx_s[1] = face * (kq[1] - kq[0])

    def plane(x, carry):
        one_plane(ch, x, x + 1, p, q, kq, kw, hb, p_old, q_late, total, fy, fz, lap, pn, qm, kqm, gx_s)
        return carry

    lax.fori_loop(1, width - 1, plane, 0)
    copy.wait()
    add_source(step, src, wav, pn, 1, width - 1)


def edge_one(which, recv, ckpt, kq, kw, hb, lap_i, pn_i, qm_i, kqm_i, send, lap, pn, qm, kqm):
    edge = edges(kq.shape[0])[which]
    p = ckpt.at[0, 1]
    face = hb[edge] + 0.5 * recv[2]
    flux = face * (recv[0] - p[edge])
    lap[edge] = lap_i[edge] + flux
    k = kw[edge]
    new = pn_i[edge] + k * flux
    send[0] = new
    pn[edge] = new
    mid = qm_i[edge] + face * (recv[1] - kq[edge])
    qm[edge] = mid
    mid = k * mid
    send[1] = mid
    kqm[edge] = mid


def step_two(part, ckpt, adj, kq, hb, fy_i, fz_i, lap_i, pn, qm, kqm, total, *refs):
    last, parts, gx_s = refs[-3:]
    width, ny, nz = kq.shape
    p, q = ckpt.at[0, 1], adj.at[0, 1]
    at_end = edges(width)[1] == width - 1
    if part == 0:
        low = jnp.where(at_end, 0, 2)
        high = low + width - 2
    else:
        low = jnp.where(at_end, width - 2, 0)
        high = low + 2
    before = jnp.maximum(low - 1, 0)
    face = hb[before] + hb[low]
    gx_s[0] = face * (pn[low] - pn[before])
    gx_s[1] = face * (kqm[low] - kqm[before])
    ch = Chunks(ny, nz)

    def plane(x, carry):
        xn = jnp.minimum(x + 1, width - 1)
        tail_p = tail_q = None
        for y in ch.starts:
            h = ch.load(hb, (x,), y)
            fx = [a + b for a, b in zip(h, ch.load(hb, (xn,), y))]
            faces = (fx, ch.load(fy_i, (x,), y), ch.load(fz_i, (x,), y))
            dpn = ch.diffs(pn, x, xn, y)
            lap_p, tail_p = ch.lap(dpn, faces, h, gx_s, 0, y, tail_p)
            mid = ch.load(qm, (x,), y)
            now = ch.load(q, (x,), y)
            lap_1 = ch.load(lap_i, (x,), y)
            ch.store(parts, (0, x), y, [a * b + c * e for a, b, c, e in zip(mid, lap_1, now, lap_p)])
            dqm = ch.diffs(kqm, x, xn, y)
            lap_q, tail_q = ch.lap(dqm, faces, h, gx_s, 1, y, tail_q)
            add = [
                total[pl.ds(pl.multiple_of(x * ny + y, TILE), CHUNK), pl.ds(nz + n * LANES, LANES)]
                for n in range(ch.blocks)
            ]
            ch.store(last, (x,), y, [2.0 * a - b + c + e for a, b, c, e in zip(mid, now, lap_q, add)])
            dp = ch.diffs(p, x, xn, y)
            sums = [
                sum(a * b for a, b in zip(u, v))
                for u, v in zip(zip(*dp[1:]), zip(*dqm[1:]))
            ]
            dq = ch.diffs(kq, x, xn, y)
            sums = [
                s + sum(a * b for a, b in zip(u, v))
                for s, u, v in zip(sums, zip(*dpn[1:]), zip(*dq[1:]))
            ]
            ch.store(parts, (1, x), y, [-s for s in sums])
        return carry

    lax.fori_loop(low, high, plane, 0)


def edge_terms(edge, recv, recv2, send, ckpt, adj, kq, hb):
    p, q = ckpt.at[0, 1], adj.at[0, 1]
    face = hb[edge] + 0.5 * recv[2]
    dpn = recv2[0] - send[0]
    dqm = recv2[1] - send[1]
    add_k = q[edge] * (face * dpn)
    add_b = -(dqm * (recv[0] - p[edge]) + dpn * (recv[1] - kq[edge]))
    return face * dqm, add_k, jnp.where(edge == kq.shape[0] - 1, add_b, 0.0)


def split(plane, off, half):
    whole = placed(plane, off, 2 * half)
    shot = lax.axis_index("shot")
    return (
        jnp.where(shot == 0, whole[:half], whole[half:]),
        jnp.where(shot == 0, whole[half:], whole[:half]),
    )


def first_edge_two(
    off, recv, recv2, send, ckpt, adj, kq, hb, last_i, parts, qm,
    adj_out, last, mine, other, add, sem,
):
    width = kq.shape[0]
    mid_copy = pltpu.make_async_copy(qm, adj_out.at[0, 0], sem.at[1])
    mid_copy.start()
    half = mine.shape[2]
    edge = edges(width)[0]
    add_q, add[0], add[1] = edge_terms(edge, recv, recv2, send, ckpt, adj, kq, hb)
    last[edge] = last_i[edge] + add_q
    copy = pltpu.make_async_copy(last, adj_out.at[0, 1], sem.at[0])
    copy.start()

    def plane(x, carry):
        here = jnp.where(x == edge, 1.0, 0.0)
        for g in range(2):
            mine[g, x], other[g, x] = split(parts[g, x] + here * add[g], off[0], half)
        return carry

    lax.fori_loop(0, width, plane, 0)
    copy.wait()
    mid_copy.wait()


def second_edge_two(off, recv, recv2, send, ckpt, adj, kq, hb, last, mine, other, last_e):
    half = mine.shape[1]
    edge = edges(kq.shape[0])[1]
    add_q, add_k, add_b = edge_terms(edge, recv, recv2, send, ckpt, adj, kq, hb)
    last_e[...] = last[edge] + add_q
    mine[0], other[0] = split(add_k, off[0], half)
    mine[1], other[1] = split(add_b, off[0], half)


def combine(mine, recv, mine_e, grad_k, grad_b, sums_e, sums, sem):
    edge = edges(sums.shape[1])[1]
    copies = []
    for g, grad in enumerate((grad_k, grad_b)):
        sums[g] = mine[g] + recv[g]
        copy = pltpu.make_async_copy(sums.at[g], grad, sem.at[g])
        copy.start()
        copies.append(copy)
    for g in range(2):
        sums_e[g] = sums[g, edge] + mine_e[g]
    for copy in copies:
        copy.wait()


def finish(sums_e, recv_e, last_e, grad_k_in, grad_b_in, adj_in, grad_k, grad_b, adj_out, sums, sem):
    edge = edges(grad_k.shape[0])[1]
    copies = [pltpu.make_async_copy(last_e, adj_out.at[0, 1, edge], sem.at[2])]
    copies[0].start()
    for g, grad in enumerate((grad_k, grad_b)):
        sums[g] = sums_e[g] + recv_e[g]
        copy = pltpu.make_async_copy(sums.at[g], grad.at[edge], sem.at[g])
        copy.start()
        copies.append(copy)
    for copy in copies:
        copy.wait()


def pairs(count, first):
    out = []
    for low in range(first, count - 1, 2):
        out += [(low, low + 1), (low + 1, low)]
    return out


def shards(
    checkpoint, adjoint, kappa, buoyancy, wavelet, src_cell, rec_cell, residuals, offsets, ckpt_step
):
    width, ny, nz = checkpoint.shape[2:]
    model_y = kappa.shape[1]
    half = model_y // 2
    count = lax.axis_size("dom")
    swaps = pairs(count, LEAD), pairs(count, 1 - LEAD)
    rrows = rec_cell.shape[1] // LANES
    slots = rrows // GROUP_ROWS * LANES
    layer = (ny, nz)
    field = (width, ny, nz)
    dma = pltpu.SemaphoreType.DMA
    adj_shape = pltpu.HBM((1, 2, *field), F32)
    grad_shape = pltpu.HBM((width, half, nz), F32)

    inputs = [far(x) for x in (checkpoint, adjoint, kappa, buoyancy)]
    edge_scratch = [vmem(*layer), vmem(model_y, nz), vmem(model_y, nz)]
    send_1 = pl.pallas_call(
        first_send,
        in_specs=[SM] + [ANY] * 4,
        out_specs=VM,
        out_shape=vmem(3, *layer),
        scratch_shapes=edge_scratch + [dma((4,))],
        compiler_params=params(),
    )(offsets, *inputs)
    recv_1 = lax.ppermute(send_1, "dom", swaps[0])

    total, send_2 = pl.pallas_call(
        receivers,
        in_specs=[SM, VM, VM] + [ANY] * 4 + [VM],
        out_specs=[VM, VM],
        out_shape=[vmem(width * ny, 2 * nz), vmem(3, *layer)],
        scratch_shapes=edge_scratch + [
            pltpu.VMEM((rrows, LANES), jnp.int32),
            vmem(rrows, LANES), vmem(rrows, LANES), vmem(rrows, LANES), vmem(rrows, LANES),
            vmem(4, rrows, LANES),
            pltpu.VMEM((width * ny, slots), BF16),
            pltpu.VMEM((slots, 2 * nz), BF16),
            pltpu.VMEM((slots, 2 * nz), BF16),
            dma((4,)),
        ],
        compiler_params=params(),
        cost_estimate=cost(RECV_COST),
    )(offsets, near(rec_cell), near(residuals), *inputs, near(send_1))
    recv_2 = lax.ppermute(send_2, "dom", swaps[1])

    kq, kw, hb, *state = pl.pallas_call(
        step_one_ends,
        in_specs=[SM] * 3 + [ANY] + [VM] * 6,
        out_specs=[VM] * 9,
        out_shape=[vmem(*field)] * 9,
        scratch_shapes=[vmem(2, *layer), pltpu.SMEM(wavelet.shape, F32), dma((1,))],
        compiler_params=params(),
        cost_estimate=cost(ENDS_COST),
    )(
        offsets, ckpt_step, src_cell, far(wavelet),
        *[near(v) for v in (checkpoint, adjoint, kappa, buoyancy, total, send_2)],
    )

    def first_edge(which, recv, state):
        send, *new = pl.pallas_call(
            functools.partial(edge_one, which),
            in_specs=[VM] * 9,
            out_specs=[VM] * 5,
            out_shape=[vmem(2, *layer)] + [vmem(*field)] * 4,
            input_output_aliases={5: 1, 6: 2, 7: 3, 8: 4},
            compiler_params=params(),
            cost_estimate=cost(EDGE_COST),
        )(*[near(v) for v in (recv, checkpoint, kq, kw, hb, *state[2:])])
        return send, list(state[:2]) + list(new)

    send2_1, state = first_edge(0, recv_1, state)
    recv2_1 = lax.ppermute(send2_1, "dom", swaps[0])
    state = pl.pallas_call(
        step_one_middle,
        in_specs=[SM] * 2 + [ANY] + [VM] * 12,
        out_specs=[VM] * 6,
        out_shape=[vmem(*field)] * 6,
        scratch_shapes=[vmem(2, *layer), pltpu.SMEM(wavelet.shape, F32), dma((1,))],
        input_output_aliases={9 + n: n for n in range(6)},
        compiler_params=params(),
        cost_estimate=cost(MIDDLE_COST),
    )(
        ckpt_step, src_cell, far(wavelet),
        *[near(v) for v in (checkpoint, adjoint, kq, kw, hb, total, *state)],
    )
    def second_step(part, state, *partial):
        out_shape = [vmem(*field), vmem(2, *field)]
        return pl.pallas_call(
            functools.partial(step_two, part),
            in_specs=[VM] * (11 + len(partial)),
            out_specs=[VM, VM],
            out_shape=out_shape,
            scratch_shapes=[vmem(2, *layer)],
            input_output_aliases={11 + n: n for n in range(len(partial))},
            compiler_params=params(),
            cost_estimate=cost(TWO_COST[part]),
        )(*[near(v) for v in (checkpoint, adjoint, kq, hb, *state, total, *partial)])

    partial = second_step(0, state)
    send2_2, state = first_edge(1, recv_2, state)
    recv2_2 = lax.ppermute(send2_2, "dom", swaps[1])
    last, parts = second_step(1, state, *partial)
    swap = [(0, 1), (1, 0)]
    adj_part, last, mine, other = pl.pallas_call(
        first_edge_two,
        in_specs=[SM] + [VM] * 10,
        out_specs=[ANY, VM, VM, VM],
        out_shape=[adj_shape, vmem(*field), vmem(2, width, half, nz), vmem(2, width, half, nz)],
        scratch_shapes=[vmem(2, *layer), dma((2,))],
        input_output_aliases={8: 1},
        compiler_params=params(),
        cost_estimate=cost(EDGE_B_COST),
    )(
        offsets,
        *[near(v) for v in (recv_1, recv2_1, send2_1, checkpoint, adjoint, kq, hb, last, parts, state[4])],
    )
    recv_g = lax.ppermute(other, "shot", swap)
    mine_e, other_e, last_e = pl.pallas_call(
        second_edge_two,
        in_specs=[SM] + [VM] * 8,
        out_specs=[VM, VM, VM],
        out_shape=[vmem(2, half, nz), vmem(2, half, nz), vmem(*layer)],
        compiler_params=params(),
        cost_estimate=cost(40),
    )(offsets, *[near(v) for v in (recv_2, recv2_2, send2_2, checkpoint, adjoint, kq, hb, last)])
    recv_e = lax.ppermute(other_e, "shot", swap)
    grad_k, grad_b, sums_e = pl.pallas_call(
        combine,
        in_specs=[VM] * 3,
        out_specs=[ANY, ANY, VM],
        out_shape=[grad_shape, grad_shape, vmem(2, half, nz)],
        scratch_shapes=[vmem(2, width, half, nz), dma((2,))],
        compiler_params=params(),
        cost_estimate=cost(40),
    )(near(mine), near(recv_g), near(mine_e))
    return pl.pallas_call(
        finish,
        in_specs=[VM] * 3 + [ANY] * 3,
        out_specs=[ANY] * 3,
        out_shape=[grad_shape, grad_shape, adj_shape],
        scratch_shapes=[vmem(2, half, nz), dma((3,))],
        input_output_aliases={3: 0, 4: 1, 5: 2},
        compiler_params=params(),
    )(near(sums_e), near(recv_e), near(last_e), far(grad_k), far(grad_b), far(adj_part))


def solution(mesh):
    in_specs = (
        P(("group", "shot"), None, "dom", None, None),
        P(("group", "shot"), None, "dom", None, None),
        P(("group", "dom"), None, None),
        P(("group", "dom"), None, None),
        P(),
        P(("group", "shot")),
        P(("group", "shot"), None),
        P(("group", "shot"), None, None),
        P(("group", "shot")),
        P(("group", "shot")),
    )
    out_specs = (
        P(("group", "dom"), "shot", None),
        P(("group", "dom"), "shot", None),
        P(("group", "shot"), None, "dom", None, None),
    )
    return jax.shard_map(shards, mesh=mesh, in_specs=in_specs, out_specs=out_specs, check_vma=False)
```

```python
import functools

import jax
import jax.numpy as jnp
from jax import lax
from jax.experimental import pallas as pl
from jax.experimental.pallas import tpu as pltpu
from jax.sharding import PartitionSpec as P

F32 = jnp.float32
BF16 = jnp.bfloat16
LANES = 128
TILE = 8
GROUP_ROWS = 5
CHUNK = 16
LEAD = 0
RECV_COST = 40
ENDS_COST = 40
MIDDLE_COST = 40
EDGE_COST = 1
TWO_COST = (40, 2)
EDGE_B_COST = 2

VM = pl.BlockSpec(memory_space=pltpu.VMEM)
SM = pl.BlockSpec(memory_space=pltpu.SMEM)
ANY = pl.BlockSpec(memory_space=pl.ANY)


def vmem(*shape):
    return pltpu.VMEM(shape, F32)


def near(x):
    return pltpu.with_memory_space_constraint(x, pltpu.VMEM)


def far(x):
    return pltpu.with_memory_space_constraint(x, pltpu.HBM)


def cost(us):
    return pl.CostEstimate(flops=int(us * 1_000_000_000), bytes_accessed=1024, transcendentals=0)


def params():
    return pltpu.CompilerParams(vmem_limit_bytes=24 * 1024 * 1024)


def edges(width):
    even = lax.rem(lax.axis_index("dom"), 2) == 0
    last = jnp.int32(width - 1)
    first = jnp.int32(0)
    ends = jnp.where(even, last, first), jnp.where(even, first, last)
    return ends[LEAD], ends[1 - LEAD]


def window(ref, lead, off, ny):
    rows, nz = ref.shape[-2:]
    base = jnp.minimum(off - lax.rem(off, TILE), rows - ny - TILE)
    skip = off - base
    block = ref[(*lead, pl.ds(pl.multiple_of(base, TILE), ny + TILE), slice(None))]
    tiles = block.reshape(ny // TILE + 1, TILE, nz)
    tiles = pltpu.roll(tiles, lax.rem(TILE - skip, TILE), 1)
    row = lax.broadcasted_iota(jnp.int32, (ny // TILE, TILE, nz), 1)
    return jnp.where(row < TILE - skip, tiles[:-1], tiles[1:]).reshape(ny, nz)


def placed(plane, off, rows):
    fill = jnp.zeros((rows - plane.shape[0], plane.shape[1]), plane.dtype)
    return pltpu.roll(jnp.concatenate([plane, fill], axis=0), off, 0)


def edge_copies(edge, ckpt, adj, kappa, buoy, send, q_e, k_e, b_e, sem):
    return [
        pltpu.make_async_copy(adj.at[0, 1, edge], q_e, sem.at[1]),
        pltpu.make_async_copy(kappa.at[edge], k_e, sem.at[2]),
        pltpu.make_async_copy(buoy.at[edge], b_e, sem.at[3]),
        pltpu.make_async_copy(ckpt.at[0, 1, edge], send.at[0], sem.at[0]),
    ]


def edge_fill(off, send, q_e, k_e, b_e):
    ny = q_e.shape[0]
    send[1] = window(k_e, (), off, ny) * q_e[...]
    send[2] = window(b_e, (), off, ny)


def first_send(off, ckpt, adj, kappa, buoy, send, q_e, k_e, b_e, sem):
    edge = edges(ckpt.shape[2])[0]
    copies = edge_copies(edge, ckpt, adj, kappa, buoy, send, q_e, k_e, b_e, sem)
    for copy in copies:
        copy.start()
    for copy in copies:
        copy.wait()
    edge_fill(off[0], send, q_e, k_e, b_e)


def receiver_sums(left, right_hi, right_lo, step, nz):
    cols = pl.ds(step * nz, nz)
    return jnp.dot(left[...], right_hi[:, cols], preferred_element_type=F32) + jnp.dot(
        left[...], right_lo[:, cols], preferred_element_type=F32
    )


def receivers(
    off, rec, res, ckpt, adj, kappa, buoy, after, total_1, total_2, send, left, right_hi, right_lo, later,
    q_e, k_e, b_e, cell_s, rank_s, row_a_s, row_b_s, z_s, val_s, sem,
):
    nz = total_1.shape[1]
    edge = edges(ckpt.shape[2])[1]
    copies = edge_copies(edge, ckpt, adj, kappa, buoy, send, q_e, k_e, b_e, sem)
    for copy in copies:
        copy.start()
    rows, lanes = cell_s.shape
    for r in range(rows):
        at = pl.ds(r * lanes, lanes)
        cell_s[r : r + 1, :] = rec[:, at]
        for step in range(2):
            val_s[2 * step, r : r + 1, :] = res[0, step : step + 1, at]
    cells = total_1.shape[0] * nz
    shift = nz.bit_length() - 1
    local = cell_s[...] - lax.axis_index("dom") * cells
    inside = (local >= 0) & (local < cells)
    row = lax.shift_right_logical(local, jnp.int32(shift))
    row_a_s[...] = lax.shift_right_logical(row, jnp.int32(2)).astype(F32)
    row_b_s[...] = (row & 3).astype(F32)
    z_s[...] = (local & (nz - 1)).astype(F32)
    for step in range(2):
        value = val_s[2 * step]
        high = value.astype(BF16).astype(F32)
        val_s[2 * step] = high
        val_s[2 * step + 1] = value - high
    mask = jnp.where(inside, 1.0, 0.0).astype(BF16)
    before = lax.broadcasted_iota(jnp.int32, (lanes, lanes), 0) < lax.broadcasted_iota(
        jnp.int32, (lanes, lanes), 1
    )
    in_row = jnp.dot(mask, jnp.where(before, 1.0, 0.0).astype(BF16), preferred_element_type=F32)
    row_sum = jnp.dot(mask, jnp.ones((lanes, lanes), BF16), preferred_element_type=F32)
    r = lax.broadcasted_iota(jnp.int32, (rows, rows), 0)
    c = lax.broadcasted_iota(jnp.int32, (rows, rows), 1)
    group_r = lax.shift_right_logical(r * 3277, jnp.int32(14))
    group_c = lax.shift_right_logical(c * 3277, jnp.int32(14))
    earlier = jnp.where((group_r == group_c) & (c < r), 1.0, 0.0).astype(BF16)
    row_start = jnp.dot(earlier, row_sum.astype(BF16), preferred_element_type=F32)
    rank = jnp.where(inside, in_row + row_start, -1.0)
    rank_s[...] = rank
    passes = lax.shift_right_logical(jnp.max(rank).astype(jnp.int32), jnp.int32(7)) + 1
    leave = (lax.rem(lax.axis_index("dom"), 2) == 0) & (passes <= 1)
    later[0] = jnp.where(leave, 1, 0)
    groups = rows // GROUP_ROWS
    slot = lax.broadcasted_iota(jnp.int32, (LANES, lanes), 0).astype(F32)
    sub8 = lax.broadcasted_iota(jnp.int32, (TILE, lanes), 0)
    row_iota = lax.broadcasted_iota(jnp.int32, (left.shape[0], LANES), 0).astype(F32)
    depth_iota = lax.broadcasted_iota(jnp.int32, (LANES, nz), 1).astype(F32)

    def one_pass(base, first):
        for g in range(groups):
            picks = []
            fields = []
            for n in range(GROUP_ROWS):
                at = pl.ds(g * GROUP_ROWS + n, 1)
                want = jnp.broadcast_to(rank_s[at, :] - base, (LANES, lanes))
                picks.append(jnp.where(want == slot, 1.0, 0.0).astype(BF16))
                data = jnp.zeros((TILE, lanes), F32)
                sources = [row_a_s, row_b_s, z_s] + [val_s.at[m] for m in range(4)]
                for m, source in enumerate(sources):
                    data = jnp.where(sub8 == m, jnp.broadcast_to(source[at, :], (TILE, lanes)), data)
                fields.append(data.astype(BF16))
            pick = jnp.concatenate(picks, axis=1)
            data = jnp.concatenate(fields, axis=1)
            dims = (((1,), (1,)), ((), ()))
            by_slot = lax.dot_general(pick, data, dims, preferred_element_type=F32)
            by_field = lax.dot_general(data, pick, dims, preferred_element_type=F32)
            where_row = by_field[0:1, :] * 4.0 + by_field[1:2, :]
            here = pl.ds(g * LANES, LANES)
            left[:, here] = jnp.where(row_iota == where_row, 1.0, 0.0).astype(BF16)
            same = by_slot[:, 2:3] == depth_iota
            for step in range(2):
                cols = pl.ds(step * nz, nz)
                high = by_slot[:, 3 + 2 * step : 4 + 2 * step]
                low = by_slot[:, 4 + 2 * step : 5 + 2 * step]
                right_hi[here, cols] = jnp.where(same, high, 0.0).astype(BF16)
                right_lo[here, cols] = jnp.where(same, low, 0.0).astype(BF16)
        if first:
            total_1[...] = receiver_sums(left, right_hi, right_lo, 0, nz)

            @pl.when(jnp.logical_not(leave))
            def _():
                total_2[...] = receiver_sums(left, right_hi, right_lo, 1, nz)

        else:
            total_1[...] += receiver_sums(left, right_hi, right_lo, 0, nz)
            total_2[...] += receiver_sums(left, right_hi, right_lo, 1, nz)

    one_pass(0.0, True)

    @pl.when(passes > 1)
    def _():
        def body(number, carry):
            one_pass((number * LANES).astype(F32), False)
            return carry

        lax.fori_loop(1, passes, body, 0)

    for copy in copies:
        copy.wait()
    edge_fill(off[0], send, q_e, k_e, b_e)


def next_row(f, tile):
    rows = f.shape[0]
    return pltpu.roll(jnp.concatenate([f, tile], axis=0), rows + TILE - 1, 0)[:rows]


def last_row(f, tile):
    return pltpu.roll(jnp.concatenate([tile, f], axis=0), 1, 0)[TILE:]


def next_depth(blocks, end):
    moved = [pltpu.roll(f, LANES - 1, 1) for f in blocks]
    return [jnp.where(end, behind, here) for here, behind in zip(moved, moved[1:] + [0.0])]


def last_depth(blocks, start, first):
    moved = [pltpu.roll(g, 1, 1) for g in blocks]
    return [jnp.where(start, ahead, here) for here, ahead in zip(moved, [first] + moved[:-1])]


class Chunks:
    def __init__(self, ny, nz):
        self.starts = list(range(0, ny, CHUNK))
        self.ny = ny
        self.blocks = nz // LANES
        lane = lax.broadcasted_iota(jnp.int32, (CHUNK, LANES), 1)
        row = lax.broadcasted_iota(jnp.int32, (CHUNK, LANES), 0)
        self.end = lane == LANES - 1
        self.start = lane == 0
        self.top = row == 0

    def load(self, ref, lead, y):
        return [ref[(*lead, pl.ds(y, CHUNK), pl.ds(n * LANES, LANES))] for n in range(self.blocks)]

    def store(self, ref, lead, y, values):
        for n, value in enumerate(values):
            ref[(*lead, pl.ds(y, CHUNK), pl.ds(n * LANES, LANES))] = value

    def behind(self, ref, lead, y):
        if y + CHUNK == self.ny:
            return [jnp.zeros((TILE, LANES), F32)] * self.blocks
        return [
            ref[(*lead, pl.ds(y + CHUNK, TILE), pl.ds(n * LANES, LANES))] for n in range(self.blocks)
        ]

    def rows_up(self, ref, lead, y, f):
        return [next_row(a, b) for a, b in zip(f, self.behind(ref, lead, y))]

    def diffs(self, ref, x, xn, y):
        f = self.load(ref, (x,), y)
        dx = [a - b for a, b in zip(self.load(ref, (xn,), y), f)]
        dy = [a - b for a, b in zip(self.rows_up(ref, (x,), y, f), f)]
        dz = [a - b for a, b in zip(next_depth(f, self.end), f)]
        return f, dx, dy, dz

    def lap(self, d, faces, h, gx_ref, slot, y, carry):
        f, dx, dy, dz = d
        gx, gy, gz = ([a * b for a, b in zip(face, diff)] for face, diff in zip(faces, (dx, dy, dz)))
        old = self.load(gx_ref, (slot,), y)
        self.store(gx_ref, (slot,), y, gx)
        if y == 0:
            ahead = [jnp.where(self.top, a * b, pltpu.roll(g, 1, 0)) for a, b, g in zip(h, f, gy)]
        else:
            ahead = [last_row(g, t) for g, t in zip(gy, carry)]
        back = last_depth(gz, self.start, h[0] * f[0])
        out = [
            (a - b) + (c - e) + (m - n) for a, b, c, e, m, n in zip(gx, old, gy, ahead, gz, back)
        ]
        return out, [g[CHUNK - TILE :] for g in gy]


def one_plane(ch, x, xn, p, q, kq, kw, hb, p_old, q_late, total, fy_o, fz_o, lap_o, pn, qm, kqm, gx_s):
    ny = ch.ny
    tail_p = tail_q = None
    for y in ch.starts:
        h = ch.load(hb, (x,), y)
        fx = [a + b for a, b in zip(h, ch.load(hb, (xn,), y))]
        fy = [a + b for a, b in zip(h, ch.rows_up(hb, (x,), y, h))]
        fz = [a + b for a, b in zip(h, next_depth(h, ch.end))]
        ch.store(fy_o, (x,), y, fy)
        ch.store(fz_o, (x,), y, fz)
        faces = (fx, fy, fz)
        k = ch.load(kw, (x,), y)
        d = ch.diffs(p, x, xn, y)
        lap_p, tail_p = ch.lap(d, faces, h, gx_s, 0, y, tail_p)
        ch.store(lap_o, (x,), y, lap_p)
        old = ch.load(p_old, (x,), y)
        ch.store(pn, (x,), y, [2.0 * a - b + c * e for a, b, c, e in zip(d[0], old, k, lap_p)])
        d = ch.diffs(kq, x, xn, y)
        lap_q, tail_q = ch.lap(d, faces, h, gx_s, 1, y, tail_q)
        now = ch.load(q, (x,), y)
        late = ch.load(q_late, (x,), y)
        at = pl.ds(pl.multiple_of(x * ny + y, TILE), CHUNK)
        add = [total[at, pl.ds(n * LANES, LANES)] for n in range(ch.blocks)]
        mid = [2.0 * a - b + c + e for a, b, c, e in zip(now, late, lap_q, add)]
        ch.store(qm, (x,), y, mid)
        ch.store(kqm, (x,), y, [a * b for a, b in zip(k, mid)])


def add_source(step, src, wav, pn, low, high):
    width, ny, nz = pn.shape
    cell = src[0] - lax.axis_index("dom") * (width * ny * nz)
    plane = ny * nz

    @pl.when((cell >= low * plane) & (cell < high * plane))
    def _():
        shift = nz.bit_length() - 1
        row = lax.shift_right_logical(cell, jnp.int32(shift))
        x = lax.div(row, jnp.int32(ny))
        y = row - x * ny
        spot = lax.broadcasted_iota(jnp.int32, (1, nz), 1) == (cell & (nz - 1))
        pn[x, pl.ds(y, 1), :] += jnp.where(spot, wav[step[0]], 0.0)


def step_one_ends(
    off, step, src, later, wav_in, ckpt, adj, k_full, b_full, total, after, left, right_hi, right_lo, total_2_in,
    kq, kw, hb, fy, fz, lap, pn, qm, kqm, total_2,
    gx_s, wav, sem,
):
    width, ny, nz = kq.shape
    copy = pltpu.make_async_copy(wav_in, wav, sem.at[0])
    copy.start()
    p_old, p, q_late, q = ckpt.at[0, 0], ckpt.at[0, 1], adj.at[0, 0], adj.at[0, 1]

    @pl.when(later[0] == 1)
    def _():
        total_2[...] = receiver_sums(left, right_hi, right_lo, 1, nz)

    def windows(x, carry):
        k = window(k_full, (x,), off[0], ny)
        kw[x] = k
        kq[x] = k * q[x]
        hb[x] = 0.5 * window(b_full, (x,), off[0], ny)
        return carry

    lax.fori_loop(0, width, windows, 0)
    ch = Chunks(ny, nz)
    end = width - 1
    rest = (p, q, kq, kw, hb, p_old, q_late, total, fy, fz, lap, pn, qm, kqm, gx_s)

    def ends(n, carry):
        x = n * end
        before = jnp.maximum(x - 1, 0)
        face = hb[before] + hb[x]
        gx_s[0] = face * (p[x] - p[before])
        gx_s[1] = face * (kq[x] - kq[before])
        one_plane(ch, x, jnp.minimum(x + 1, end), *rest)
        return carry

    lax.fori_loop(0, 2, ends, 0)
    copy.wait()
    add_source(step, src, wav, pn, 0, 1)
    add_source(step, src, wav, pn, end, width)


def step_one_middle(
    step, src, wav_in, ckpt, adj, kq, kw, hb, total, fy_i, fz_i, lap_i, pn_i, qm_i, kqm_i,
    fy, fz, lap, pn, qm, kqm,
    gx_s, wav, sem,
):
    width, ny, nz = kq.shape
    copy = pltpu.make_async_copy(wav_in, wav, sem.at[0])
    copy.start()
    p_old, p, q_late, q = ckpt.at[0, 0], ckpt.at[0, 1], adj.at[0, 0], adj.at[0, 1]
    ch = Chunks(ny, nz)
    face = hb[0] + hb[1]
    gx_s[0] = face * (p[1] - p[0])
    gx_s[1] = face * (kq[1] - kq[0])

    def plane(x, carry):
        one_plane(ch, x, x + 1, p, q, kq, kw, hb, p_old, q_late, total, fy, fz, lap, pn, qm, kqm, gx_s)
        return carry

    lax.fori_loop(1, width - 1, plane, 0)
    copy.wait()
    add_source(step, src, wav, pn, 1, width - 1)


def edge_one(which, recv, ckpt, kq, kw, hb, lap_i, pn_i, qm_i, kqm_i, send, lap, pn, qm, kqm):
    edge = edges(kq.shape[0])[which]
    p = ckpt.at[0, 1]
    face = hb[edge] + 0.5 * recv[2]
    flux = face * (recv[0] - p[edge])
    lap[edge] = lap_i[edge] + flux
    k = kw[edge]
    new = pn_i[edge] + k * flux
    send[0] = new
    pn[edge] = new
    mid = qm_i[edge] + face * (recv[1] - kq[edge])
    qm[edge] = mid
    mid = k * mid
    send[1] = mid
    kqm[edge] = mid


def step_two(part, ckpt, adj, kq, hb, fy_i, fz_i, lap_i, pn, qm, kqm, total, *refs):
    last, parts, gx_s = refs[-3:]
    width, ny, nz = kq.shape
    p, q = ckpt.at[0, 1], adj.at[0, 1]
    at_end = edges(width)[1] == width - 1
    if part == 0:
        low = jnp.where(at_end, 0, 2)
        high = low + width - 2
    else:
        low = jnp.where(at_end, width - 2, 0)
        high = low + 2
    before = jnp.maximum(low - 1, 0)
    face = hb[before] + hb[low]
    gx_s[0] = face * (pn[low] - pn[before])
    gx_s[1] = face * (kqm[low] - kqm[before])
    ch = Chunks(ny, nz)

    def plane(x, carry):
        xn = jnp.minimum(x + 1, width - 1)
        tail_p = tail_q = None
        for y in ch.starts:
            h = ch.load(hb, (x,), y)
            fx = [a + b for a, b in zip(h, ch.load(hb, (xn,), y))]
            faces = (fx, ch.load(fy_i, (x,), y), ch.load(fz_i, (x,), y))
            dpn = ch.diffs(pn, x, xn, y)
            lap_p, tail_p = ch.lap(dpn, faces, h, gx_s, 0, y, tail_p)
            mid = ch.load(qm, (x,), y)
            now = ch.load(q, (x,), y)
            lap_1 = ch.load(lap_i, (x,), y)
            ch.store(parts, (0, x), y, [a * b + c * e for a, b, c, e in zip(mid, lap_1, now, lap_p)])
            dqm = ch.diffs(kqm, x, xn, y)
            lap_q, tail_q = ch.lap(dqm, faces, h, gx_s, 1, y, tail_q)
            add = [
                total[pl.ds(pl.multiple_of(x * ny + y, TILE), CHUNK), pl.ds(n * LANES, LANES)]
                for n in range(ch.blocks)
            ]
            ch.store(last, (x,), y, [2.0 * a - b + c + e for a, b, c, e in zip(mid, now, lap_q, add)])
            dp = ch.diffs(p, x, xn, y)
            sums = [
                sum(a * b for a, b in zip(u, v))
                for u, v in zip(zip(*dp[1:]), zip(*dqm[1:]))
            ]
            dq = ch.diffs(kq, x, xn, y)
            sums = [
                s + sum(a * b for a, b in zip(u, v))
                for s, u, v in zip(sums, zip(*dpn[1:]), zip(*dq[1:]))
            ]
            ch.store(parts, (1, x), y, [-s for s in sums])
        return carry

    lax.fori_loop(low, high, plane, 0)


def edge_terms(edge, recv, recv2, send, ckpt, adj, kq, hb):
    p, q = ckpt.at[0, 1], adj.at[0, 1]
    face = hb[edge] + 0.5 * recv[2]
    dpn = recv2[0] - send[0]
    dqm = recv2[1] - send[1]
    add_k = q[edge] * (face * dpn)
    add_b = -(dqm * (recv[0] - p[edge]) + dpn * (recv[1] - kq[edge]))
    return face * dqm, add_k, jnp.where(edge == kq.shape[0] - 1, add_b, 0.0)


def split(plane, off, half):
    whole = placed(plane, off, 2 * half)
    shot = lax.axis_index("shot")
    return (
        jnp.where(shot == 0, whole[:half], whole[half:]),
        jnp.where(shot == 0, whole[half:], whole[:half]),
    )


def first_edge_two(
    off, recv, recv2, send, ckpt, adj, kq, hb, last_i, parts, qm,
    adj_out, last, mine, other, add, sem,
):
    width = kq.shape[0]
    mid_copy = pltpu.make_async_copy(qm, adj_out.at[0, 0], sem.at[1])
    mid_copy.start()
    half = mine.shape[2]
    edge = edges(width)[0]
    add_q, add[0], add[1] = edge_terms(edge, recv, recv2, send, ckpt, adj, kq, hb)
    last[edge] = last_i[edge] + add_q
    copy = pltpu.make_async_copy(last, adj_out.at[0, 1], sem.at[0])
    copy.start()

    def plane(x, carry):
        here = jnp.where(x == edge, 1.0, 0.0)
        for g in range(2):
            mine[g, x], other[g, x] = split(parts[g, x] + here * add[g], off[0], half)
        return carry

    lax.fori_loop(0, width, plane, 0)
    copy.wait()
    mid_copy.wait()


def second_edge_two(off, recv, recv2, send, ckpt, adj, kq, hb, last, mine, other, last_e):
    half = mine.shape[1]
    edge = edges(kq.shape[0])[1]
    add_q, add_k, add_b = edge_terms(edge, recv, recv2, send, ckpt, adj, kq, hb)
    last_e[...] = last[edge] + add_q
    mine[0], other[0] = split(add_k, off[0], half)
    mine[1], other[1] = split(add_b, off[0], half)


def combine(mine, recv, mine_e, grad_k, grad_b, sums_e, sums, sem):
    edge = edges(sums.shape[1])[1]
    copies = []
    for g, grad in enumerate((grad_k, grad_b)):
        sums[g] = mine[g] + recv[g]
        copy = pltpu.make_async_copy(sums.at[g], grad, sem.at[g])
        copy.start()
        copies.append(copy)
    for g in range(2):
        sums_e[g] = sums[g, edge] + mine_e[g]
    for copy in copies:
        copy.wait()


def finish(sums_e, recv_e, last_e, grad_k_in, grad_b_in, adj_in, grad_k, grad_b, adj_out, sums, sem):
    edge = edges(grad_k.shape[0])[1]
    copies = [pltpu.make_async_copy(last_e, adj_out.at[0, 1, edge], sem.at[2])]
    copies[0].start()
    for g, grad in enumerate((grad_k, grad_b)):
        sums[g] = sums_e[g] + recv_e[g]
        copy = pltpu.make_async_copy(sums.at[g], grad.at[edge], sem.at[g])
        copy.start()
        copies.append(copy)
    for copy in copies:
        copy.wait()


def pairs(count, first):
    out = []
    for low in range(first, count - 1, 2):
        out += [(low, low + 1), (low + 1, low)]
    return out


def shards(
    checkpoint, adjoint, kappa, buoyancy, wavelet, src_cell, rec_cell, residuals, offsets, ckpt_step
):
    width, ny, nz = checkpoint.shape[2:]
    model_y = kappa.shape[1]
    half = model_y // 2
    count = lax.axis_size("dom")
    swaps = pairs(count, LEAD), pairs(count, 1 - LEAD)
    rrows = rec_cell.shape[1] // LANES
    slots = rrows // GROUP_ROWS * LANES
    layer = (ny, nz)
    field = (width, ny, nz)
    dma = pltpu.SemaphoreType.DMA
    adj_shape = pltpu.HBM((1, 2, *field), F32)
    grad_shape = pltpu.HBM((width, half, nz), F32)

    inputs = [far(x) for x in (checkpoint, adjoint, kappa, buoyancy)]
    edge_scratch = [vmem(*layer), vmem(model_y, nz), vmem(model_y, nz)]
    send_1 = pl.pallas_call(
        first_send,
        in_specs=[SM] + [ANY] * 4,
        out_specs=VM,
        out_shape=vmem(3, *layer),
        scratch_shapes=edge_scratch + [dma((4,))],
        compiler_params=params(),
    )(offsets, *inputs)
    recv_1 = lax.ppermute(send_1, "dom", swaps[0])

    sums_shape = vmem(width * ny, nz)
    hot_shapes = [pltpu.VMEM(shape, BF16) for shape in ((width * ny, slots), (slots, 2 * nz), (slots, 2 * nz))]
    total_1, total_2, send_2, *hot, later = pl.pallas_call(
        receivers,
        in_specs=[SM, VM, VM] + [ANY] * 4 + [VM],
        out_specs=[VM] * 6 + [SM],
        out_shape=[sums_shape, sums_shape, vmem(3, *layer)] + hot_shapes + [pltpu.SMEM((1,), jnp.int32)],
        scratch_shapes=edge_scratch + [
            pltpu.VMEM((rrows, LANES), jnp.int32),
            vmem(rrows, LANES), vmem(rrows, LANES), vmem(rrows, LANES), vmem(rrows, LANES),
            vmem(4, rrows, LANES),
            dma((4,)),
        ],
        compiler_params=params(),
        cost_estimate=cost(RECV_COST),
    )(offsets, near(rec_cell), near(residuals), *inputs, near(send_1))
    recv_2 = lax.ppermute(send_2, "dom", swaps[1])

    kq, kw, hb, *state, total_2 = pl.pallas_call(
        step_one_ends,
        in_specs=[SM] * 4 + [ANY] + [VM] * 10,
        out_specs=[VM] * 10,
        out_shape=[vmem(*field)] * 9 + [sums_shape],
        scratch_shapes=[vmem(2, *layer), pltpu.SMEM(wavelet.shape, F32), dma((1,))],
        compiler_params=params(),
        input_output_aliases={14: 9},
        cost_estimate=cost(ENDS_COST),
    )(
        offsets, ckpt_step, src_cell, later, far(wavelet),
        *[near(v) for v in (checkpoint, adjoint, kappa, buoyancy, total_1, send_2, *hot, total_2)],
    )

    def first_edge(which, recv, state):
        send, *new = pl.pallas_call(
            functools.partial(edge_one, which),
            in_specs=[VM] * 9,
            out_specs=[VM] * 5,
            out_shape=[vmem(2, *layer)] + [vmem(*field)] * 4,
            input_output_aliases={5: 1, 6: 2, 7: 3, 8: 4},
            compiler_params=params(),
            cost_estimate=cost(EDGE_COST),
        )(*[near(v) for v in (recv, checkpoint, kq, kw, hb, *state[2:])])
        return send, list(state[:2]) + list(new)

    state = pl.pallas_call(
        step_one_middle,
        in_specs=[SM] * 2 + [ANY] + [VM] * 12,
        out_specs=[VM] * 6,
        out_shape=[vmem(*field)] * 6,
        scratch_shapes=[vmem(2, *layer), pltpu.SMEM(wavelet.shape, F32), dma((1,))],
        input_output_aliases={9 + n: n for n in range(6)},
        compiler_params=params(),
        cost_estimate=cost(MIDDLE_COST),
    )(
        ckpt_step, src_cell, far(wavelet),
        *[near(v) for v in (checkpoint, adjoint, kq, kw, hb, total_1, *state)],
    )
    send2_1, state = first_edge(0, recv_1, state)
    recv2_1 = lax.ppermute(send2_1, "dom", swaps[0])

    def second_step(part, state, *partial):
        out_shape = [vmem(*field), vmem(2, *field)]
        return pl.pallas_call(
            functools.partial(step_two, part),
            in_specs=[VM] * (11 + len(partial)),
            out_specs=[VM, VM],
            out_shape=out_shape,
            scratch_shapes=[vmem(2, *layer)],
            input_output_aliases={11 + n: n for n in range(len(partial))},
            compiler_params=params(),
            cost_estimate=cost(TWO_COST[part]),
        )(*[near(v) for v in (checkpoint, adjoint, kq, hb, *state, total_2, *partial)])

    partial = second_step(0, state)
    send2_2, state = first_edge(1, recv_2, state)
    recv2_2 = lax.ppermute(send2_2, "dom", swaps[1])
    last, parts = second_step(1, state, *partial)
    swap = [(0, 1), (1, 0)]
    adj_part, last, mine, other = pl.pallas_call(
        first_edge_two,
        in_specs=[SM] + [VM] * 10,
        out_specs=[ANY, VM, VM, VM],
        out_shape=[adj_shape, vmem(*field), vmem(2, width, half, nz), vmem(2, width, half, nz)],
        scratch_shapes=[vmem(2, *layer), dma((2,))],
        input_output_aliases={8: 1},
        compiler_params=params(),
        cost_estimate=cost(EDGE_B_COST),
    )(
        offsets,
        *[near(v) for v in (recv_1, recv2_1, send2_1, checkpoint, adjoint, kq, hb, last, parts, state[4])],
    )
    recv_g = lax.ppermute(other, "shot", swap)
    mine_e, other_e, last_e = pl.pallas_call(
        second_edge_two,
        in_specs=[SM] + [VM] * 8,
        out_specs=[VM, VM, VM],
        out_shape=[vmem(2, half, nz), vmem(2, half, nz), vmem(*layer)],
        compiler_params=params(),
        cost_estimate=cost(40),
    )(offsets, *[near(v) for v in (recv_2, recv2_2, send2_2, checkpoint, adjoint, kq, hb, last)])
    recv_e = lax.ppermute(other_e, "shot", swap)
    grad_k, grad_b, sums_e = pl.pallas_call(
        combine,
        in_specs=[VM] * 3,
        out_specs=[ANY, ANY, VM],
        out_shape=[grad_shape, grad_shape, vmem(2, half, nz)],
        scratch_shapes=[vmem(2, width, half, nz), dma((2,))],
        compiler_params=params(),
        cost_estimate=cost(40),
    )(near(mine), near(recv_g), near(mine_e))
    return pl.pallas_call(
        finish,
        in_specs=[VM] * 3 + [ANY] * 3,
        out_specs=[ANY] * 3,
        out_shape=[grad_shape, grad_shape, adj_shape],
        scratch_shapes=[vmem(2, half, nz), dma((3,))],
        input_output_aliases={3: 0, 4: 1, 5: 2},
        compiler_params=params(),
    )(near(sums_e), near(recv_e), near(last_e), far(grad_k), far(grad_b), far(adj_part))


def solution(mesh):
    in_specs = (
        P(("group", "shot"), None, "dom", None, None),
        P(("group", "shot"), None, "dom", None, None),
        P(("group", "dom"), None, None),
        P(("group", "dom"), None, None),
        P(),
        P(("group", "shot")),
        P(("group", "shot"), None),
        P(("group", "shot"), None, None),
        P(("group", "shot")),
        P(("group", "shot")),
    )
    out_specs = (
        P(("group", "dom"), "shot", None),
        P(("group", "dom"), "shot", None),
        P(("group", "shot"), None, "dom", None, None),
    )
    return jax.shard_map(shards, mesh=mesh, in_specs=in_specs, out_specs=out_specs, check_vma=False)
```

```python
import functools

import jax
import jax.numpy as jnp
from jax import lax
from jax.experimental import pallas as pl
from jax.experimental.pallas import tpu as pltpu
from jax.sharding import PartitionSpec as P

F32 = jnp.float32
BF16 = jnp.bfloat16
LANES = 128
TILE = 8
GROUP_ROWS = 5
CHUNK = 16
LEAD = 0
RECV_COST = 40
ENDS_COST = 40
MIDDLE_COST = 40
EDGE_COST = 1
TWO_COST = (40, 2)
EDGE_B_COST = 2

VM = pl.BlockSpec(memory_space=pltpu.VMEM)
SM = pl.BlockSpec(memory_space=pltpu.SMEM)
ANY = pl.BlockSpec(memory_space=pl.ANY)


def vmem(*shape):
    return pltpu.VMEM(shape, F32)


def near(x):
    return pltpu.with_memory_space_constraint(x, pltpu.VMEM)


def far(x):
    return pltpu.with_memory_space_constraint(x, pltpu.HBM)


def cost(us):
    return pl.CostEstimate(flops=int(us * 1_000_000_000), bytes_accessed=1024, transcendentals=0)


def params():
    return pltpu.CompilerParams(vmem_limit_bytes=24 * 1024 * 1024)


def edges(width):
    even = lax.rem(lax.axis_index("dom"), 2) == 0
    last = jnp.int32(width - 1)
    first = jnp.int32(0)
    ends = jnp.where(even, last, first), jnp.where(even, first, last)
    return ends[LEAD], ends[1 - LEAD]


def window(ref, lead, off, ny):
    rows, nz = ref.shape[-2:]
    base = jnp.minimum(off - lax.rem(off, TILE), rows - ny - TILE)
    skip = off - base
    block = ref[(*lead, pl.ds(pl.multiple_of(base, TILE), ny + TILE), slice(None))]
    tiles = block.reshape(ny // TILE + 1, TILE, nz)
    tiles = pltpu.roll(tiles, lax.rem(TILE - skip, TILE), 1)
    row = lax.broadcasted_iota(jnp.int32, (ny // TILE, TILE, nz), 1)
    return jnp.where(row < TILE - skip, tiles[:-1], tiles[1:]).reshape(ny, nz)


def placed(plane, off, rows):
    fill = jnp.zeros((rows - plane.shape[0], plane.shape[1]), plane.dtype)
    return pltpu.roll(jnp.concatenate([plane, fill], axis=0), off, 0)


def edge_copies(edge, ckpt, adj, kappa, buoy, send, q_e, k_e, b_e, sem):
    return [
        pltpu.make_async_copy(adj.at[0, 1, edge], q_e, sem.at[1]),
        pltpu.make_async_copy(kappa.at[edge], k_e, sem.at[2]),
        pltpu.make_async_copy(buoy.at[edge], b_e, sem.at[3]),
        pltpu.make_async_copy(ckpt.at[0, 1, edge], send.at[0], sem.at[0]),
    ]


def edge_fill(off, send, q_e, k_e, b_e):
    ny = q_e.shape[0]
    send[1] = window(k_e, (), off, ny) * q_e[...]
    send[2] = window(b_e, (), off, ny)


def first_send(off, ckpt, adj, kappa, buoy, send, q_e, k_e, b_e, sem):
    edge = edges(ckpt.shape[2])[0]
    copies = edge_copies(edge, ckpt, adj, kappa, buoy, send, q_e, k_e, b_e, sem)
    for copy in copies:
        copy.start()
    for copy in copies:
        copy.wait()
    edge_fill(off[0], send, q_e, k_e, b_e)


def receiver_sums(left, right_hi, right_lo, step, nz):
    cols = pl.ds(step * nz, nz)
    return jnp.dot(left[...], right_hi[:, cols], preferred_element_type=F32) + jnp.dot(
        left[...], right_lo[:, cols], preferred_element_type=F32
    )


def receivers(
    off, rec, res, ckpt, adj, kappa, buoy, after, total_1, total_2, send, left, right_hi, right_lo, later,
    q_e, k_e, b_e, cell_s, rank_s, row_a_s, row_b_s, z_s, val_s, sem,
):
    nz = total_1.shape[1]
    edge = edges(ckpt.shape[2])[1]
    copies = edge_copies(edge, ckpt, adj, kappa, buoy, send, q_e, k_e, b_e, sem)
    for copy in copies:
        copy.start()
    rows, lanes = cell_s.shape
    for r in range(rows):
        at = pl.ds(r * lanes, lanes)
        cell_s[r : r + 1, :] = rec[:, at]
        for step in range(2):
            val_s[2 * step, r : r + 1, :] = res[0, step : step + 1, at]
    cells = total_1.shape[0] * nz
    shift = nz.bit_length() - 1
    local = cell_s[...] - lax.axis_index("dom") * cells
    inside = (local >= 0) & (local < cells)
    row = lax.shift_right_logical(local, jnp.int32(shift))
    row_a_s[...] = lax.shift_right_logical(row, jnp.int32(2)).astype(F32)
    row_b_s[...] = (row & 3).astype(F32)
    z_s[...] = (local & (nz - 1)).astype(F32)
    for step in range(2):
        value = val_s[2 * step]
        high = value.astype(BF16).astype(F32)
        val_s[2 * step] = high
        val_s[2 * step + 1] = value - high
    mask = jnp.where(inside, 1.0, 0.0).astype(BF16)
    before = lax.broadcasted_iota(jnp.int32, (lanes, lanes), 0) < lax.broadcasted_iota(
        jnp.int32, (lanes, lanes), 1
    )
    in_row = jnp.dot(mask, jnp.where(before, 1.0, 0.0).astype(BF16), preferred_element_type=F32)
    row_sum = jnp.dot(mask, jnp.ones((lanes, lanes), BF16), preferred_element_type=F32)
    r = lax.broadcasted_iota(jnp.int32, (rows, rows), 0)
    c = lax.broadcasted_iota(jnp.int32, (rows, rows), 1)
    group_r = lax.shift_right_logical(r * 3277, jnp.int32(14))
    group_c = lax.shift_right_logical(c * 3277, jnp.int32(14))
    earlier = jnp.where((group_r == group_c) & (c < r), 1.0, 0.0).astype(BF16)
    row_start = jnp.dot(earlier, row_sum.astype(BF16), preferred_element_type=F32)
    rank = jnp.where(inside, in_row + row_start, -1.0)
    rank_s[...] = rank
    passes = lax.shift_right_logical(jnp.max(rank).astype(jnp.int32), jnp.int32(7)) + 1
    leave = (lax.rem(lax.axis_index("dom"), 2) == 0) & (passes <= 1)
    later[0] = jnp.where(leave, 1, 0)
    groups = rows // GROUP_ROWS
    slot = lax.broadcasted_iota(jnp.int32, (LANES, lanes), 0).astype(F32)
    sub8 = lax.broadcasted_iota(jnp.int32, (TILE, lanes), 0)
    row_iota = lax.broadcasted_iota(jnp.int32, (left.shape[0], LANES), 0).astype(F32)
    depth_iota = lax.broadcasted_iota(jnp.int32, (LANES, nz), 1).astype(F32)

    def one_pass(base, first):
        for g in range(groups):
            picks = []
            fields = []
            for n in range(GROUP_ROWS):
                at = pl.ds(g * GROUP_ROWS + n, 1)
                want = jnp.broadcast_to(rank_s[at, :] - base, (LANES, lanes))
                picks.append(jnp.where(want == slot, 1.0, 0.0).astype(BF16))
                data = jnp.zeros((TILE, lanes), F32)
                sources = [row_a_s, row_b_s, z_s] + [val_s.at[m] for m in range(4)]
                for m, source in enumerate(sources):
                    data = jnp.where(sub8 == m, jnp.broadcast_to(source[at, :], (TILE, lanes)), data)
                fields.append(data.astype(BF16))
            pick = jnp.concatenate(picks, axis=1)
            data = jnp.concatenate(fields, axis=1)
            dims = (((1,), (1,)), ((), ()))
            by_slot = lax.dot_general(pick, data, dims, preferred_element_type=F32)
            by_field = lax.dot_general(data, pick, dims, preferred_element_type=F32)
            where_row = by_field[0:1, :] * 4.0 + by_field[1:2, :]
            here = pl.ds(g * LANES, LANES)
            left[:, here] = jnp.where(row_iota == where_row, 1.0, 0.0).astype(BF16)
            same = by_slot[:, 2:3] == depth_iota
            for step in range(2):
                cols = pl.ds(step * nz, nz)
                high = by_slot[:, 3 + 2 * step : 4 + 2 * step]
                low = by_slot[:, 4 + 2 * step : 5 + 2 * step]
                right_hi[here, cols] = jnp.where(same, high, 0.0).astype(BF16)
                right_lo[here, cols] = jnp.where(same, low, 0.0).astype(BF16)
        if first:
            total_1[...] = receiver_sums(left, right_hi, right_lo, 0, nz)

            @pl.when(jnp.logical_not(leave))
            def _():
                total_2[...] = receiver_sums(left, right_hi, right_lo, 1, nz)

        else:
            total_1[...] += receiver_sums(left, right_hi, right_lo, 0, nz)
            total_2[...] += receiver_sums(left, right_hi, right_lo, 1, nz)

    one_pass(0.0, True)

    @pl.when(passes > 1)
    def _():
        def body(number, carry):
            one_pass((number * LANES).astype(F32), False)
            return carry

        lax.fori_loop(1, passes, body, 0)

    for copy in copies:
        copy.wait()
    edge_fill(off[0], send, q_e, k_e, b_e)


def next_row(f, tile):
    rows = f.shape[0]
    return pltpu.roll(jnp.concatenate([f, tile], axis=0), rows + TILE - 1, 0)[:rows]


def last_row(f, tile):
    return pltpu.roll(jnp.concatenate([tile, f], axis=0), 1, 0)[TILE:]


def next_depth(blocks, end):
    moved = [pltpu.roll(f, LANES - 1, 1) for f in blocks]
    return [jnp.where(end, behind, here) for here, behind in zip(moved, moved[1:] + [0.0])]


def last_depth(blocks, start, first):
    moved = [pltpu.roll(g, 1, 1) for g in blocks]
    return [jnp.where(start, ahead, here) for here, ahead in zip(moved, [first] + moved[:-1])]


class Chunks:
    def __init__(self, ny, nz):
        self.starts = list(range(0, ny, CHUNK))
        self.ny = ny
        self.blocks = nz // LANES
        lane = lax.broadcasted_iota(jnp.int32, (CHUNK, LANES), 1)
        row = lax.broadcasted_iota(jnp.int32, (CHUNK, LANES), 0)
        self.end = lane == LANES - 1
        self.start = lane == 0
        self.top = row == 0

    def load(self, ref, lead, y):
        return [ref[(*lead, pl.ds(y, CHUNK), pl.ds(n * LANES, LANES))] for n in range(self.blocks)]

    def store(self, ref, lead, y, values):
        for n, value in enumerate(values):
            ref[(*lead, pl.ds(y, CHUNK), pl.ds(n * LANES, LANES))] = value

    def behind(self, ref, lead, y):
        if y + CHUNK == self.ny:
            return [jnp.zeros((TILE, LANES), F32)] * self.blocks
        return [
            ref[(*lead, pl.ds(y + CHUNK, TILE), pl.ds(n * LANES, LANES))] for n in range(self.blocks)
        ]

    def rows_up(self, ref, lead, y, f):
        return [next_row(a, b) for a, b in zip(f, self.behind(ref, lead, y))]

    def diffs(self, ref, x, xn, y):
        f = self.load(ref, (x,), y)
        dx = [a - b for a, b in zip(self.load(ref, (xn,), y), f)]
        dy = [a - b for a, b in zip(self.rows_up(ref, (x,), y, f), f)]
        dz = [a - b for a, b in zip(next_depth(f, self.end), f)]
        return f, dx, dy, dz

    def lap(self, d, faces, h, gx_ref, slot, y, carry):
        f, dx, dy, dz = d
        gx, gy, gz = ([a * b for a, b in zip(face, diff)] for face, diff in zip(faces, (dx, dy, dz)))
        old = self.load(gx_ref, (slot,), y)
        self.store(gx_ref, (slot,), y, gx)
        if y == 0:
            ahead = [jnp.where(self.top, a * b, pltpu.roll(g, 1, 0)) for a, b, g in zip(h, f, gy)]
        else:
            ahead = [last_row(g, t) for g, t in zip(gy, carry)]
        back = last_depth(gz, self.start, h[0] * f[0])
        out = [
            (a - b) + (c - e) + (m - n) for a, b, c, e, m, n in zip(gx, old, gy, ahead, gz, back)
        ]
        return out, [g[CHUNK - TILE :] for g in gy]


def one_plane(ch, x, xn, p, q, kq, kw, hb, p_old, q_late, total, fy_o, fz_o, lap_o, pn, qm, kqm, gx_s):
    ny = ch.ny
    tail_p = tail_q = None
    for y in ch.starts:
        h = ch.load(hb, (x,), y)
        fx = [a + b for a, b in zip(h, ch.load(hb, (xn,), y))]
        fy = [a + b for a, b in zip(h, ch.rows_up(hb, (x,), y, h))]
        fz = [a + b for a, b in zip(h, next_depth(h, ch.end))]
        ch.store(fy_o, (x,), y, fy)
        ch.store(fz_o, (x,), y, fz)
        faces = (fx, fy, fz)
        k = ch.load(kw, (x,), y)
        d = ch.diffs(p, x, xn, y)
        lap_p, tail_p = ch.lap(d, faces, h, gx_s, 0, y, tail_p)
        ch.store(lap_o, (x,), y, lap_p)
        old = ch.load(p_old, (x,), y)
        ch.store(pn, (x,), y, [2.0 * a - b + c * e for a, b, c, e in zip(d[0], old, k, lap_p)])
        d = ch.diffs(kq, x, xn, y)
        lap_q, tail_q = ch.lap(d, faces, h, gx_s, 1, y, tail_q)
        now = ch.load(q, (x,), y)
        late = ch.load(q_late, (x,), y)
        at = pl.ds(pl.multiple_of(x * ny + y, TILE), CHUNK)
        add = [total[at, pl.ds(n * LANES, LANES)] for n in range(ch.blocks)]
        mid = [2.0 * a - b + c + e for a, b, c, e in zip(now, late, lap_q, add)]
        ch.store(qm, (x,), y, mid)
        ch.store(kqm, (x,), y, [a * b for a, b in zip(k, mid)])


def add_source(step, src, wav, pn, low, high):
    width, ny, nz = pn.shape
    cell = src[0] - lax.axis_index("dom") * (width * ny * nz)
    plane = ny * nz

    @pl.when((cell >= low * plane) & (cell < high * plane))
    def _():
        shift = nz.bit_length() - 1
        row = lax.shift_right_logical(cell, jnp.int32(shift))
        x = lax.div(row, jnp.int32(ny))
        y = row - x * ny
        spot = lax.broadcasted_iota(jnp.int32, (1, nz), 1) == (cell & (nz - 1))
        pn[x, pl.ds(y, 1), :] += jnp.where(spot, wav[step[0]], 0.0)


def step_one_ends(
    off, step, src, later, wav_in, ckpt, adj, k_full, b_full, total, after, left, right_hi, right_lo, total_2_in,
    kq, kw, hb, fy, fz, lap, pn, qm, kqm, total_2,
    gx_s, wav, sem,
):
    width, ny, nz = kq.shape
    copy = pltpu.make_async_copy(wav_in, wav, sem.at[0])
    copy.start()
    p_old, p, q_late, q = ckpt.at[0, 0], ckpt.at[0, 1], adj.at[0, 0], adj.at[0, 1]

    @pl.when(later[0] == 1)
    def _():
        total_2[...] = receiver_sums(left, right_hi, right_lo, 1, nz)

    def windows(x, carry):
        k = window(k_full, (x,), off[0], ny)
        kw[x] = k
        kq[x] = k * q[x]
        hb[x] = 0.5 * window(b_full, (x,), off[0], ny)
        return carry

    lax.fori_loop(0, width, windows, 0)
    ch = Chunks(ny, nz)
    end = width - 1
    rest = (p, q, kq, kw, hb, p_old, q_late, total, fy, fz, lap, pn, qm, kqm, gx_s)

    def ends(n, carry):
        x = n * end
        before = jnp.maximum(x - 1, 0)
        face = hb[before] + hb[x]
        gx_s[0] = face * (p[x] - p[before])
        gx_s[1] = face * (kq[x] - kq[before])
        one_plane(ch, x, jnp.minimum(x + 1, end), *rest)
        return carry

    lax.fori_loop(0, 2, ends, 0)
    copy.wait()
    add_source(step, src, wav, pn, 0, 1)
    add_source(step, src, wav, pn, end, width)


def step_one_middle(
    step, src, wav_in, ckpt, adj, kq, kw, hb, total, fy_i, fz_i, lap_i, pn_i, qm_i, kqm_i,
    fy, fz, lap, pn, qm, kqm,
    gx_s, wav, sem,
):
    width, ny, nz = kq.shape
    copy = pltpu.make_async_copy(wav_in, wav, sem.at[0])
    copy.start()
    p_old, p, q_late, q = ckpt.at[0, 0], ckpt.at[0, 1], adj.at[0, 0], adj.at[0, 1]
    ch = Chunks(ny, nz)
    face = hb[0] + hb[1]
    gx_s[0] = face * (p[1] - p[0])
    gx_s[1] = face * (kq[1] - kq[0])

    def plane(x, carry):
        one_plane(ch, x, x + 1, p, q, kq, kw, hb, p_old, q_late, total, fy, fz, lap, pn, qm, kqm, gx_s)
        return carry

    lax.fori_loop(1, width - 1, plane, 0)
    copy.wait()
    add_source(step, src, wav, pn, 1, width - 1)


def edge_one(which, recv, ckpt, kq, kw, hb, lap_i, pn_i, qm_i, kqm_i, send, lap, pn, qm, kqm):
    edge = edges(kq.shape[0])[which]
    p = ckpt.at[0, 1]
    face = hb[edge] + 0.5 * recv[2]
    flux = face * (recv[0] - p[edge])
    lap[edge] = lap_i[edge] + flux
    k = kw[edge]
    new = pn_i[edge] + k * flux
    send[0] = new
    pn[edge] = new
    mid = qm_i[edge] + face * (recv[1] - kq[edge])
    qm[edge] = mid
    mid = k * mid
    send[1] = mid
    kqm[edge] = mid


def step_two(part, ckpt, adj, kq, hb, fy_i, fz_i, lap_i, pn, qm, kqm, total, *refs):
    last, parts, gx_s = refs[-3:]
    width, ny, nz = kq.shape
    p, q = ckpt.at[0, 1], adj.at[0, 1]
    at_end = edges(width)[1] == width - 1
    if part == 0:
        low = jnp.where(at_end, 0, 2)
        high = low + width - 2
    else:
        low = jnp.where(at_end, width - 2, 0)
        high = low + 2
    before = jnp.maximum(low - 1, 0)
    face = hb[before] + hb[low]
    gx_s[0] = face * (pn[low] - pn[before])
    gx_s[1] = face * (kqm[low] - kqm[before])
    ch = Chunks(ny, nz)

    def plane(x, carry):
        xn = jnp.minimum(x + 1, width - 1)
        tail_p = tail_q = None
        for y in ch.starts:
            h = ch.load(hb, (x,), y)
            fx = [a + b for a, b in zip(h, ch.load(hb, (xn,), y))]
            faces = (fx, ch.load(fy_i, (x,), y), ch.load(fz_i, (x,), y))
            dpn = ch.diffs(pn, x, xn, y)
            lap_p, tail_p = ch.lap(dpn, faces, h, gx_s, 0, y, tail_p)
            mid = ch.load(qm, (x,), y)
            now = ch.load(q, (x,), y)
            lap_1 = ch.load(lap_i, (x,), y)
            ch.store(parts, (0, x), y, [a * b + c * e for a, b, c, e in zip(mid, lap_1, now, lap_p)])
            dqm = ch.diffs(kqm, x, xn, y)
            lap_q, tail_q = ch.lap(dqm, faces, h, gx_s, 1, y, tail_q)
            add = [
                total[pl.ds(pl.multiple_of(x * ny + y, TILE), CHUNK), pl.ds(n * LANES, LANES)]
                for n in range(ch.blocks)
            ]
            ch.store(last, (x,), y, [2.0 * a - b + c + e for a, b, c, e in zip(mid, now, lap_q, add)])
            dp = ch.diffs(p, x, xn, y)
            sums = [
                sum(a * b for a, b in zip(u, v))
                for u, v in zip(zip(*dp[1:]), zip(*dqm[1:]))
            ]
            dq = ch.diffs(kq, x, xn, y)
            sums = [
                s + sum(a * b for a, b in zip(u, v))
                for s, u, v in zip(sums, zip(*dpn[1:]), zip(*dq[1:]))
            ]
            ch.store(parts, (1, x), y, [-s for s in sums])
        return carry

    lax.fori_loop(low, high, plane, 0)


def edge_terms(edge, recv, recv2, send, ckpt, adj, kq, hb):
    p, q = ckpt.at[0, 1], adj.at[0, 1]
    face = hb[edge] + 0.5 * recv[2]
    dpn = recv2[0] - send[0]
    dqm = recv2[1] - send[1]
    add_k = q[edge] * (face * dpn)
    add_b = -(dqm * (recv[0] - p[edge]) + dpn * (recv[1] - kq[edge]))
    return face * dqm, add_k, jnp.where(edge == kq.shape[0] - 1, add_b, 0.0)


def split(plane, off, half):
    whole = placed(plane, off, 2 * half)
    shot = lax.axis_index("shot")
    return (
        jnp.where(shot == 0, whole[:half], whole[half:]),
        jnp.where(shot == 0, whole[half:], whole[:half]),
    )


def first_edge_two(
    off, recv, recv2, send, ckpt, adj, kq, hb, last_i, parts, qm,
    adj_out, last, mine, other, add, sem,
):
    width = kq.shape[0]
    mid_copy = pltpu.make_async_copy(qm, adj_out.at[0, 0], sem.at[1])
    mid_copy.start()
    half = mine.shape[2]
    edge = edges(width)[0]
    add_q, add[0], add[1] = edge_terms(edge, recv, recv2, send, ckpt, adj, kq, hb)
    last[edge] = last_i[edge] + add_q
    copy = pltpu.make_async_copy(last, adj_out.at[0, 1], sem.at[0])
    copy.start()

    def plane(x, carry):
        here = jnp.where(x == edge, 1.0, 0.0)
        for g in range(2):
            mine[g, x], other[g, x] = split(parts[g, x] + here * add[g], off[0], half)
        return carry

    lax.fori_loop(0, width, plane, 0)
    copy.wait()
    mid_copy.wait()


def second_edge_two(off, recv, recv2, send, ckpt, adj, kq, hb, last, mine, other, last_e):
    half = mine.shape[1]
    edge = edges(kq.shape[0])[1]
    add_q, add_k, add_b = edge_terms(edge, recv, recv2, send, ckpt, adj, kq, hb)
    last_e[...] = last[edge] + add_q
    mine[0], other[0] = split(add_k, off[0], half)
    mine[1], other[1] = split(add_b, off[0], half)


def combine(mine, recv, mine_e, last_e, adj_in, grad_k, grad_b, sums_e, adj_out, sums, sem):
    edge = edges(sums.shape[1])[1]
    copies = [pltpu.make_async_copy(last_e, adj_out.at[0, 1, edge], sem.at[2])]
    copies[0].start()
    for g, grad in enumerate((grad_k, grad_b)):
        sums[g] = mine[g] + recv[g]
        copy = pltpu.make_async_copy(sums.at[g], grad, sem.at[g])
        copy.start()
        copies.append(copy)
    for g in range(2):
        sums_e[g] = sums[g, edge] + mine_e[g]
    for copy in copies:
        copy.wait()


def finish(sums_e, recv_e, grad_k_in, grad_b_in, grad_k, grad_b, sums, sem):
    edge = edges(grad_k.shape[0])[1]
    copies = []
    for g, grad in enumerate((grad_k, grad_b)):
        sums[g] = sums_e[g] + recv_e[g]
        copy = pltpu.make_async_copy(sums.at[g], grad.at[edge], sem.at[g])
        copy.start()
        copies.append(copy)
    for copy in copies:
        copy.wait()


def pairs(count, first):
    out = []
    for low in range(first, count - 1, 2):
        out += [(low, low + 1), (low + 1, low)]
    return out


def shards(
    checkpoint, adjoint, kappa, buoyancy, wavelet, src_cell, rec_cell, residuals, offsets, ckpt_step
):
    width, ny, nz = checkpoint.shape[2:]
    model_y = kappa.shape[1]
    half = model_y // 2
    count = lax.axis_size("dom")
    swaps = pairs(count, LEAD), pairs(count, 1 - LEAD)
    rrows = rec_cell.shape[1] // LANES
    slots = rrows // GROUP_ROWS * LANES
    layer = (ny, nz)
    field = (width, ny, nz)
    dma = pltpu.SemaphoreType.DMA
    adj_shape = pltpu.HBM((1, 2, *field), F32)
    grad_shape = pltpu.HBM((width, half, nz), F32)

    inputs = [far(x) for x in (checkpoint, adjoint, kappa, buoyancy)]
    edge_scratch = [vmem(*layer), vmem(model_y, nz), vmem(model_y, nz)]
    send_1 = pl.pallas_call(
        first_send,
        in_specs=[SM] + [ANY] * 4,
        out_specs=VM,
        out_shape=vmem(3, *layer),
        scratch_shapes=edge_scratch + [dma((4,))],
        compiler_params=params(),
    )(offsets, *inputs)
    recv_1 = lax.ppermute(send_1, "dom", swaps[0])

    sums_shape = vmem(width * ny, nz)
    hot_shapes = [pltpu.VMEM(shape, BF16) for shape in ((width * ny, slots), (slots, 2 * nz), (slots, 2 * nz))]
    total_1, total_2, send_2, *hot, later = pl.pallas_call(
        receivers,
        in_specs=[SM, VM, VM] + [ANY] * 4 + [VM],
        out_specs=[VM] * 6 + [SM],
        out_shape=[sums_shape, sums_shape, vmem(3, *layer)] + hot_shapes + [pltpu.SMEM((1,), jnp.int32)],
        scratch_shapes=edge_scratch + [
            pltpu.VMEM((rrows, LANES), jnp.int32),
            vmem(rrows, LANES), vmem(rrows, LANES), vmem(rrows, LANES), vmem(rrows, LANES),
            vmem(4, rrows, LANES),
            dma((4,)),
        ],
        compiler_params=params(),
        cost_estimate=cost(RECV_COST),
    )(offsets, near(rec_cell), near(residuals), *inputs, near(send_1))
    recv_2 = lax.ppermute(send_2, "dom", swaps[1])

    kq, kw, hb, *state, total_2 = pl.pallas_call(
        step_one_ends,
        in_specs=[SM] * 4 + [ANY] + [VM] * 10,
        out_specs=[VM] * 10,
        out_shape=[vmem(*field)] * 9 + [sums_shape],
        scratch_shapes=[vmem(2, *layer), pltpu.SMEM(wavelet.shape, F32), dma((1,))],
        compiler_params=params(),
        input_output_aliases={14: 9},
        cost_estimate=cost(ENDS_COST),
    )(
        offsets, ckpt_step, src_cell, later, far(wavelet),
        *[near(v) for v in (checkpoint, adjoint, kappa, buoyancy, total_1, send_2, *hot, total_2)],
    )

    def first_edge(which, recv, state):
        send, *new = pl.pallas_call(
            functools.partial(edge_one, which),
            in_specs=[VM] * 9,
            out_specs=[VM] * 5,
            out_shape=[vmem(2, *layer)] + [vmem(*field)] * 4,
            input_output_aliases={5: 1, 6: 2, 7: 3, 8: 4},
            compiler_params=params(),
            cost_estimate=cost(EDGE_COST),
        )(*[near(v) for v in (recv, checkpoint, kq, kw, hb, *state[2:])])
        return send, list(state[:2]) + list(new)

    state = pl.pallas_call(
        step_one_middle,
        in_specs=[SM] * 2 + [ANY] + [VM] * 12,
        out_specs=[VM] * 6,
        out_shape=[vmem(*field)] * 6,
        scratch_shapes=[vmem(2, *layer), pltpu.SMEM(wavelet.shape, F32), dma((1,))],
        input_output_aliases={9 + n: n for n in range(6)},
        compiler_params=params(),
        cost_estimate=cost(MIDDLE_COST),
    )(
        ckpt_step, src_cell, far(wavelet),
        *[near(v) for v in (checkpoint, adjoint, kq, kw, hb, total_1, *state)],
    )
    send2_1, state = first_edge(0, recv_1, state)
    recv2_1 = lax.ppermute(send2_1, "dom", swaps[0])

    def second_step(part, state, *partial):
        out_shape = [vmem(*field), vmem(2, *field)]
        return pl.pallas_call(
            functools.partial(step_two, part),
            in_specs=[VM] * (11 + len(partial)),
            out_specs=[VM, VM],
            out_shape=out_shape,
            scratch_shapes=[vmem(2, *layer)],
            input_output_aliases={11 + n: n for n in range(len(partial))},
            compiler_params=params(),
            cost_estimate=cost(TWO_COST[part]),
        )(*[near(v) for v in (checkpoint, adjoint, kq, hb, *state, total_2, *partial)])

    partial = second_step(0, state)
    send2_2, state = first_edge(1, recv_2, state)
    recv2_2 = lax.ppermute(send2_2, "dom", swaps[1])
    last, parts = second_step(1, state, *partial)
    swap = [(0, 1), (1, 0)]
    adj_part, last, mine, other = pl.pallas_call(
        first_edge_two,
        in_specs=[SM] + [VM] * 10,
        out_specs=[ANY, VM, VM, VM],
        out_shape=[adj_shape, vmem(*field), vmem(2, width, half, nz), vmem(2, width, half, nz)],
        scratch_shapes=[vmem(2, *layer), dma((2,))],
        input_output_aliases={8: 1},
        compiler_params=params(),
        cost_estimate=cost(EDGE_B_COST),
    )(
        offsets,
        *[near(v) for v in (recv_1, recv2_1, send2_1, checkpoint, adjoint, kq, hb, last, parts, state[4])],
    )
    recv_g = lax.ppermute(other, "shot", swap)
    mine_e, other_e, last_e = pl.pallas_call(
        second_edge_two,
        in_specs=[SM] + [VM] * 8,
        out_specs=[VM, VM, VM],
        out_shape=[vmem(2, half, nz), vmem(2, half, nz), vmem(*layer)],
        compiler_params=params(),
        cost_estimate=cost(40),
    )(offsets, *[near(v) for v in (recv_2, recv2_2, send2_2, checkpoint, adjoint, kq, hb, last)])
    recv_e = lax.ppermute(other_e, "shot", swap)
    grad_k, grad_b, sums_e, adj_next = pl.pallas_call(
        combine,
        in_specs=[VM] * 4 + [ANY],
        out_specs=[ANY, ANY, VM, ANY],
        out_shape=[grad_shape, grad_shape, vmem(2, half, nz), adj_shape],
        scratch_shapes=[vmem(2, width, half, nz), dma((3,))],
        input_output_aliases={4: 3},
        compiler_params=params(),
        cost_estimate=cost(40),
    )(near(mine), near(recv_g), near(mine_e), near(last_e), far(adj_part))
    grad_k, grad_b = pl.pallas_call(
        finish,
        in_specs=[VM] * 2 + [ANY] * 2,
        out_specs=[ANY] * 2,
        out_shape=[grad_shape, grad_shape],
        scratch_shapes=[vmem(2, half, nz), dma((2,))],
        input_output_aliases={2: 0, 3: 1},
        compiler_params=params(),
    )(near(sums_e), near(recv_e), far(grad_k), far(grad_b))
    return grad_k, grad_b, adj_next


def solution(mesh):
    in_specs = (
        P(("group", "shot"), None, "dom", None, None),
        P(("group", "shot"), None, "dom", None, None),
        P(("group", "dom"), None, None),
        P(("group", "dom"), None, None),
        P(),
        P(("group", "shot")),
        P(("group", "shot"), None),
        P(("group", "shot"), None, None),
        P(("group", "shot")),
        P(("group", "shot")),
    )
    out_specs = (
        P(("group", "dom"), "shot", None),
        P(("group", "dom"), "shot", None),
        P(("group", "shot"), None, "dom", None, None),
    )
    return jax.shard_map(shards, mesh=mesh, in_specs=in_specs, out_specs=out_specs, check_vma=False)
```

```python
import functools

import jax
import jax.numpy as jnp
from jax import lax
from jax.experimental import pallas as pl
from jax.experimental.pallas import tpu as pltpu
from jax.sharding import PartitionSpec as P

F32 = jnp.float32
BF16 = jnp.bfloat16
LANES = 128
TILE = 8
GROUP_ROWS = 5
CHUNK = 16
LEAD = 0
RECV_COST = 40
ENDS_COST = 40
MIDDLE_COST = 40
EDGE_COST = 1
TWO_COST = (40, 2)
EDGE_B_COST = 2

VM = pl.BlockSpec(memory_space=pltpu.VMEM)
SM = pl.BlockSpec(memory_space=pltpu.SMEM)
ANY = pl.BlockSpec(memory_space=pl.ANY)


def vmem(*shape):
    return pltpu.VMEM(shape, F32)


def near(x):
    return pltpu.with_memory_space_constraint(x, pltpu.VMEM)


def far(x):
    return pltpu.with_memory_space_constraint(x, pltpu.HBM)


def cost(us):
    return pl.CostEstimate(flops=int(us * 1_000_000_000), bytes_accessed=1024, transcendentals=0)


def params():
    return pltpu.CompilerParams(vmem_limit_bytes=24 * 1024 * 1024)


def edges(width):
    even = lax.rem(lax.axis_index("dom"), 2) == 0
    last = jnp.int32(width - 1)
    first = jnp.int32(0)
    ends = jnp.where(even, last, first), jnp.where(even, first, last)
    return ends[LEAD], ends[1 - LEAD]


def window(ref, lead, off, ny):
    rows, nz = ref.shape[-2:]
    base = jnp.minimum(off - lax.rem(off, TILE), rows - ny - TILE)
    skip = off - base
    block = ref[(*lead, pl.ds(pl.multiple_of(base, TILE), ny + TILE), slice(None))]
    tiles = block.reshape(ny // TILE + 1, TILE, nz)
    tiles = pltpu.roll(tiles, lax.rem(TILE - skip, TILE), 1)
    row = lax.broadcasted_iota(jnp.int32, (ny // TILE, TILE, nz), 1)
    return jnp.where(row < TILE - skip, tiles[:-1], tiles[1:]).reshape(ny, nz)


def placed(plane, off, rows):
    fill = jnp.zeros((rows - plane.shape[0], plane.shape[1]), plane.dtype)
    return pltpu.roll(jnp.concatenate([plane, fill], axis=0), off, 0)


def edge_copies(edge, ckpt, adj, kappa, buoy, send, q_e, k_e, b_e, sem):
    return [
        pltpu.make_async_copy(kappa.at[edge], k_e, sem.at[2]),
        pltpu.make_async_copy(buoy.at[edge], b_e, sem.at[3]),
        pltpu.make_async_copy(adj.at[0, 1, edge], q_e, sem.at[1]),
        pltpu.make_async_copy(ckpt.at[0, 1, edge], send.at[0], sem.at[0]),
    ]


def edge_fill(off, send, q_e, k_e, b_e):
    ny = q_e.shape[0]
    send[1] = window(k_e, (), off, ny) * q_e[...]
    send[2] = window(b_e, (), off, ny)


def first_send(off, ckpt, adj, kappa, buoy, send, q_e, k_e, b_e, sem):
    edge = edges(ckpt.shape[2])[0]
    copies = edge_copies(edge, ckpt, adj, kappa, buoy, send, q_e, k_e, b_e, sem)
    for copy in copies:
        copy.start()
    ny = q_e.shape[0]
    copies[0].wait()
    k = window(k_e, (), off[0], ny)
    copies[1].wait()
    send[2] = window(b_e, (), off[0], ny)
    copies[2].wait()
    send[1] = k * q_e[...]
    copies[3].wait()


def receiver_sums(left, right_hi, right_lo, step, nz):
    cols = pl.ds(step * nz, nz)
    return jnp.dot(left[...], right_hi[:, cols], preferred_element_type=F32) + jnp.dot(
        left[...], right_lo[:, cols], preferred_element_type=F32
    )


def receivers(
    off, rec, res, ckpt, adj, kappa, buoy, after, total_1, total_2, send, left, right_hi, right_lo, later,
    q_e, k_e, b_e, cell_s, rank_s, row_a_s, row_b_s, z_s, val_s, sem,
):
    nz = total_1.shape[1]
    edge = edges(ckpt.shape[2])[1]
    copies = edge_copies(edge, ckpt, adj, kappa, buoy, send, q_e, k_e, b_e, sem)
    for copy in copies:
        copy.start()
    rows, lanes = cell_s.shape
    for r in range(rows):
        at = pl.ds(r * lanes, lanes)
        cell_s[r : r + 1, :] = rec[:, at]
        for step in range(2):
            val_s[2 * step, r : r + 1, :] = res[0, step : step + 1, at]
    cells = total_1.shape[0] * nz
    shift = nz.bit_length() - 1
    local = cell_s[...] - lax.axis_index("dom") * cells
    inside = (local >= 0) & (local < cells)
    row = lax.shift_right_logical(local, jnp.int32(shift))
    row_a_s[...] = lax.shift_right_logical(row, jnp.int32(2)).astype(F32)
    row_b_s[...] = (row & 3).astype(F32)
    z_s[...] = (local & (nz - 1)).astype(F32)
    for step in range(2):
        value = val_s[2 * step]
        high = value.astype(BF16).astype(F32)
        val_s[2 * step] = high
        val_s[2 * step + 1] = value - high
    mask = jnp.where(inside, 1.0, 0.0).astype(BF16)
    before = lax.broadcasted_iota(jnp.int32, (lanes, lanes), 0) < lax.broadcasted_iota(
        jnp.int32, (lanes, lanes), 1
    )
    in_row = jnp.dot(mask, jnp.where(before, 1.0, 0.0).astype(BF16), preferred_element_type=F32)
    row_sum = jnp.dot(mask, jnp.ones((lanes, lanes), BF16), preferred_element_type=F32)
    r = lax.broadcasted_iota(jnp.int32, (rows, rows), 0)
    c = lax.broadcasted_iota(jnp.int32, (rows, rows), 1)
    group_r = lax.shift_right_logical(r * 3277, jnp.int32(14))
    group_c = lax.shift_right_logical(c * 3277, jnp.int32(14))
    earlier = jnp.where((group_r == group_c) & (c < r), 1.0, 0.0).astype(BF16)
    row_start = jnp.dot(earlier, row_sum.astype(BF16), preferred_element_type=F32)
    rank = jnp.where(inside, in_row + row_start, -1.0)
    rank_s[...] = rank
    passes = lax.shift_right_logical(jnp.max(rank).astype(jnp.int32), jnp.int32(7)) + 1
    leave = (lax.rem(lax.axis_index("dom"), 2) == 0) & (passes <= 1)
    later[0] = jnp.where(leave, 1, 0)
    groups = rows // GROUP_ROWS
    slot = lax.broadcasted_iota(jnp.int32, (LANES, lanes), 0).astype(F32)
    sub8 = lax.broadcasted_iota(jnp.int32, (TILE, lanes), 0)
    row_iota = lax.broadcasted_iota(jnp.int32, (left.shape[0], LANES), 0).astype(F32)
    depth_iota = lax.broadcasted_iota(jnp.int32, (LANES, nz), 1).astype(F32)

    def one_pass(base, first):
        for g in range(groups):
            picks = []
            fields = []
            for n in range(GROUP_ROWS):
                at = pl.ds(g * GROUP_ROWS + n, 1)
                want = jnp.broadcast_to(rank_s[at, :] - base, (LANES, lanes))
                picks.append(jnp.where(want == slot, 1.0, 0.0).astype(BF16))
                data = jnp.zeros((TILE, lanes), F32)
                sources = [row_a_s, row_b_s, z_s] + [val_s.at[m] for m in range(4)]
                for m, source in enumerate(sources):
                    data = jnp.where(sub8 == m, jnp.broadcast_to(source[at, :], (TILE, lanes)), data)
                fields.append(data.astype(BF16))
            pick = jnp.concatenate(picks, axis=1)
            data = jnp.concatenate(fields, axis=1)
            dims = (((1,), (1,)), ((), ()))
            by_slot = lax.dot_general(pick, data, dims, preferred_element_type=F32)
            by_field = lax.dot_general(data, pick, dims, preferred_element_type=F32)
            where_row = by_field[0:1, :] * 4.0 + by_field[1:2, :]
            here = pl.ds(g * LANES, LANES)
            left[:, here] = jnp.where(row_iota == where_row, 1.0, 0.0).astype(BF16)
            same = by_slot[:, 2:3] == depth_iota
            for step in range(2):
                cols = pl.ds(step * nz, nz)
                high = by_slot[:, 3 + 2 * step : 4 + 2 * step]
                low = by_slot[:, 4 + 2 * step : 5 + 2 * step]
                right_hi[here, cols] = jnp.where(same, high, 0.0).astype(BF16)
                right_lo[here, cols] = jnp.where(same, low, 0.0).astype(BF16)
        if first:
            total_1[...] = receiver_sums(left, right_hi, right_lo, 0, nz)

            @pl.when(jnp.logical_not(leave))
            def _():
                total_2[...] = receiver_sums(left, right_hi, right_lo, 1, nz)

        else:
            total_1[...] += receiver_sums(left, right_hi, right_lo, 0, nz)
            total_2[...] += receiver_sums(left, right_hi, right_lo, 1, nz)

    one_pass(0.0, True)

    @pl.when(passes > 1)
    def _():
        def body(number, carry):
            one_pass((number * LANES).astype(F32), False)
            return carry

        lax.fori_loop(1, passes, body, 0)

    for copy in copies:
        copy.wait()
    edge_fill(off[0], send, q_e, k_e, b_e)


def next_row(f, tile):
    rows = f.shape[0]
    return pltpu.roll(jnp.concatenate([f, tile], axis=0), rows + TILE - 1, 0)[:rows]


def last_row(f, tile):
    return pltpu.roll(jnp.concatenate([tile, f], axis=0), 1, 0)[TILE:]


def next_depth(blocks, end):
    moved = [pltpu.roll(f, LANES - 1, 1) for f in blocks]
    return [jnp.where(end, behind, here) for here, behind in zip(moved, moved[1:] + [0.0])]


def last_depth(blocks, start, first):
    moved = [pltpu.roll(g, 1, 1) for g in blocks]
    return [jnp.where(start, ahead, here) for here, ahead in zip(moved, [first] + moved[:-1])]


class Chunks:
    def __init__(self, ny, nz):
        self.starts = list(range(0, ny, CHUNK))
        self.ny = ny
        self.blocks = nz // LANES
        lane = lax.broadcasted_iota(jnp.int32, (CHUNK, LANES), 1)
        row = lax.broadcasted_iota(jnp.int32, (CHUNK, LANES), 0)
        self.end = lane == LANES - 1
        self.start = lane == 0
        self.top = row == 0

    def load(self, ref, lead, y):
        return [ref[(*lead, pl.ds(y, CHUNK), pl.ds(n * LANES, LANES))] for n in range(self.blocks)]

    def store(self, ref, lead, y, values):
        for n, value in enumerate(values):
            ref[(*lead, pl.ds(y, CHUNK), pl.ds(n * LANES, LANES))] = value

    def behind(self, ref, lead, y):
        if y + CHUNK == self.ny:
            return [jnp.zeros((TILE, LANES), F32)] * self.blocks
        return [
            ref[(*lead, pl.ds(y + CHUNK, TILE), pl.ds(n * LANES, LANES))] for n in range(self.blocks)
        ]

    def rows_up(self, ref, lead, y, f):
        return [next_row(a, b) for a, b in zip(f, self.behind(ref, lead, y))]

    def diffs(self, ref, x, xn, y):
        f = self.load(ref, (x,), y)
        dx = [a - b for a, b in zip(self.load(ref, (xn,), y), f)]
        dy = [a - b for a, b in zip(self.rows_up(ref, (x,), y, f), f)]
        dz = [a - b for a, b in zip(next_depth(f, self.end), f)]
        return f, dx, dy, dz

    def lap(self, d, faces, h, gx_ref, slot, y, carry):
        f, dx, dy, dz = d
        gx, gy, gz = ([a * b for a, b in zip(face, diff)] for face, diff in zip(faces, (dx, dy, dz)))
        old = self.load(gx_ref, (slot,), y)
        self.store(gx_ref, (slot,), y, gx)
        if y == 0:
            ahead = [jnp.where(self.top, a * b, pltpu.roll(g, 1, 0)) for a, b, g in zip(h, f, gy)]
        else:
            ahead = [last_row(g, t) for g, t in zip(gy, carry)]
        back = last_depth(gz, self.start, h[0] * f[0])
        out = [
            (a - b) + (c - e) + (m - n) for a, b, c, e, m, n in zip(gx, old, gy, ahead, gz, back)
        ]
        return out, [g[CHUNK - TILE :] for g in gy]


def one_plane(ch, x, xn, p, q, kq, kw, hb, p_old, q_late, total, fy_o, fz_o, lap_o, pn, qm, kqm, gx_s):
    ny = ch.ny
    tail_p = tail_q = None
    for y in ch.starts:
        h = ch.load(hb, (x,), y)
        fx = [a + b for a, b in zip(h, ch.load(hb, (xn,), y))]
        fy = [a + b for a, b in zip(h, ch.rows_up(hb, (x,), y, h))]
        fz = [a + b for a, b in zip(h, next_depth(h, ch.end))]
        ch.store(fy_o, (x,), y, fy)
        ch.store(fz_o, (x,), y, fz)
        faces = (fx, fy, fz)
        k = ch.load(kw, (x,), y)
        d = ch.diffs(p, x, xn, y)
        lap_p, tail_p = ch.lap(d, faces, h, gx_s, 0, y, tail_p)
        ch.store(lap_o, (x,), y, lap_p)
        old = ch.load(p_old, (x,), y)
        ch.store(pn, (x,), y, [2.0 * a - b + c * e for a, b, c, e in zip(d[0], old, k, lap_p)])
        d = ch.diffs(kq, x, xn, y)
        lap_q, tail_q = ch.lap(d, faces, h, gx_s, 1, y, tail_q)
        now = ch.load(q, (x,), y)
        late = ch.load(q_late, (x,), y)
        at = pl.ds(pl.multiple_of(x * ny + y, TILE), CHUNK)
        add = [total[at, pl.ds(n * LANES, LANES)] for n in range(ch.blocks)]
        mid = [2.0 * a - b + c + e for a, b, c, e in zip(now, late, lap_q, add)]
        ch.store(qm, (x,), y, mid)
        ch.store(kqm, (x,), y, [a * b for a, b in zip(k, mid)])


def add_source(step, src, wav, pn, low, high):
    width, ny, nz = pn.shape
    cell = src[0] - lax.axis_index("dom") * (width * ny * nz)
    plane = ny * nz

    @pl.when((cell >= low * plane) & (cell < high * plane))
    def _():
        shift = nz.bit_length() - 1
        row = lax.shift_right_logical(cell, jnp.int32(shift))
        x = lax.div(row, jnp.int32(ny))
        y = row - x * ny
        spot = lax.broadcasted_iota(jnp.int32, (1, nz), 1) == (cell & (nz - 1))
        pn[x, pl.ds(y, 1), :] += jnp.where(spot, wav[step[0]], 0.0)


def step_one_ends(
    off, step, src, later, wav_in, ckpt, adj, k_full, b_full, total, after, left, right_hi, right_lo, total_2_in,
    kq, kw, hb, fy, fz, lap, pn, qm, kqm, total_2,
    gx_s, wav, sem,
):
    width, ny, nz = kq.shape
    copy = pltpu.make_async_copy(wav_in, wav, sem.at[0])
    copy.start()
    p_old, p, q_late, q = ckpt.at[0, 0], ckpt.at[0, 1], adj.at[0, 0], adj.at[0, 1]

    @pl.when(later[0] == 1)
    def _():
        total_2[...] = receiver_sums(left, right_hi, right_lo, 1, nz)

    def windows(x, carry):
        k = window(k_full, (x,), off[0], ny)
        kw[x] = k
        kq[x] = k * q[x]
        hb[x] = 0.5 * window(b_full, (x,), off[0], ny)
        return carry

    lax.fori_loop(0, width, windows, 0)
    ch = Chunks(ny, nz)
    end = width - 1
    rest = (p, q, kq, kw, hb, p_old, q_late, total, fy, fz, lap, pn, qm, kqm, gx_s)

    def ends(n, carry):
        x = n * end
        before = jnp.maximum(x - 1, 0)
        face = hb[before] + hb[x]
        gx_s[0] = face * (p[x] - p[before])
        gx_s[1] = face * (kq[x] - kq[before])
        one_plane(ch, x, jnp.minimum(x + 1, end), *rest)
        return carry

    lax.fori_loop(0, 2, ends, 0)
    copy.wait()
    add_source(step, src, wav, pn, 0, 1)
    add_source(step, src, wav, pn, end, width)


def step_one_middle(
    step, src, wav_in, ckpt, adj, kq, kw, hb, total, fy_i, fz_i, lap_i, pn_i, qm_i, kqm_i,
    fy, fz, lap, pn, qm, kqm,
    gx_s, wav, sem,
):
    width, ny, nz = kq.shape
    copy = pltpu.make_async_copy(wav_in, wav, sem.at[0])
    copy.start()
    p_old, p, q_late, q = ckpt.at[0, 0], ckpt.at[0, 1], adj.at[0, 0], adj.at[0, 1]
    ch = Chunks(ny, nz)
    face = hb[0] + hb[1]
    gx_s[0] = face * (p[1] - p[0])
    gx_s[1] = face * (kq[1] - kq[0])

    def plane(x, carry):
        one_plane(ch, x, x + 1, p, q, kq, kw, hb, p_old, q_late, total, fy, fz, lap, pn, qm, kqm, gx_s)
        return carry

    lax.fori_loop(1, width - 1, plane, 0)
    copy.wait()
    add_source(step, src, wav, pn, 1, width - 1)


def edge_one(which, recv, ckpt, kq, kw, hb, lap_i, pn_i, qm_i, kqm_i, send, lap, pn, qm, kqm):
    edge = edges(kq.shape[0])[which]
    p = ckpt.at[0, 1]
    face = hb[edge] + 0.5 * recv[2]
    flux = face * (recv[0] - p[edge])
    lap[edge] = lap_i[edge] + flux
    k = kw[edge]
    new = pn_i[edge] + k * flux
    send[0] = new
    pn[edge] = new
    mid = qm_i[edge] + face * (recv[1] - kq[edge])
    qm[edge] = mid
    mid = k * mid
    send[1] = mid
    kqm[edge] = mid


def step_two(part, ckpt, adj, kq, hb, fy_i, fz_i, lap_i, pn, qm, kqm, total, *refs):
    last, parts, gx_s = refs[-3:]
    width, ny, nz = kq.shape
    p, q = ckpt.at[0, 1], adj.at[0, 1]
    at_end = edges(width)[1] == width - 1
    if part == 0:
        low = jnp.where(at_end, 0, 2)
        high = low + width - 2
    else:
        low = jnp.where(at_end, width - 2, 0)
        high = low + 2
    before = jnp.maximum(low - 1, 0)
    face = hb[before] + hb[low]
    gx_s[0] = face * (pn[low] - pn[before])
    gx_s[1] = face * (kqm[low] - kqm[before])
    ch = Chunks(ny, nz)

    def plane(x, carry):
        xn = jnp.minimum(x + 1, width - 1)
        tail_p = tail_q = None
        for y in ch.starts:
            h = ch.load(hb, (x,), y)
            fx = [a + b for a, b in zip(h, ch.load(hb, (xn,), y))]
            faces = (fx, ch.load(fy_i, (x,), y), ch.load(fz_i, (x,), y))
            dpn = ch.diffs(pn, x, xn, y)
            lap_p, tail_p = ch.lap(dpn, faces, h, gx_s, 0, y, tail_p)
            mid = ch.load(qm, (x,), y)
            now = ch.load(q, (x,), y)
            lap_1 = ch.load(lap_i, (x,), y)
            ch.store(parts, (0, x), y, [a * b + c * e for a, b, c, e in zip(mid, lap_1, now, lap_p)])
            dqm = ch.diffs(kqm, x, xn, y)
            lap_q, tail_q = ch.lap(dqm, faces, h, gx_s, 1, y, tail_q)
            add = [
                total[pl.ds(pl.multiple_of(x * ny + y, TILE), CHUNK), pl.ds(n * LANES, LANES)]
                for n in range(ch.blocks)
            ]
            ch.store(last, (x,), y, [2.0 * a - b + c + e for a, b, c, e in zip(mid, now, lap_q, add)])
            dp = ch.diffs(p, x, xn, y)
            sums = [
                sum(a * b for a, b in zip(u, v))
                for u, v in zip(zip(*dp[1:]), zip(*dqm[1:]))
            ]
            dq = ch.diffs(kq, x, xn, y)
            sums = [
                s + sum(a * b for a, b in zip(u, v))
                for s, u, v in zip(sums, zip(*dpn[1:]), zip(*dq[1:]))
            ]
            ch.store(parts, (1, x), y, [-s for s in sums])
        return carry

    lax.fori_loop(low, high, plane, 0)


def edge_terms(edge, recv, recv2, send, ckpt, adj, kq, hb):
    p, q = ckpt.at[0, 1], adj.at[0, 1]
    face = hb[edge] + 0.5 * recv[2]
    dpn = recv2[0] - send[0]
    dqm = recv2[1] - send[1]
    add_k = q[edge] * (face * dpn)
    add_b = -(dqm * (recv[0] - p[edge]) + dpn * (recv[1] - kq[edge]))
    return face * dqm, add_k, jnp.where(edge == kq.shape[0] - 1, add_b, 0.0)


def split(plane, off, half):
    whole = placed(plane, off, 2 * half)
    shot = lax.axis_index("shot")
    return (
        jnp.where(shot == 0, whole[:half], whole[half:]),
        jnp.where(shot == 0, whole[half:], whole[:half]),
    )


def first_edge_two(
    off, recv, recv2, send, ckpt, adj, kq, hb, last_i, parts, qm,
    adj_out, last, mine, other, add, sem,
):
    width = kq.shape[0]
    mid_copy = pltpu.make_async_copy(qm, adj_out.at[0, 0], sem.at[1])
    mid_copy.start()
    half = mine.shape[2]
    edge = edges(width)[0]
    add_q, add[0], add[1] = edge_terms(edge, recv, recv2, send, ckpt, adj, kq, hb)
    last[edge] = last_i[edge] + add_q
    copy = pltpu.make_async_copy(last, adj_out.at[0, 1], sem.at[0])
    copy.start()

    def plane(x, carry):
        here = jnp.where(x == edge, 1.0, 0.0)
        for g in range(2):
            mine[g, x], other[g, x] = split(parts[g, x] + here * add[g], off[0], half)
        return carry

    lax.fori_loop(0, width, plane, 0)
    copy.wait()
    mid_copy.wait()


def second_edge_two(off, recv, recv2, send, ckpt, adj, kq, hb, last, mine, other, last_e):
    half = mine.shape[1]
    edge = edges(kq.shape[0])[1]
    add_q, add_k, add_b = edge_terms(edge, recv, recv2, send, ckpt, adj, kq, hb)
    last_e[...] = last[edge] + add_q
    mine[0], other[0] = split(add_k, off[0], half)
    mine[1], other[1] = split(add_b, off[0], half)


def combine(mine, recv, mine_e, last_e, adj_in, grad_k, grad_b, sums_e, adj_out, sums, sem):
    edge = edges(sums.shape[1])[1]
    copies = [pltpu.make_async_copy(last_e, adj_out.at[0, 1, edge], sem.at[2])]
    copies[0].start()
    for g, grad in enumerate((grad_k, grad_b)):
        sums[g] = mine[g] + recv[g]
        copy = pltpu.make_async_copy(sums.at[g], grad, sem.at[g])
        copy.start()
        copies.append(copy)
    for g in range(2):
        sums_e[g] = sums[g, edge] + mine_e[g]
    for copy in copies:
        copy.wait()


def finish(sums_e, recv_e, grad_k_in, grad_b_in, grad_k, grad_b, sums, sem):
    edge = edges(grad_k.shape[0])[1]
    copies = []
    for g, grad in enumerate((grad_k, grad_b)):
        sums[g] = sums_e[g] + recv_e[g]
        copy = pltpu.make_async_copy(sums.at[g], grad.at[edge], sem.at[g])
        copy.start()
        copies.append(copy)
    for copy in copies:
        copy.wait()


def pairs(count, first):
    out = []
    for low in range(first, count - 1, 2):
        out += [(low, low + 1), (low + 1, low)]
    return out


def shards(
    checkpoint, adjoint, kappa, buoyancy, wavelet, src_cell, rec_cell, residuals, offsets, ckpt_step
):
    width, ny, nz = checkpoint.shape[2:]
    model_y = kappa.shape[1]
    half = model_y // 2
    count = lax.axis_size("dom")
    swaps = pairs(count, LEAD), pairs(count, 1 - LEAD)
    rrows = rec_cell.shape[1] // LANES
    slots = rrows // GROUP_ROWS * LANES
    layer = (ny, nz)
    field = (width, ny, nz)
    dma = pltpu.SemaphoreType.DMA
    adj_shape = pltpu.HBM((1, 2, *field), F32)
    grad_shape = pltpu.HBM((width, half, nz), F32)

    inputs = [far(x) for x in (checkpoint, adjoint, kappa, buoyancy)]
    edge_scratch = [vmem(*layer), vmem(model_y, nz), vmem(model_y, nz)]
    send_1 = pl.pallas_call(
        first_send,
        in_specs=[SM] + [ANY] * 4,
        out_specs=VM,
        out_shape=vmem(3, *layer),
        scratch_shapes=edge_scratch + [dma((4,))],
        compiler_params=params(),
    )(offsets, *inputs)
    recv_1 = lax.ppermute(send_1, "dom", swaps[0])

    sums_shape = vmem(width * ny, nz)
    hot_shapes = [pltpu.VMEM(shape, BF16) for shape in ((width * ny, slots), (slots, 2 * nz), (slots, 2 * nz))]
    total_1, total_2, send_2, *hot, later = pl.pallas_call(
        receivers,
        in_specs=[SM, VM, VM] + [ANY] * 4 + [VM],
        out_specs=[VM] * 6 + [SM],
        out_shape=[sums_shape, sums_shape, vmem(3, *layer)] + hot_shapes + [pltpu.SMEM((1,), jnp.int32)],
        scratch_shapes=edge_scratch + [
            pltpu.VMEM((rrows, LANES), jnp.int32),
            vmem(rrows, LANES), vmem(rrows, LANES), vmem(rrows, LANES), vmem(rrows, LANES),
            vmem(4, rrows, LANES),
            dma((4,)),
        ],
        compiler_params=params(),
        cost_estimate=cost(RECV_COST),
    )(offsets, near(rec_cell), near(residuals), *inputs, near(send_1))
    recv_2 = lax.ppermute(send_2, "dom", swaps[1])

    kq, kw, hb, *state, total_2 = pl.pallas_call(
        step_one_ends,
        in_specs=[SM] * 4 + [ANY] + [VM] * 10,
        out_specs=[VM] * 10,
        out_shape=[vmem(*field)] * 9 + [sums_shape],
        scratch_shapes=[vmem(2, *layer), pltpu.SMEM(wavelet.shape, F32), dma((1,))],
        compiler_params=params(),
        input_output_aliases={14: 9},
        cost_estimate=cost(ENDS_COST),
    )(
        offsets, ckpt_step, src_cell, later, far(wavelet),
        *[near(v) for v in (checkpoint, adjoint, kappa, buoyancy, total_1, send_2, *hot, total_2)],
    )

    def first_edge(which, recv, state):
        send, *new = pl.pallas_call(
            functools.partial(edge_one, which),
            in_specs=[VM] * 9,
            out_specs=[VM] * 5,
            out_shape=[vmem(2, *layer)] + [vmem(*field)] * 4,
            input_output_aliases={5: 1, 6: 2, 7: 3, 8: 4},
            compiler_params=params(),
            cost_estimate=cost(EDGE_COST),
        )(*[near(v) for v in (recv, checkpoint, kq, kw, hb, *state[2:])])
        return send, list(state[:2]) + list(new)

    state = pl.pallas_call(
        step_one_middle,
        in_specs=[SM] * 2 + [ANY] + [VM] * 12,
        out_specs=[VM] * 6,
        out_shape=[vmem(*field)] * 6,
        scratch_shapes=[vmem(2, *layer), pltpu.SMEM(wavelet.shape, F32), dma((1,))],
        input_output_aliases={9 + n: n for n in range(6)},
        compiler_params=params(),
        cost_estimate=cost(MIDDLE_COST),
    )(
        ckpt_step, src_cell, far(wavelet),
        *[near(v) for v in (checkpoint, adjoint, kq, kw, hb, total_1, *state)],
    )
    send2_1, state = first_edge(0, recv_1, state)
    recv2_1 = lax.ppermute(send2_1, "dom", swaps[0])

    def second_step(part, state, *partial):
        out_shape = [vmem(*field), vmem(2, *field)]
        return pl.pallas_call(
            functools.partial(step_two, part),
            in_specs=[VM] * (11 + len(partial)),
            out_specs=[VM, VM],
            out_shape=out_shape,
            scratch_shapes=[vmem(2, *layer)],
            input_output_aliases={11 + n: n for n in range(len(partial))},
            compiler_params=params(),
            cost_estimate=cost(TWO_COST[part]),
        )(*[near(v) for v in (checkpoint, adjoint, kq, hb, *state, total_2, *partial)])

    partial = second_step(0, state)
    send2_2, state = first_edge(1, recv_2, state)
    recv2_2 = lax.ppermute(send2_2, "dom", swaps[1])
    last, parts = second_step(1, state, *partial)
    swap = [(0, 1), (1, 0)]
    adj_part, last, mine, other = pl.pallas_call(
        first_edge_two,
        in_specs=[SM] + [VM] * 10,
        out_specs=[ANY, VM, VM, VM],
        out_shape=[adj_shape, vmem(*field), vmem(2, width, half, nz), vmem(2, width, half, nz)],
        scratch_shapes=[vmem(2, *layer), dma((2,))],
        input_output_aliases={8: 1},
        compiler_params=params(),
        cost_estimate=cost(EDGE_B_COST),
    )(
        offsets,
        *[near(v) for v in (recv_1, recv2_1, send2_1, checkpoint, adjoint, kq, hb, last, parts, state[4])],
    )
    recv_g = lax.ppermute(other, "shot", swap)
    mine_e, other_e, last_e = pl.pallas_call(
        second_edge_two,
        in_specs=[SM] + [VM] * 8,
        out_specs=[VM, VM, VM],
        out_shape=[vmem(2, half, nz), vmem(2, half, nz), vmem(*layer)],
        compiler_params=params(),
        cost_estimate=cost(40),
    )(offsets, *[near(v) for v in (recv_2, recv2_2, send2_2, checkpoint, adjoint, kq, hb, last)])
    recv_e = lax.ppermute(other_e, "shot", swap)
    grad_k, grad_b, sums_e, adj_next = pl.pallas_call(
        combine,
        in_specs=[VM] * 4 + [ANY],
        out_specs=[ANY, ANY, VM, ANY],
        out_shape=[grad_shape, grad_shape, vmem(2, half, nz), adj_shape],
        scratch_shapes=[vmem(2, width, half, nz), dma((3,))],
        input_output_aliases={4: 3},
        compiler_params=params(),
        cost_estimate=cost(40),
    )(near(mine), near(recv_g), near(mine_e), near(last_e), far(adj_part))
    grad_k, grad_b = pl.pallas_call(
        finish,
        in_specs=[VM] * 2 + [ANY] * 2,
        out_specs=[ANY] * 2,
        out_shape=[grad_shape, grad_shape],
        scratch_shapes=[vmem(2, half, nz), dma((2,))],
        input_output_aliases={2: 0, 3: 1},
        compiler_params=params(),
    )(near(sums_e), near(recv_e), far(grad_k), far(grad_b))
    return grad_k, grad_b, adj_next


def solution(mesh):
    in_specs = (
        P(("group", "shot"), None, "dom", None, None),
        P(("group", "shot"), None, "dom", None, None),
        P(("group", "dom"), None, None),
        P(("group", "dom"), None, None),
        P(),
        P(("group", "shot")),
        P(("group", "shot"), None),
        P(("group", "shot"), None, None),
        P(("group", "shot")),
        P(("group", "shot")),
    )
    out_specs = (
        P(("group", "dom"), "shot", None),
        P(("group", "dom"), "shot", None),
        P(("group", "shot"), None, "dom", None, None),
    )
    return jax.shard_map(shards, mesh=mesh, in_specs=in_specs, out_specs=out_specs, check_vma=False)
```
